32 devices in a mesh: batch: 4 (over x, core), seq: 8 (over z, y).
Axes of the slice: x: 2, y: 2, z: 4, core: 2. Of those that a mesh axis runs over, the one named last changes fastest.
Arguments:
- tokens: bfloat16 [4, 1024, 768], P('batch', 'seq'), may hold values from -6 to 6
- memory: bfloat16 [4, 1024, 768], P('batch', 'seq'), may hold values from -6 to 6
- target_segments: int32 [4, 1024], P('batch'), may hold values from 0 to 14, as said below
- memory_segments: int32 [4, 1024], P('batch'), may hold values from 0 to 14, as said below
- cotangent: bfloat16 [4, 1024, 768], P('batch', 'seq'), may hold values from -6 to 6
- selfquery: bfloat16 [768, 768], P(('batch', 'seq')), may hold values from -0.21875 to 0.21875
- selfkey: bfloat16 [768, 768], P(('batch', 'seq')), may hold values from -0.21875 to 0.21875
- selfvalue: bfloat16 [768, 768], P(('batch', 'seq')), may hold values from -0.21875 to 0.21875
- selfout: bfloat16 [768, 768], P(('batch', 'seq')), may hold values from -1.75 to 1.75
- selfqbias: bfloat16 [768], P(('batch', 'seq')), may hold values from -1.75 to 1.75
- selfvbias: bfloat16 [768], P(('batch', 'seq')), may hold values from -1.75 to 1.75
- selfobias: bfloat16 [768], P(('batch', 'seq')), may hold values from -3.5 to 3.5
- selfgain: bfloat16 [768], P(('batch', 'seq')), may hold values from 0.25 to 1.75
- selfshift: bfloat16 [768], P(('batch', 'seq')), may hold values from -1.75 to 1.75
- crossquery: bfloat16 [768, 768], P(('batch', 'seq')), may hold values from -0.21875 to 0.21875
- crosskey: bfloat16 [768, 768], P(('batch', 'seq')), may hold values from -0.21875 to 0.21875
- crossvalue: bfloat16 [768, 768], P(('batch', 'seq')), may hold values from -0.21875 to 0.21875
- crossout: bfloat16 [768, 768], P(('batch', 'seq')), may hold values from -1.75 to 1.75
- crossqbias: bfloat16 [768], P(('batch', 'seq')), may hold values from -1.75 to 1.75
- crossvbias: bfloat16 [768], P(('batch', 'seq')), may hold values from -1.75 to 1.75
- crossobias: bfloat16 [768], P(('batch', 'seq')), may hold values from -3.5 to 3.5
- crossgain: bfloat16 [768], P(('batch', 'seq')), may hold values from 0.25 to 1.75
- crossshift: bfloat16 [768], P(('batch', 'seq')), may hold values from -1.75 to 1.75
- innerweight: bfloat16 [768, 3072], P(('batch', 'seq')), may hold values from -0.21875 to 0.21875
- innerbias: bfloat16 [3072], P(('batch', 'seq')), may hold values from -1.75 to 1.75
- outerweight: bfloat16 [3072, 768], P(('batch', 'seq')), may hold values from -0.21875 to 0.21875
- outerbias: bfloat16 [768], P(('batch', 'seq')), may hold values from -1.75 to 1.75
- finalgain: bfloat16 [768], P(('batch', 'seq')), may hold values from 0.25 to 1.75
- finalshift: bfloat16 [768], P(('batch', 'seq')), may hold values from -1.75 to 1.75
Outputs:
- output: bfloat16 [4, 1024, 768], P('batch', 'seq')
- tokens_grad: float32 [4, 1024, 768], P('batch', 'seq')
- memory_grad: float32 [4, 1024, 768], P('batch', 'seq')
- selfquery_grad: float32 [768, 768], P(('batch', 'seq'))
- selfkey_grad: float32 [768, 768], P(('batch', 'seq'))
- selfvalue_grad: float32 [768, 768], P(('batch', 'seq'))
- selfout_grad: float32 [768, 768], P(('batch', 'seq'))
- selfqbias_grad: float32 [768], P(('batch', 'seq'))
- selfvbias_grad: float32 [768], P(('batch', 'seq'))
- selfobias_grad: float32 [768], P(('batch', 'seq'))
- selfgain_grad: float32 [768], P(('batch', 'seq'))
- selfshift_grad: float32 [768], P(('batch', 'seq'))
- crossquery_grad: float32 [768, 768], P(('batch', 'seq'))
- crosskey_grad: float32 [768, 768], P(('batch', 'seq'))
- crossvalue_grad: float32 [768, 768], P(('batch', 'seq'))
- crossout_grad: float32 [768, 768], P(('batch', 'seq'))
- crossqbias_grad: float32 [768], P(('batch', 'seq'))
- crossvbias_grad: float32 [768], P(('batch', 'seq'))
- crossobias_grad: float32 [768], P(('batch', 'seq'))
- crossgain_grad: float32 [768], P(('batch', 'seq'))
- crossshift_grad: float32 [768], P(('batch', 'seq'))
- innerweight_grad: float32 [768, 3072], P(('batch', 'seq'))
- innerbias_grad: float32 [3072], P(('batch', 'seq'))
- outerweight_grad: float32 [3072, 768], P(('batch', 'seq'))
- outerbias_grad: float32 [768], P(('batch', 'seq'))
- finalgain_grad: float32 [768], P(('batch', 'seq'))
- finalshift_grad: float32 [768], P(('batch', 'seq'))
The draws below stay inside these ranges and needn't reach their ends.
Inputs may be any that keep to these rules, and one draw needn't show every extreme that they name: `target_segments`: along each row the numbers never fall until the padding 0 that ends it; every row holds each of 0 to 14, each document has at least 64 and at most 128 tokens. `memory_segments`: every row holds each of 0 to 14; the documents stand in falling order of their numbers, followed by the padding 0 that ends the row; each document has at least 64 and at most 128 tokens.
All inputs are finite; a program needn't handle non-finite values.
Results may differ from the reference program's by a relative error of at most 0.034.
Values may be sent and summed in bfloat16 or wider, within the bound.
A program may use at most 192 MiB of HBM per device.

```python
import jax
import jax.numpy as jnp
from jax import lax

D = 768
HD = 64
FF = 3072
TOK_DEV = 128
LEN = 1024
ROWS = 4


document_count = 14


def segment_layout(key, row_count, length, piece):
    weight_key, pad_key = jax.random.split(key, 2)
    shares = jax.random.randint(weight_key, (row_count, document_count), 1, 9)
    padding = jax.random.randint(pad_key, (row_count, 1), 1, piece // 8 + 2)
    base = length // 16
    running = jnp.cumsum(shares, axis=1)
    total = running[:, -1:]
    extra = length - padding - document_count * base
    steps = jnp.arange(1, document_count + 1, dtype=jnp.int32)[None, :] * base
    ends = steps + running * extra // total
    position = jnp.arange(length, dtype=jnp.int32)[None, None, :]
    labels = 1 + jnp.sum((position >= ends[:, :, None]).astype(jnp.int32), axis=1)
    return jnp.where(labels > document_count, 0, labels).astype(jnp.int32)


def draw_target_segments(key, part):
    key = jax.random.fold_in(key, 11)
    return segment_layout(key, ROWS, LEN, TOK_DEV)


def draw_memory_segments(key, part):
    key = jax.random.fold_in(key, 23)
    labels = segment_layout(key, ROWS, LEN, TOK_DEV)
    return jnp.where(labels > 0, document_count + 1 - labels, 0).astype(jnp.int32)


def block_levels(key, extent, cuts, low, top_value):
    level = 1.0
    for dim, shards_of in cuts:
        steps = jax.random.uniform(jax.random.fold_in(jax.random.fold_in(key, 6), dim), (shards_of,), jnp.float32, low / len(cuts), top_value / len(cuts))
        level = level * jnp.repeat(jnp.exp(steps), extent[dim] // shards_of).reshape((-1,) + (1,) * (len(extent) - 1 - dim))
    return level


def scatter_about(rng, shape, deviation, limit, shards=(), held_as=jnp.bfloat16):
    level = block_levels(rng, shape, shards, -0.22, 0.18) if shards else 1.0
    values = jax.random.normal(rng, shape, jnp.float32) * deviation * level
    return jnp.minimum(jnp.maximum(values, -limit), limit).astype(held_as)


def setup_inputs(seed: int = 0) -> dict:
    key_of = jax.random.split(jax.random.key(seed), 30)
    tokens = scatter_about(key_of[0], (ROWS, LEN, D), 1.0, 6.0, ((0, 4), (1, 8)))
    memory = scatter_about(key_of[1], (ROWS, LEN, D), 1.0, 6.0, ((0, 4), (1, 8)))
    target_segments = draw_target_segments(jax.random.fold_in(key_of[29], 71), 0)
    memory_segments = draw_memory_segments(jax.random.fold_in(key_of[29], 71), 0)
    cotangent = scatter_about(key_of[4], (ROWS, LEN, D), 1.0, 6.0, ((0, 4), (1, 8)))
    selfquery = scatter_about(key_of[5], (D, D), D ** -0.5, 0.21875, ((0, 32),))
    selfkey = scatter_about(key_of[6], (D, D), D ** -0.5, 0.21875, ((0, 32),))
    selfvalue = scatter_about(key_of[7], (D, D), D ** -0.5, 0.21875, ((0, 32),))
    selfout = scatter_about(key_of[8], (D, D), (D // 64) ** -0.5, 1.75, ((0, 32),))
    selfqbias = scatter_about(key_of[9], (D,), 0.3, 1.75, ((0, 32),))
    selfvbias = scatter_about(key_of[10], (D,), 0.3, 1.75, ((0, 32),))
    selfobias = scatter_about(key_of[11], (D,), 0.6, 3.5, ((0, 32),))
    selfgain = jnp.clip(1.0 + 0.15 * jax.random.normal(key_of[12], (D,), jnp.float32), 0.25, 1.75).astype(jnp.bfloat16)
    selfshift = scatter_about(key_of[13], (D,), 0.3, 1.75, ((0, 32),))
    crossquery = scatter_about(key_of[14], (D, D), D ** -0.5, 0.21875, ((0, 32),))
    crosskey = scatter_about(key_of[15], (D, D), D ** -0.5, 0.21875, ((0, 32),))
    crossvalue = scatter_about(key_of[16], (D, D), D ** -0.5, 0.21875, ((0, 32),))
    crossout = scatter_about(key_of[17], (D, D), (D // 64) ** -0.5, 1.75, ((0, 32),))
    crossqbias = scatter_about(key_of[18], (D,), 0.3, 1.75, ((0, 32),))
    crossvbias = scatter_about(key_of[19], (D,), 0.3, 1.75, ((0, 32),))
    crossobias = scatter_about(key_of[20], (D,), 0.6, 3.5, ((0, 32),))
    crossgain = jnp.clip(1.0 + 0.15 * jax.random.normal(key_of[21], (D,), jnp.float32), 0.25, 1.75).astype(jnp.bfloat16)
    crossshift = scatter_about(key_of[22], (D,), 0.3, 1.75, ((0, 32),))
    innerweight = scatter_about(key_of[23], (D, FF), D ** -0.5, 0.21875, ((0, 32),))
    innerbias = scatter_about(key_of[24], (FF,), 0.3, 1.75, ((0, 32),))
    outerweight = scatter_about(key_of[25], (FF, D), (FF // 4) ** -0.5, 0.21875, ((0, 32),))
    outerbias = scatter_about(key_of[26], (D,), 0.3, 1.75, ((0, 32),))
    finalgain = jnp.clip(1.0 + 0.15 * jax.random.normal(key_of[27], (D,), jnp.float32), 0.25, 1.75).astype(jnp.bfloat16)
    finalshift = scatter_about(key_of[28], (D,), 0.3, 1.75, ((0, 32),))
    return dict(tokens=tokens, memory=memory, target_segments=target_segments, memory_segments=memory_segments, cotangent=cotangent, selfquery=selfquery, selfkey=selfkey, selfvalue=selfvalue, selfout=selfout, selfqbias=selfqbias, selfvbias=selfvbias, selfobias=selfobias, selfgain=selfgain, selfshift=selfshift, crossquery=crossquery, crosskey=crosskey, crossvalue=crossvalue, crossout=crossout, crossqbias=crossqbias, crossvbias=crossvbias, crossobias=crossobias, crossgain=crossgain, crossshift=crossshift, innerweight=innerweight, innerbias=innerbias, outerweight=outerweight, outerbias=outerbias, finalgain=finalgain, finalshift=finalshift)


SCALE = 0.125
NEGATIVE = -1e+30
EPSILON = 1e-05
HIGHEST = lax.Precision.HIGHEST

@jax.custom_vjp
def low(v):
    return lax.optimization_barrier(v.astype(jnp.bfloat16)).astype(jnp.float32)

@jax.custom_vjp
def low_back(v):
    return v

def low_keep(v):
    return (low(v), None)

def low_pass(kept, grad):
    return (grad,)

def back_keep(v):
    return (v, None)

def back_low(kept, grad):
    return (low(grad),)
low.defvjp(low_keep, low_pass)
low_back.defvjp(back_keep, back_low)

def normalize(values, gain, shift):
    center = values - lax.optimization_barrier(jnp.mean(values, axis=-1, keepdims=True))
    spread = lax.optimization_barrier(jnp.mean(center * center, axis=-1, keepdims=True))
    return center * lax.rsqrt(spread + EPSILON) * gain + shift

def product(left, right):
    return jnp.dot(left, right, precision=HIGHEST)

def attention(queries, keys, values, query_ids, key_ids, causal):
    length = queries.shape[0]
    head_count = queries.shape[1] // HD
    block_rows = 512 if length % 512 == 0 else length
    key_heads = keys.reshape(keys.shape[0], head_count, HD)
    value_heads = values.reshape(values.shape[0], head_count, HD)
    key_pos = jnp.arange(keys.shape[0], dtype=jnp.int32)
    query_blocks = queries.reshape(length // block_rows, block_rows, head_count, HD)
    id_blocks = query_ids.reshape(length // block_rows, block_rows)
    pos_blocks = jnp.arange(length, dtype=jnp.int32).reshape(length // block_rows, block_rows)

    @jax.checkpoint
    def one_block(block):
        query_block, id_block, pos_block = block
        raw = jnp.einsum('qhd,khd->hqk', query_block, key_heads, precision=HIGHEST)
        scores = low_back(raw * SCALE)
        allowed = id_block[:, None] == key_ids[None, :]
        if causal:
            allowed = jnp.logical_and(allowed, key_pos[None, :] <= pos_block[:, None])
        scores = jnp.where(allowed[None], scores, NEGATIVE)
        probs = low(jax.nn.softmax(scores, axis=-1))
        context = jnp.einsum('hqk,khd->qhd', probs, value_heads, precision=HIGHEST)
        return context.reshape(block_rows, head_count * HD)
    result = lax.map(one_block, (query_blocks, id_blocks, pos_blocks))
    return result.reshape(length, head_count * HD)

def layer(weights, inputs, source, target_ids, source_ids):
    selfquery, selfkey, selfvalue, selfout, selfqbias, selfvbias, selfobias, selfgain, selfshift, crossquery, crosskey, crossvalue, crossout, crossqbias, crossvbias, crossobias, crossgain, crossshift, innerweight, innerbias, outerweight, outerbias, finalgain, finalshift = weights
    queries = low_back(low(product(inputs, selfquery) + selfqbias))
    keys_self = low_back(low(product(inputs, selfkey)))
    values_self = low_back(low(product(inputs, selfvalue) + selfvbias))
    context = low(low_back(attention(queries, keys_self, values_self, target_ids, target_ids, True)))
    first = normalize(inputs + low_back(product(context, selfout) + selfobias), selfgain, selfshift)
    first_low = low(first)
    cross_queries = low_back(low(product(first_low, crossquery) + crossqbias))
    cross_keys = low_back(low(product(source, crosskey)))
    cross_values = low_back(low(product(source, crossvalue) + crossvbias))
    cross_context = low(low_back(attention(cross_queries, cross_keys, cross_values, target_ids, source_ids, False)))
    second = normalize(first + low_back(product(cross_context, crossout) + crossobias), crossgain, crossshift)
    inner = low_back(product(low(second), innerweight) + innerbias)
    activation = low(jax.nn.gelu(inner, approximate=False))
    return normalize(second + low_back(product(activation, outerweight) + outerbias), finalgain, finalshift)

def reference(tokens, memory, target_segments, memory_segments, cotangent, selfquery, selfkey, selfvalue, selfout, selfqbias, selfvbias, selfobias, selfgain, selfshift, crossquery, crosskey, crossvalue, crossout, crossqbias, crossvbias, crossobias, crossgain, crossshift, innerweight, innerbias, outerweight, outerbias, finalgain, finalshift):
    weights = tuple((matrix.astype(jnp.float32) for matrix in (selfquery, selfkey, selfvalue, selfout, selfqbias, selfvbias, selfobias, selfgain, selfshift, crossquery, crosskey, crossvalue, crossout, crossqbias, crossvbias, crossobias, crossgain, crossshift, innerweight, innerbias, outerweight, outerbias, finalgain, finalshift)))

    def forward(weight_set, inputs, sources):

        def one_row(row):
            row_inputs, row_sources, row_targets, row_ids = row
            return layer(weight_set, row_inputs, row_sources, row_targets, row_ids)
        return lax.map(one_row, (inputs, sources, target_segments, memory_segments))
    output, pullback = jax.vjp(forward, weights, tokens.astype(jnp.float32), memory.astype(jnp.float32))
    grads, tokens_grad, memory_grad = pullback(cotangent.astype(jnp.float32))
    return (output.astype(jnp.bfloat16), tokens_grad, memory_grad, grads[0], grads[1], grads[2], grads[3], grads[4], grads[5], grads[6], grads[7], grads[8], grads[9], grads[10], grads[11], grads[12], grads[13], grads[14], grads[15], grads[16], grads[17], grads[18], grads[19], grads[20], grads[21], grads[22], grads[23])
```

```python
from functools import partial

import jax
import jax.numpy as jnp
from jax import lax
from jax.experimental import pallas as pl
from jax.experimental.pallas import tpu as pltpu
from jax.sharding import PartitionSpec as P

BATCH, SEQ = ("batch", "seq")
BOTH = (BATCH, SEQ)
HD = 64
SCALE = 0.125
NEGATIVE = -1e30
EPSILON = 1e-05
block_limit = 1024


def spans(total):
    if total > block_limit and total % block_limit == 0:
        return (block_limit, total // block_limit)
    return (total, 1)


def heads_of(matrix):
    return matrix.reshape(matrix.shape[0], -1, HD)


def normalize(values, gain, shift):
    center = values - jnp.mean(values, axis=-1, keepdims=True)
    spread = jnp.mean(center * center, axis=-1, keepdims=True)
    return center * lax.rsqrt(spread + EPSILON) * gain + shift


def norm_back(values, gain, shift, grad):
    _, pullback = jax.vjp(normalize, values, gain, shift)
    return pullback(grad)


def matmul(left, right):
    return jnp.dot(left, right, preferred_element_type=jnp.float32)


def left_product(left, right):
    return lax.dot_general(
        left, right, (((0,), (0,)), ((), ())), preferred_element_type=jnp.float32
    )


def right_product(left, right):
    return lax.dot_general(
        left, right, (((1,), (1,)), ((), ())), preferred_element_type=jnp.float32
    )


def row_total(matrix):
    return jnp.sum(matrix.astype(jnp.float32), axis=0)


def allowed_mask(query_seg, query_pos, key_seg, key_pos, causal):
    same = query_seg[:, None] == key_seg[None, :]
    if causal:
        same = jnp.logical_and(same, key_pos[None, :] <= query_pos[:, None])
    return same


def block_terms(
    query_block, upstream_block, logsum_block, delta_block, allowed, key_block, value_block
):
    scores = (
        jnp.einsum("qhd,khd->hqk", query_block, key_block, preferred_element_type=jnp.float32)
        * SCALE
    )
    scores = jnp.where(allowed[None], scores, NEGATIVE)
    probs = jnp.where(allowed[None], jnp.exp(scores - logsum_block[:, :, None]), 0.0)
    dprobs = jnp.einsum(
        "qhd,khd->hqk", upstream_block, value_block, preferred_element_type=jnp.float32
    )
    dscores = (probs * (dprobs - delta_block[:, :, None]) * SCALE).astype(jnp.bfloat16)
    return (probs.astype(jnp.bfloat16), dscores)


def attend(queries, keys, values, query_seg, query_pos, key_ids, causal):
    row_count = queries.shape[0]
    head_count = queries.shape[1] // HD
    query_heads = heads_of(queries)
    all_keys, all_values = (
        lax.all_gather(keys, SEQ, axis=0, tiled=True),
        lax.all_gather(values, SEQ, axis=0, tiled=True),
    )
    block_rows, block_count = spans(all_keys.shape[0])

    def scored(index):
        offset = index * block_rows
        key_block = heads_of(lax.dynamic_slice_in_dim(all_keys, offset, block_rows, 0))
        key_pos = offset + jnp.arange(block_rows, dtype=jnp.int32)
        key_seg = lax.dynamic_slice_in_dim(key_ids, offset, block_rows, 0)
        allowed = allowed_mask(query_seg, query_pos, key_seg, key_pos, causal)[None]
        scores = (
            jnp.einsum("qhd,khd->hqk", query_heads, key_block, preferred_element_type=jnp.float32)
            * SCALE
        )
        return (jnp.where(allowed, scores, NEGATIVE), allowed)

    def stat_step(index, state):
        run_max, run_sum = state
        scores, allowed = scored(index)
        new_max = jnp.maximum(run_max, jnp.max(scores, axis=2))
        weights = jnp.where(allowed, jnp.exp(scores - new_max[:, :, None]), 0.0)
        run_sum = run_sum * jnp.exp(run_max - new_max) + jnp.sum(weights, axis=2)
        return (new_max, run_sum)

    run_max, run_sum = lax.fori_loop(
        0,
        block_count,
        stat_step,
        (
            jnp.full((head_count, row_count), NEGATIVE, jnp.float32),
            jnp.zeros((head_count, row_count), jnp.float32),
        ),
    )
    logsum = run_max + jnp.log(run_sum)

    def value_step(index, accum):
        scores, allowed = scored(index)
        probs = jnp.where(allowed, jnp.exp(scores - logsum[:, :, None]), 0.0).astype(jnp.bfloat16)
        value_block = heads_of(
            lax.dynamic_slice_in_dim(all_values, index * block_rows, block_rows, 0)
        )
        return accum + jnp.einsum(
            "hqk,khd->qhd", probs, value_block, preferred_element_type=jnp.float32
        )

    accum = lax.fori_loop(
        0, block_count, value_step, jnp.zeros((row_count, head_count, HD), jnp.float32)
    )
    outcome = accum.reshape(row_count, head_count * HD)
    return (outcome, logsum)


def head_delta(upstream, context):
    row_count = upstream.shape[0]
    return jnp.sum((upstream.astype(jnp.float32) * context).reshape(row_count, -1, HD), axis=2).T


def attend_back(queries, keys, values, upstream, logsum, delta, query_ids, key_ids, causal):
    row_count = queries.shape[0]
    head_count = queries.shape[1] // HD
    own_first = lax.axis_index(SEQ) * row_count
    own_pos = own_first + jnp.arange(row_count, dtype=jnp.int32)
    query_seg = lax.dynamic_slice_in_dim(query_ids, own_first, row_count, 0)
    key_seg = lax.dynamic_slice_in_dim(key_ids, own_first, row_count, 0)
    query_heads = heads_of(queries)
    upstream_heads = heads_of(upstream)
    empty = jnp.zeros((row_count, head_count, HD), jnp.float32)
    key_source = lax.all_gather(keys, SEQ, axis=0, tiled=True)
    value_source = lax.all_gather(values, SEQ, axis=0, tiled=True)
    block_rows, block_count = spans(key_source.shape[0])

    def key_step(index, running):
        local = index * block_rows
        key_block = heads_of(lax.dynamic_slice_in_dim(key_source, local, block_rows, 0))
        value_block = heads_of(lax.dynamic_slice_in_dim(value_source, local, block_rows, 0))
        block_seg = lax.dynamic_slice_in_dim(key_ids, local, block_rows, 0)
        block_pos = local + jnp.arange(block_rows, dtype=jnp.int32)
        allowed = allowed_mask(query_seg, own_pos, block_seg, block_pos, causal)
        probs, dscores = block_terms(
            query_heads, upstream_heads, logsum, delta, allowed, key_block, value_block
        )
        return running + jnp.einsum(
            "hqk,khd->qhd", dscores, key_block, preferred_element_type=jnp.float32
        )

    dqueries = lax.fori_loop(0, block_count, key_step, empty)
    all_logsum, all_delta = (
        lax.all_gather(logsum, SEQ, axis=1, tiled=True),
        lax.all_gather(delta, SEQ, axis=1, tiled=True),
    )
    key_heads = heads_of(keys)
    value_heads = heads_of(values)
    piece_queries = lax.all_gather(queries, SEQ, axis=0, tiled=True)
    piece_upstream = lax.all_gather(upstream, SEQ, axis=0, tiled=True)
    query_block_rows, block_count = spans(piece_queries.shape[0])

    def query_step(index, running):
        key_total, value_total = running
        local = index * query_block_rows
        query_block = heads_of(lax.dynamic_slice_in_dim(piece_queries, local, query_block_rows, 0))
        upstream_block = heads_of(
            lax.dynamic_slice_in_dim(piece_upstream, local, query_block_rows, 0)
        )
        logsum_block = lax.dynamic_slice_in_dim(all_logsum, local, query_block_rows, 1)
        delta_block = lax.dynamic_slice_in_dim(all_delta, local, query_block_rows, 1)
        block_seg = lax.dynamic_slice_in_dim(query_ids, local, query_block_rows, 0)
        block_pos = local + jnp.arange(query_block_rows, dtype=jnp.int32)
        allowed = allowed_mask(block_seg, block_pos, key_seg, own_pos, causal)
        probs, dscores = block_terms(
            query_block, upstream_block, logsum_block, delta_block, allowed, key_heads, value_heads
        )
        key_total = key_total + jnp.einsum(
            "hqk,qhd->khd", dscores, query_block, preferred_element_type=jnp.float32
        )
        value_total = value_total + jnp.einsum(
            "hqk,qhd->khd", probs, upstream_block, preferred_element_type=jnp.float32
        )
        return (key_total, value_total)

    key_grad, value_grad = lax.fori_loop(0, block_count, query_step, (empty, empty))
    key_grad = key_grad.reshape(row_count, -1)
    value_grad = value_grad.reshape(row_count, -1)
    return (dqueries.reshape(row_count, -1), key_grad, value_grad)


def shards(
    tokens,
    memory,
    target_segments,
    memory_segments,
    cotangent,
    selfquery,
    selfkey,
    selfvalue,
    selfout,
    selfqbias,
    selfvbias,
    selfobias,
    selfgain,
    selfshift,
    crossquery,
    crosskey,
    crossvalue,
    crossout,
    crossqbias,
    crossvbias,
    crossobias,
    crossgain,
    crossshift,
    innerweight,
    innerbias,
    outerweight,
    outerbias,
    finalgain,
    finalshift,
):
    inputs = tokens[0]
    source = memory[0]
    target_ids = target_segments[0]
    source_ids = memory_segments[0]
    row_count = inputs.shape[0]
    own_first = lax.axis_index(SEQ) * row_count
    own_pos = own_first + jnp.arange(row_count, dtype=jnp.int32)
    query_seg = lax.dynamic_slice_in_dim(target_ids, own_first, row_count, 0)
    (
        query_full,
        key_full,
        value_full,
        out_full,
        qbias_full,
        vbias_full,
        obias_full,
        sgain_full,
        sshift_full,
    ) = (
        lax.all_gather(selfquery, BOTH, axis=0, tiled=True),
        lax.all_gather(selfkey, BOTH, axis=0, tiled=True),
        lax.all_gather(selfvalue, BOTH, axis=0, tiled=True),
        lax.all_gather(selfout, BOTH, axis=0, tiled=True),
        lax.all_gather(selfqbias, BOTH, axis=0, tiled=True),
        lax.all_gather(selfvbias, BOTH, axis=0, tiled=True),
        lax.all_gather(selfobias, BOTH, axis=0, tiled=True),
        lax.all_gather(selfgain, BOTH, axis=0, tiled=True),
        lax.all_gather(selfshift, BOTH, axis=0, tiled=True),
    )
    sgain = sgain_full.astype(jnp.float32)
    sshift = sshift_full.astype(jnp.float32)
    query_self = (matmul(inputs, query_full) + qbias_full.astype(jnp.float32)).astype(jnp.bfloat16)
    key_self = matmul(inputs, key_full).astype(jnp.bfloat16)
    value_self = (matmul(inputs, value_full) + vbias_full.astype(jnp.float32)).astype(jnp.bfloat16)
    attn_self, logsum_self = attend(
        query_self, key_self, value_self, query_seg, own_pos, target_ids, True
    )
    self_low = attn_self.astype(jnp.bfloat16)
    hidden_one = (
        inputs.astype(jnp.float32) + matmul(self_low, out_full) + obias_full.astype(jnp.float32)
    )
    first = normalize(hidden_one, sgain, sshift)
    first_low = first.astype(jnp.bfloat16)
    (
        cquery_full,
        ckey_full,
        cvalue_full,
        cout_full,
        cqbias_full,
        cvbias_full,
        cobias_full,
        cgain_full,
        cshift_full,
    ) = (
        lax.all_gather(crossquery, BOTH, axis=0, tiled=True),
        lax.all_gather(crosskey, BOTH, axis=0, tiled=True),
        lax.all_gather(crossvalue, BOTH, axis=0, tiled=True),
        lax.all_gather(crossout, BOTH, axis=0, tiled=True),
        lax.all_gather(crossqbias, BOTH, axis=0, tiled=True),
        lax.all_gather(crossvbias, BOTH, axis=0, tiled=True),
        lax.all_gather(crossobias, BOTH, axis=0, tiled=True),
        lax.all_gather(crossgain, BOTH, axis=0, tiled=True),
        lax.all_gather(crossshift, BOTH, axis=0, tiled=True),
    )
    cgain = cgain_full.astype(jnp.float32)
    cshift = cshift_full.astype(jnp.float32)
    query_cross = (matmul(first_low, cquery_full) + cqbias_full.astype(jnp.float32)).astype(
        jnp.bfloat16
    )
    key_cross = matmul(source, ckey_full).astype(jnp.bfloat16)
    value_cross = (matmul(source, cvalue_full) + cvbias_full.astype(jnp.float32)).astype(
        jnp.bfloat16
    )
    attn_cross, logsum_cross = attend(
        query_cross, key_cross, value_cross, query_seg, own_pos, source_ids, False
    )
    cross_low = attn_cross.astype(jnp.bfloat16)
    hidden_two = first + matmul(cross_low, cout_full) + cobias_full.astype(jnp.float32)
    second = normalize(hidden_two, cgain, cshift)
    second_low = second.astype(jnp.bfloat16)
    inner_full, ibias_full, outer_full, obias_feed, fgain_full, fshift_full = (
        lax.all_gather(innerweight, BOTH, axis=0, tiled=True),
        lax.all_gather(innerbias, BOTH, axis=0, tiled=True),
        lax.all_gather(outerweight, BOTH, axis=0, tiled=True),
        lax.all_gather(outerbias, BOTH, axis=0, tiled=True),
        lax.all_gather(finalgain, BOTH, axis=0, tiled=True),
        lax.all_gather(finalshift, BOTH, axis=0, tiled=True),
    )
    fgain = fgain_full.astype(jnp.float32)
    fshift = fshift_full.astype(jnp.float32)
    smooth = partial(jax.nn.gelu, approximate=False)
    inner_pre = matmul(second_low, inner_full) + ibias_full.astype(jnp.float32)
    activation = smooth(inner_pre).astype(jnp.bfloat16)
    hidden_three = second + matmul(activation, outer_full) + obias_feed.astype(jnp.float32)
    output = normalize(hidden_three, fgain, fshift).astype(jnp.bfloat16)
    grad_hidden3, grad_fgain, grad_fshift = norm_back(
        hidden_three, fgain, fshift, cotangent[0].astype(jnp.float32)
    )
    branch_grad = grad_hidden3.astype(jnp.bfloat16)
    grad_outer = left_product(activation, branch_grad)
    grad_obias_feed = row_total(branch_grad)
    _, gelu_back = jax.vjp(smooth, inner_pre)
    inner_grad = gelu_back(right_product(branch_grad, outer_full))[0].astype(jnp.bfloat16)
    grad_inner = left_product(second_low, inner_grad)
    grad_ibias = row_total(inner_grad)
    grad_second = grad_hidden3 + right_product(inner_grad, inner_full)
    feed_grads = (
        lax.psum_scatter(grad_inner, BOTH, scatter_dimension=0, tiled=True),
        lax.psum_scatter(grad_ibias, BOTH, scatter_dimension=0, tiled=True),
        lax.psum_scatter(grad_outer, BOTH, scatter_dimension=0, tiled=True),
        lax.psum_scatter(grad_obias_feed, BOTH, scatter_dimension=0, tiled=True),
        lax.psum_scatter(grad_fgain, BOTH, scatter_dimension=0, tiled=True),
        lax.psum_scatter(grad_fshift, BOTH, scatter_dimension=0, tiled=True),
    )
    grad_hidden2, grad_cgain, grad_cshift = norm_back(hidden_two, cgain, cshift, grad_second)
    cross_branch = grad_hidden2.astype(jnp.bfloat16)
    grad_cout = left_product(cross_low, cross_branch)
    grad_cobias = row_total(cross_branch)
    cross_up = right_product(cross_branch, cout_full).astype(jnp.bfloat16)
    cross_delta = head_delta(cross_up, attn_cross)
    cq_grad, ck_grad, cv_grad = attend_back(
        query_cross,
        key_cross,
        value_cross,
        cross_up,
        logsum_cross,
        cross_delta,
        target_ids,
        source_ids,
        False,
    )
    cq_low = cq_grad.astype(jnp.bfloat16)
    ck_low = ck_grad.astype(jnp.bfloat16)
    cv_low = cv_grad.astype(jnp.bfloat16)
    grad_cquery = left_product(first_low, cq_low)
    grad_cqbias = row_total(cq_low)
    grad_ckey = left_product(source, ck_low)
    grad_cvalue = left_product(source, cv_low)
    grad_cvbias = row_total(cv_low)
    memory_grad = right_product(ck_low, ckey_full) + right_product(cv_low, cvalue_full)
    grad_first = grad_hidden2 + right_product(cq_low, cquery_full)
    cross_grads = (
        lax.psum_scatter(grad_cquery, BOTH, scatter_dimension=0, tiled=True),
        lax.psum_scatter(grad_ckey, BOTH, scatter_dimension=0, tiled=True),
        lax.psum_scatter(grad_cvalue, BOTH, scatter_dimension=0, tiled=True),
        lax.psum_scatter(grad_cout, BOTH, scatter_dimension=0, tiled=True),
        lax.psum_scatter(grad_cqbias, BOTH, scatter_dimension=0, tiled=True),
        lax.psum_scatter(grad_cvbias, BOTH, scatter_dimension=0, tiled=True),
        lax.psum_scatter(grad_cobias, BOTH, scatter_dimension=0, tiled=True),
        lax.psum_scatter(grad_cgain, BOTH, scatter_dimension=0, tiled=True),
        lax.psum_scatter(grad_cshift, BOTH, scatter_dimension=0, tiled=True),
    )
    grad_hidden1, grad_sgain, grad_sshift = norm_back(hidden_one, sgain, sshift, grad_first)
    self_branch = grad_hidden1.astype(jnp.bfloat16)
    grad_out = left_product(self_low, self_branch)
    grad_obias = row_total(self_branch)
    self_up = right_product(self_branch, out_full).astype(jnp.bfloat16)
    self_delta = head_delta(self_up, attn_self)
    sq_grad, sk_grad, sv_grad = attend_back(
        query_self,
        key_self,
        value_self,
        self_up,
        logsum_self,
        self_delta,
        target_ids,
        target_ids,
        True,
    )
    sq_low = sq_grad.astype(jnp.bfloat16)
    sk_low = sk_grad.astype(jnp.bfloat16)
    sv_low = sv_grad.astype(jnp.bfloat16)
    grad_query = left_product(inputs, sq_low)
    grad_qbias = row_total(sq_low)
    grad_key = left_product(inputs, sk_low)
    grad_value = left_product(inputs, sv_low)
    grad_vbias = row_total(sv_low)
    tokens_grad = (
        grad_hidden1
        + right_product(sq_low, query_full)
        + right_product(sk_low, key_full)
        + right_product(sv_low, value_full)
    )
    self_grads = (
        lax.psum_scatter(grad_query, BOTH, scatter_dimension=0, tiled=True),
        lax.psum_scatter(grad_key, BOTH, scatter_dimension=0, tiled=True),
        lax.psum_scatter(grad_value, BOTH, scatter_dimension=0, tiled=True),
        lax.psum_scatter(grad_out, BOTH, scatter_dimension=0, tiled=True),
        lax.psum_scatter(grad_qbias, BOTH, scatter_dimension=0, tiled=True),
        lax.psum_scatter(grad_vbias, BOTH, scatter_dimension=0, tiled=True),
        lax.psum_scatter(grad_obias, BOTH, scatter_dimension=0, tiled=True),
        lax.psum_scatter(grad_sgain, BOTH, scatter_dimension=0, tiled=True),
        lax.psum_scatter(grad_sshift, BOTH, scatter_dimension=0, tiled=True),
    )
    return (
        (output[None], tokens_grad[None], memory_grad[None])
        + tuple(self_grads)
        + tuple(cross_grads)
        + tuple(feed_grads)
    )


LOW = jnp.bfloat16
WIDE = jnp.float32
MESH = pl.DeviceIdType.MESH
VMEM_BYTES = 64 << 20
ALL2 = pl.ds(0, 2)
ALL4 = pl.ds(0, 4)


def place():
    b, s = lax.axis_index(BATCH), lax.axis_index(SEQ)
    return (lax.div(b, 2), lax.rem(b, 2), lax.rem(s, 2), lax.div(s, 2))


def device(x, c, y, z):
    return (2 * x + c, 2 * z + y)


class Peers:
    def __init__(self):
        self.x, self.c, self.y, self.z = place()
        x, c, y, z = self.x, self.c, self.y, self.z
        b, s = lax.axis_index(BATCH), lax.axis_index(SEQ)
        self.across_x = device(1 - x, c, y, z)
        self.across_y = device(x, c, 1 - y, z)
        self.sibling = device(x, 1 - c, y, z)
        self.along_z = [device(x, c, y, lax.rem(z + k, 4)) for k in (1, 2, 3)]
        self.after = (b, lax.rem(s + 1, 8))
        self.before = (b, lax.rem(s + 7, 8))
        self.mirror = (b, 7 - s)

    def all(self):
        return [
            self.across_x, self.across_y, self.sibling, *self.along_z, self.after, self.before, self.mirror,
        ]

    def meet(self):
        barrier = pltpu.get_barrier_semaphore()
        for peer in self.all():
            pl.semaphore_signal(barrier, inc=1, device_id=peer, device_id_type=MESH)
        pl.semaphore_wait(barrier, len(self.all()))


class Wires:
    def __init__(self, send, recv):
        self.send, self.recv, self.used = send, recv, 0

    def copies(self, pairs, target):
        made = []
        for source, landing in pairs:
            made.append(
                pltpu.make_async_remote_copy(
                    src_ref=source,
                    dst_ref=landing,
                    send_sem=self.send.at[self.used],
                    recv_sem=self.recv.at[self.used],
                    device_id=target,
                    device_id_type=MESH,
                )
            )
            self.used += 1
        return made


def start(copies):
    for copy in copies:
        copy.start()


def landed(copies):
    for copy in copies:
        copy.wait_recv()


def sent(copies):
    for copy in copies:
        copy.wait_send()


class Gather:
    def __init__(self, peers, wires, mats, rests, outer, vectors):
        self.peers, self.wires = peers, wires
        self.mats, self.rests, self.outer, self.vectors = mats, rests, outer, vectors
        self.steps = [{} for _ in range(8)]
        self.done = []

    def parts(self, unit, x, c, z, y):
        both = y is None
        if unit >= 6:
            rows = pl.ds(48 * (unit - 6), 48)
            return [self.outer.at[x, c, z, ALL2 if both else y, rows]]
        mats = pl.ds(2 * unit, 2)
        if both:
            refs = [self.mats.at[mats, x, c, z, pl.ds(0, 16)], self.mats.at[mats, x, c, z, pl.ds(32, 16)]]
        else:
            refs = [self.mats.at[mats, x, c, z, pl.ds(pl.multiple_of(32 * y, 16), 16)]]
        refs.append(self.rests.at[unit, x, c, z, ALL2 if both else y])
        if unit == 0:
            refs.append(self.vectors.at[x, c, z, ALL2 if both else y])
        return refs

    def send(self, unit, name, spot, target):
        pairs = [(part, part) for part in self.parts(unit, *spot)]
        copies = self.wires.copies(pairs, target)
        start(copies)
        self.steps[unit][name] = copies
        self.done += copies

    def z_start(self, unit):
        p = self.peers
        for k, peer in enumerate(p.along_z):
            self.send(unit, ("z", k), (p.x, p.c, p.z, p.y), peer)

    def first(self, unit):
        p = self.peers
        for k in range(3):
            landed(self.steps[unit]["z", k])
        self.send(unit, "first", (p.x, p.c, ALL4, p.y), p.across_y if unit % 2 else p.across_x)

    def second(self, unit):
        p = self.peers
        landed(self.steps[unit]["first"])
        if unit % 2:
            self.send(unit, "second", (p.x, p.c, ALL4, None), p.across_x)
            self.send(unit, "near", (p.x, p.c, ALL4, None), p.sibling)
        else:
            self.send(unit, "second", (ALL2, p.c, ALL4, p.y), p.across_y)
            self.send(unit, "near", (ALL2, p.c, ALL4, p.y), p.sibling)

    def third(self, unit):
        p = self.peers
        landed(self.steps[unit]["second"])
        if unit % 2:
            self.send(unit, "far", (1 - p.x, p.c, ALL4, None), p.sibling)
        else:
            self.send(unit, "far", (ALL2, p.c, ALL4, 1 - p.y), p.sibling)

    def last(self, unit):
        landed(self.steps[unit]["near"])
        landed(self.steps[unit]["far"])


def gather_pack(y, x, c, z, squares, inner, outer, small, mats, rests, whole_outer, vectors):
    def split(values):
        values = values.astype(WIDE)
        body = jnp.where(y == 0, values[0:16], values[8:24])
        rest = jnp.where(y == 0, values[16:24], values[0:8])
        return (body.astype(LOW), rest)

    for unit in range(6):
        rests_of = []
        for k in range(2):
            m = 2 * unit + k
            values = squares[m][...] if m < 8 else inner[:, 768 * (m - 8) : 768 * (m - 7)]
            body, rest = split(values)
            mats[m, x, c, z, pl.ds(pl.multiple_of(32 * y, 16), 16), :] = body
            rests_of.append(rest)
        rests[unit, x, c, z, y] = jnp.concatenate(rests_of, axis=0).astype(LOW)
    whole_outer[x, c, z, y] = outer[...]
    index = (2 * x + c) * 8 + 2 * z + y
    wide = small[...].astype(WIDE)
    row = lax.broadcasted_iota(jnp.int32, (16, 128), 0)
    by24 = pltpu.roll(wide, lax.rem(24 * index, 128), 1)
    by96 = pltpu.roll(wide, lax.rem(96 * index, 128), 1)
    vectors[x, c, z, y] = jnp.where(row == 13, by96, by24).astype(LOW)


def merge_rests(unit, mats, rests):
    def one(step, carry):
        x, c, z = lax.div(step, 8), lax.rem(lax.div(step, 4), 2), lax.rem(step, 4)
        low_half = rests[unit, x, c, z, 0].astype(WIDE)
        high_half = rests[unit, x, c, z, 1].astype(WIDE)
        mats[2 * unit, x, c, z, 16:32, :] = jnp.concatenate(
            [low_half[0:8], high_half[0:8]], axis=0
        ).astype(LOW)
        mats[2 * unit + 1, x, c, z, 16:32, :] = jnp.concatenate(
            [low_half[8:16], high_half[8:16]], axis=0
        ).astype(LOW)
        return carry

    lax.fori_loop(0, 16, one, 0)


def gather_kernel(*refs):
    squares, refs = refs[:8], refs[8:]
    inner, outer, small, tokens, memory = refs[:5]
    mats, whole_outer, vectors, tokens_two, memory_three = refs[5:10]
    rests, send, recv = refs[10:]
    peers = Peers()
    x, c, y, z = peers.x, peers.c, peers.y, peers.z
    gather_pack(y, x, c, z, squares, inner, outer, small, mats, rests, whole_outer, vectors)
    tokens_two[128:256, :] = tokens[...]
    peers.meet()
    wires = Wires(send, recv)
    weights = Gather(peers, wires, mats, rests, whole_outer, vectors)
    weights.z_start(0)
    weights.z_start(1)
    left = wires.copies([(tokens, tokens_two.at[pl.ds(0, 128)])], peers.after)
    mirrored = wires.copies([(memory, memory_three.at[1])], peers.mirror)
    start(left)
    start(mirrored)
    weights.z_start(2)
    weights.z_start(3)
    spread = []
    for pair in range(6):
        if pair < 4:
            for unit in (2 * pair, 2 * pair + 1):
                weights.first(unit)
            if pair + 2 < 4:
                weights.z_start(2 * pair + 4)
                weights.z_start(2 * pair + 5)
        if 1 <= pair < 5:
            for unit in (2 * pair - 2, 2 * pair - 1):
                weights.second(unit)
        if pair == 1:
            landed(mirrored)
            spread = wires.copies([(memory_three.at[1], memory_three.at[2])], peers.after)
            spread += wires.copies([(memory_three.at[1], memory_three.at[0])], peers.before)
            start(spread)
        if pair >= 2:
            for unit in (2 * pair - 4, 2 * pair - 3):
                weights.third(unit)
    for unit in range(8):
        weights.last(unit)
        if unit < 6:
            merge_rests(unit, mats, rests)
    landed(left)
    landed(spread)
    sent(weights.done + left + mirrored + spread)


def vmem():
    return pl.BlockSpec(memory_space=pltpu.VMEM)


def gather_call(squares, inner, outer, small, tokens, memory):
    shapes = [
        jax.ShapeDtypeStruct((12, 2, 2, 4, 48, 768), LOW),
        jax.ShapeDtypeStruct((2, 2, 4, 2, 96, 768), LOW),
        jax.ShapeDtypeStruct((2, 2, 4, 2, 16, 128), LOW),
        jax.ShapeDtypeStruct((256, 768), LOW),
        jax.ShapeDtypeStruct((3, 128, 768), LOW),
    ]
    return pl.pallas_call(
        gather_kernel,
        out_shape=shapes,
        in_specs=[vmem()] * 13,
        out_specs=[vmem()] * 5,
        scratch_shapes=[
            pltpu.VMEM((6, 2, 2, 4, 2, 16, 768), LOW),
            pltpu.SemaphoreType.DMA((160,)),
            pltpu.SemaphoreType.DMA((160,)),
        ],
        compiler_params=pltpu.CompilerParams(
            collective_id=0, has_side_effects=True, vmem_limit_bytes=VMEM_BYTES
        ),
    )(*squares, inner, outer, small, tokens, memory)


def dot(left, right):
    return jnp.dot(left, right, preferred_element_type=WIDE)


def dot_nt(left, right):
    return lax.dot_general(left, right, (((1,), (1,)), ((), ())), preferred_element_type=WIDE)


def dot_tn(left, right):
    return lax.dot_general(left, right, (((0,), (0,)), ((), ())), preferred_element_type=WIDE)


def strip(n):
    return slice(256 * n, 256 * n + 256)


def columns(mats, m, n):
    return mats[m, :, :, :, :, strip(n)].reshape(768, 256)


def rows(mats, m, x):
    return mats[m, x].reshape(384, 768)


def outer_columns(outer, j, n):
    return outer[j // 2, j % 2, :, :, :, strip(n)].reshape(768, 256)


def outer_rows(outer, j, half):
    return outer[j // 2, j % 2, 2 * half : 2 * half + 2].reshape(384, 768)


def unpack_vectors(vectors, vec, inner_bias):
    lane = lax.broadcasted_iota(jnp.int32, (16, 128), 1)

    def shard(d):
        b, s = d // 8, d % 8
        return vectors[b // 2, b % 2, s // 2, s % 2].astype(WIDE)

    for width, tiles, ref in ((24, 6, vec), (96, 24, inner_bias)):
        for t in range(tiles):
            first = (128 * t) // width
            final = (128 * t + 127) // width
            total = shard(first)
            for d in range(first + 1, final + 1):
                total = jnp.where(lane >= width * d - 128 * t, shard(d), total)
            if width == 24:
                ref[:, 128 * t : 128 * t + 128] = total
            else:
                ref[0:1, 128 * t : 128 * t + 128] = total[13:14]


def pack_vectors(vec, inner_bias, c, place_at):
    lane = lax.broadcasted_iota(jnp.int32, (16, 128), 1)
    row = lax.broadcasted_iota(jnp.int32, (16, 128), 0)

    def shard(ref, width, d):
        t, offset = width * d // 128, width * d % 128
        block = ref[:, 128 * t : 128 * t + 128]
        if offset + width > 128:
            block = jnp.where(lane >= offset, block, ref[:, 128 * t + 128 : 128 * t + 256])
        return block

    for d in range(32):
        b, s = d // 8, d % 8
        block = shard(vec, 24, d)
        t, offset = 96 * d // 128, 96 * d % 128
        bias = inner_bias[0:1, 128 * t : 128 * t + 128]
        if offset + 96 > 128:
            bias = jnp.where(lane[0:1] >= offset, bias, inner_bias[0:1, 128 * t + 128 : 128 * t + 256])
        place_at(b % 2, b // 2, s // 2, s % 2, jnp.where(row == 13, jnp.broadcast_to(bias, (16, 128)), block))


def centered(values):
    center = values - jnp.mean(values, axis=-1, keepdims=True)
    scale = lax.rsqrt(jnp.mean(center * center, axis=-1, keepdims=True) + EPSILON)
    return (center * scale, scale)


def norm_grad(unit_values, scale, gain, grad):
    scaled = grad * gain
    mean = jnp.mean(scaled, axis=-1, keepdims=True)
    along = jnp.mean(scaled * unit_values, axis=-1, keepdims=True)
    return (scaled - mean - unit_values * along) * scale


def total_rows(values):
    return jnp.sum(values.astype(WIDE), axis=0, keepdims=True)


def lane_halves():
    lane = lax.broadcasted_iota(jnp.int32, (128, 128), 1)
    low_half = jnp.where(lane < 64, 1.0, 0.0).astype(LOW)
    high_half = jnp.where(lane < 64, 0.0, 1.0).astype(LOW)
    return (lane < 64, low_half, high_half)


def pair_rows(block, low_half, high_half):
    return jnp.concatenate([block * low_half, block * high_half], axis=0)


def attention(queries, keys, values, mask, probs, context):
    pick, low_half, high_half = lane_halves()

    def heads(h, carry):
        here = pl.ds(pl.multiple_of(128 * h, 128), 128)
        both = pair_rows(queries[:, here], low_half, high_half)
        bias = mask[...]
        scores = dot_nt(both, keys[:, here]) * SCALE + jnp.concatenate([bias, bias], axis=0)
        weights = jnp.exp(scores - jnp.max(scores, axis=1, keepdims=True))
        weights = weights * (1.0 / jnp.sum(weights, axis=1, keepdims=True))
        rounded = weights.astype(LOW)
        probs[h] = rounded
        mixed = dot(rounded, values[:, here])
        context[:, here] = jnp.where(pick, mixed[:128], mixed[128:]).astype(LOW)
        return carry

    lax.fori_loop(0, 6, heads, 0)


def attention_back(queries, keys, values, upstream, probs, dqueries, dkeys, dvalues, count):
    pick, low_half, high_half = lane_halves()

    def heads(h, carry):
        here = pl.ds(pl.multiple_of(128 * h, 128), 128)
        both = pair_rows(queries[:, here], low_half, high_half)
        both_up = pair_rows(upstream[:, here], low_half, high_half)
        dprobs = dot_nt(both_up, values[:, here])
        weights = probs[h].astype(WIDE)
        delta = jnp.sum(weights * dprobs, axis=1, keepdims=True)
        dscores = (weights * (dprobs - delta) * SCALE).astype(LOW)
        mixed = dot(dscores, keys[:, here])
        dqueries[:, here] = jnp.where(pick, mixed[:128], mixed[128:]).astype(LOW)
        dkeys[0:count, here] = dot_tn(dscores, both).astype(LOW)
        dvalues[0:count, here] = dot_tn(probs[h], both_up).astype(LOW)
        return carry

    lax.fori_loop(0, 6, heads, 0)


class Grads:
    ORDER = (6, 7, 4, 5, 2, 3, 0, 1)

    def __init__(self, peers, wires, held, r0, r1_even, r1_odd, r2, out, mine, credit):
        self.peers, self.wires, self.held = peers, wires, held
        self.r0, self.r1_even, self.r1_odd, self.r2, self.out = r0, r1_even, r1_odd, r2, out
        self.mine, self.credit = mine, credit
        self.stage = {}
        self.open = []
        self.first_sends = {}

    def at(self, unit):
        return self.ORDER.index(unit)

    def slot(self, unit, c):
        return jnp.where(c == self.peers.c, unit, 8 + self.at(unit) % 4)

    def ready(self, unit):
        turn = self.at(unit)
        if turn >= 4:
            sent(self.first_sends.pop(self.ORDER[turn - 4]))

    def ship(self, pairs, target):
        copies = self.wires.copies(pairs, target)
        start(copies)
        self.open += copies
        return copies

    def step0(self, unit):
        turn = self.at(unit)
        if turn >= 4:
            pl.semaphore_wait(self.credit, 1)
        ring = turn % 4
        copies = self.wires.copies([(self.held.at[8 + ring], self.r0.at[ring])], self.peers.sibling)
        start(copies)
        self.first_sends[unit] = copies
        self.stage[unit] = copies

    def step1(self, unit):
        p, held = self.peers, self.held
        landed(self.stage[unit])
        turn = self.at(unit)
        ring = turn % 4

        def add(i, carry):
            j, k = lax.div(i, 4), lax.rem(i, 4)
            held[unit, j, k] = held[unit, j, k] + self.r0[ring, j, k]
            return carry

        lax.fori_loop(0, 8, add, 0)
        if turn < 4:
            pl.semaphore_signal(self.credit, inc=1, device_id=p.sibling, device_id_type=MESH)
        if unit % 2:
            pairs = [(held.at[unit, 1 - p.x], self.r1_odd.at[unit // 2])]
            self.stage[unit] = self.ship(pairs, p.across_x)
        else:
            pairs = [(held.at[unit, ALL2, ALL4, 1 - p.y], self.r1_even.at[unit // 2])]
            self.stage[unit] = self.ship(pairs, p.across_y)

    def step2(self, unit):
        p, held = self.peers, self.held
        landed(self.stage[unit])

        def add(i, carry):
            if unit % 2:
                held[unit, p.x, i] = held[unit, p.x, i] + self.r1_odd[unit // 2, i]
            else:
                for j in range(2):
                    held[unit, j, i, p.y] = held[unit, j, i, p.y] + self.r1_even[unit // 2, j, i]
            return carry

        lax.fori_loop(0, 4, add, 0)
        if unit % 2:
            pairs = [(held.at[unit, p.x, ALL4, 1 - p.y], self.r2.at[unit])]
            self.stage[unit] = self.ship(pairs, p.across_y)
        else:
            pairs = [(held.at[unit, 1 - p.x, ALL4, p.y], self.r2.at[unit])]
            self.stage[unit] = self.ship(pairs, p.across_x)

    def step3(self, unit):
        p, held = self.peers, self.held
        landed(self.stage[unit])

        def add(i, carry):
            held[unit, p.x, i, p.y] = held[unit, p.x, i, p.y] + self.r2[unit, i]
            return carry

        lax.fori_loop(0, 4, add, 0)
        copies = []
        for k in (1, 2, 3):
            source = held.at[unit, p.x, lax.rem(p.z + k, 4), p.y]
            copies += self.ship([(source, self.out.at[unit, k - 1])], p.along_z[k - 1])
        self.stage[unit] = copies
        self.mine[unit] = held[unit, p.x, p.z, p.y]

    def finish(self):
        for unit in self.ORDER:
            landed(self.stage[unit])
        for copies in self.first_sends.values():
            sent(copies)
        sent(self.open)

    def pair_grad(self, unit, first_left, first_right, second_left, second_right):
        self.ready(unit)
        for x in range(2):
            here = slice(384 * x, 384 * x + 384)
            one_left = jnp.transpose(first_left[:, here])
            two_left = jnp.transpose(second_left[:, here])
            for n in range(3):
                s = strip(n)
                one = dot(one_left, first_right[:, s])
                two = dot(two_left, second_right[:, s])
                for c in range(2):
                    slot = self.slot(unit, c)
                    for z in range(4):
                        for y in range(2):
                            base = 24 * (8 * c + 2 * z + y)
                            body = base + 8 * y
                            rest = base + 16 * (1 - y)
                            self.held[slot, x, z, y, 0:16, s] = one[body : body + 16].astype(LOW)
                            self.held[slot, x, z, y, 16:32, s] = two[body : body + 16].astype(LOW)
                            self.held[slot, x, z, y, 32:48, s] = jnp.concatenate(
                                [one[rest : rest + 8], two[rest : rest + 8]], axis=0
                            ).astype(LOW)

    def outer_grad(self, hidden, upstream):
        for j in range(4):
            x, c = j // 2, j % 2
            for half in range(2):
                here = slice(768 * j + 384 * half, 768 * j + 384 * half + 384)
                left = jnp.transpose(hidden[:, here])
                for n in range(3):
                    s = strip(n)
                    one = dot(left, upstream[:, s])
                    for unit in (6, 7):
                        slot = self.slot(unit, c)
                        for k in range(4):
                            base = 96 * k + 48 * (unit - 6)
                            z, y = 2 * half + k // 2, k % 2
                            self.held[slot, x, z, y, :, s] = one[base : base + 48].astype(LOW)


def layer_kernel(*refs):
    mats, outer, vectors, tokens, memory, cotangent, mask_self, mask_cross = refs[:8]
    output, out, mine, vout, left_out, memory_out, tokens_part = refs[8:15]
    scratch = refs[15:]
    (
        vec, inner_bias, query, key, value, probs, context, unit1, first_low,
        query2, key2, value2, probs2, context2, unit2, second_low,
        hidden, slope, total, grad, branch, upstream, dquery, dkey, dvalue,
        gvec, ginner,
        held, r0, r1_even, r1_odd, r2, vheld, v0, v1, v2, left_part, memory_parts,
        from_after, from_before, sum_up, credit, send, recv,
    ) = scratch
    peers = Peers()
    peers.meet()
    wires = Wires(send, recv)
    grads = Grads(peers, wires, held, r0, r1_even, r1_odd, r2, out, mine, credit)
    own = slice(128, 256)

    unpack_vectors(vectors, vec, inner_bias)

    def vector(j):
        return vec[j : j + 1, :]

    for n in range(3):
        s = strip(n)
        query[:, s] = (dot(tokens[own, :], columns(mats, 0, n)) + vec[0:1, s]).astype(LOW)
        key[:, s] = dot(tokens[...], columns(mats, 1, n)).astype(LOW)
        value[:, s] = (dot(tokens[...], columns(mats, 2, n)) + vec[1:2, s]).astype(LOW)
    attention(query, key, value, mask_self, probs, context)
    for n in range(3):
        s = strip(n)
        total[:, s] = (
            tokens[own, s].astype(WIDE) + dot(context[...], columns(mats, 3, n)) + vec[2:3, s]
        )
    unit, scale1 = centered(total[...])
    unit1[...] = unit
    first = unit * vector(3) + vector(4)
    total[...] = first
    first_low[...] = first.astype(LOW)
    for n in range(3):
        s = strip(n)
        query2[:, s] = (dot(first_low[...], columns(mats, 4, n)) + vec[5:6, s]).astype(LOW)
        key2[:, s] = dot(memory[...], columns(mats, 5, n)).astype(LOW)
        value2[:, s] = (dot(memory[...], columns(mats, 6, n)) + vec[6:7, s]).astype(LOW)
    attention(query2, key2, value2, mask_cross, probs2, context2)
    for n in range(3):
        s = strip(n)
        total[:, s] = total[:, s] + dot(context2[...], columns(mats, 7, n)) + vec[7:8, s]
    unit, scale2 = centered(total[...])
    unit2[...] = unit
    second = unit * vector(8) + vector(9)
    total[...] = second + vector(10)
    second_low[...] = second.astype(LOW)
    for j in range(4):
        for n in range(3):
            s = slice(768 * j + 256 * n, 768 * j + 256 * n + 256)
            pre = dot(second_low[...], columns(mats, 8 + j, n)) + inner_bias[0:1, s]
            normal = 0.5 + 0.5 * lax.erf(pre * 0.7071067811865476)
            hidden[:, s] = (pre * normal).astype(LOW)
            slope[:, s] = (
                normal + pre * (0.3989422804014327 * jnp.exp(-0.5 * pre * pre))
            ).astype(LOW)
        for n in range(3):
            s = strip(n)
            total[:, s] = total[:, s] + dot(
                hidden[:, 768 * j : 768 * j + 768], outer_columns(outer, j, n)
            )
    unit, scale3 = centered(total[...])
    output[...] = (unit * vector(11) + vector(12)).astype(LOW)
    arrived = cotangent[...].astype(WIDE)
    gvec[11:12, :] = total_rows(arrived * unit)
    gvec[12:13, :] = total_rows(arrived)
    dhidden = norm_grad(unit, scale3, vector(11), arrived)
    grad[...] = dhidden
    branch[...] = dhidden.astype(LOW)
    gvec[10:11, :] = total_rows(branch[...])
    grads.outer_grad(hidden, branch)
    grads.step0(6)
    grads.step0(7)
    for j in range(4):
        for half in range(2):
            s = slice(768 * j + 384 * half, 768 * j + 384 * half + 384)
            raised = dot_nt(branch[...], outer_rows(outer, j, half)) * slope[:, s].astype(WIDE)
            raised = raised.astype(LOW)
            slope[:, s] = raised
            ginner[0:1, s] = total_rows(raised)
    for unit in (4, 5):
        spans_of = [slope.at[:, pl.ds(768 * j, 768)] for j in (2 * unit - 8, 2 * unit - 7)]
        grads.pair_grad(unit, second_low, spans_of[0], second_low, spans_of[1])
        grads.step0(unit)
    for x in range(2):
        s = slice(384 * x, 384 * x + 384)
        summed = grad[:, s]
        for j in range(4):
            summed = summed + dot_nt(slope[:, 768 * j : 768 * j + 768], rows(mats, 8 + j, x))
        grad[:, s] = summed
    grads.step1(6)
    grads.step1(7)
    arrived = grad[...]
    unit = unit2[...]
    gvec[8:9, :] = total_rows(arrived * unit)
    gvec[9:10, :] = total_rows(arrived)
    dhidden = norm_grad(unit, scale2, vector(8), arrived)
    grad[...] = dhidden
    branch[...] = dhidden.astype(LOW)
    gvec[7:8, :] = total_rows(branch[...])
    for x in range(2):
        upstream[:, 384 * x : 384 * x + 384] = dot_nt(branch[...], rows(mats, 7, x)).astype(LOW)
    grads.step1(4)
    grads.step1(5)
    attention_back(query2, key2, value2, upstream, probs2, dquery, dkey, dvalue, 384)
    grads.step2(6)
    grads.step2(7)
    gvec[5:6, :] = total_rows(dquery[...])
    gvec[6:7, :] = total_rows(dvalue[...])
    for x in range(2):
        s = slice(384 * x, 384 * x + 384)
        grad[:, s] = grad[:, s] + dot_nt(dquery[...], rows(mats, 4, x))
        backed = dot_nt(dkey[...], rows(mats, 5, x)) + dot_nt(dvalue[...], rows(mats, 6, x))
        for block in range(3):
            memory_parts[block, :, s] = backed[128 * block : 128 * block + 128].astype(LOW)
    near = grads.ship([(memory_parts.at[0], from_after)], peers.after)
    near += grads.ship([(memory_parts.at[2], from_before)], peers.before)
    grads.pair_grad(2, first_low, dquery, memory, dkey)
    grads.step0(2)
    grads.pair_grad(3, memory, dvalue, context2, branch)
    grads.step0(3)
    grads.step2(4)
    grads.step2(5)
    grads.step3(6)
    grads.step3(7)
    arrived = grad[...]
    unit = unit1[...]
    gvec[3:4, :] = total_rows(arrived * unit)
    gvec[4:5, :] = total_rows(arrived)
    dhidden = norm_grad(unit, scale1, vector(3), arrived)
    grad[...] = dhidden
    branch[...] = dhidden.astype(LOW)
    gvec[2:3, :] = total_rows(branch[...])
    for x in range(2):
        upstream[:, 384 * x : 384 * x + 384] = dot_nt(branch[...], rows(mats, 3, x)).astype(LOW)
    grads.step1(2)
    grads.step1(3)
    attention_back(query, key, value, upstream, probs, dquery, dkey, dvalue, 256)
    dkey_two, dvalue_two = dkey.at[pl.ds(0, 256)], dvalue.at[pl.ds(0, 256)]
    grads.pair_grad(0, tokens.at[pl.ds(128, 128)], dquery, tokens, dkey_two)
    grads.step0(0)
    grads.pair_grad(1, tokens, dvalue_two, context, branch)
    grads.step0(1)
    gvec[0:1, :] = total_rows(dquery[...])
    gvec[1:2, :] = total_rows(dvalue_two[...])
    gvec[13:16, :] = jnp.zeros((3, 768), WIDE)

    def put(c, x, z, y, block):
        vheld[c, x, z, y] = block

    pack_vectors(gvec, ginner, peers.c, put)
    c, x, y, z = peers.c, peers.x, peers.y, peers.z
    vstage = grads.ship([(vheld.at[1 - c], v0)], peers.sibling)
    grads.step3(4)
    grads.step3(5)
    grads.step2(2)
    grads.step2(3)
    for x_ in range(2):
        s = slice(384 * x_, 384 * x_ + 384)
        backed = dot_nt(dkey_two[...], rows(mats, 1, x_)) + dot_nt(dvalue_two[...], rows(mats, 2, x_))
        left_part[:, s] = backed[0:128].astype(LOW)
        tokens_part[:, s] = grad[:, s] + dot_nt(dquery[...], rows(mats, 0, x_)) + backed[128:256]
    left = grads.ship([(left_part, left_out)], peers.before)
    grads.step1(0)
    grads.step1(1)
    landed(near)
    sum_up[...] = (
        memory_parts[1].astype(WIDE) + from_after[...].astype(WIDE) + from_before[...].astype(WIDE)
    ).astype(LOW)
    home = grads.ship([(sum_up, memory_out)], peers.mirror)
    landed(vstage)
    vheld[c] = vheld[c] + v0[...]
    vstage = grads.ship([(vheld.at[c, ALL2, ALL4, 1 - y], v1)], peers.across_y)
    grads.step3(2)
    grads.step3(3)
    grads.step2(0)
    grads.step2(1)
    landed(vstage)
    for j in range(2):
        for k in range(4):
            vheld[c, j, k, y] = vheld[c, j, k, y] + v1[j, k]
    vstage = grads.ship([(vheld.at[c, 1 - x, ALL4, y], v2)], peers.across_x)
    grads.step3(0)
    grads.step3(1)
    landed(vstage)
    for k in range(4):
        vheld[c, x, k, y] = vheld[c, x, k, y] + v2[k]
    vstage = []
    for k in (1, 2, 3):
        source = vheld.at[c, x, lax.rem(z + k, 4), y]
        vstage += grads.ship([(source, vout.at[k])], peers.along_z[k - 1])
    vout[0] = vheld[c, x, z, y]
    landed(vstage + left + home)
    grads.finish()


def layer_call(mats, outer, vectors, tokens, memory, cotangent, mask_self, mask_cross):
    shapes = [
        jax.ShapeDtypeStruct((128, 768), LOW),
        jax.ShapeDtypeStruct((8, 3, 48, 768), LOW),
        jax.ShapeDtypeStruct((8, 48, 768), LOW),
        jax.ShapeDtypeStruct((4, 16, 128), WIDE),
        jax.ShapeDtypeStruct((128, 768), LOW),
        jax.ShapeDtypeStruct((128, 768), LOW),
        jax.ShapeDtypeStruct((128, 768), WIDE),
    ]
    low = [
        (128, 768), (256, 768), (256, 768), (6, 256, 256), (128, 768),
    ]
    scratch = [pltpu.VMEM((16, 768), WIDE), pltpu.VMEM((8, 3072), WIDE)]
    scratch += [pltpu.VMEM(shape, LOW) for shape in low]
    scratch += [pltpu.VMEM((128, 768), WIDE), pltpu.VMEM((128, 768), LOW)]
    scratch += [pltpu.VMEM(s, LOW) for s in [(128, 768), (384, 768), (384, 768), (6, 256, 384), (128, 768)]]
    scratch += [pltpu.VMEM((128, 768), WIDE), pltpu.VMEM((128, 768), LOW)]
    scratch += [pltpu.VMEM((128, 3072), LOW)] * 2
    scratch += [pltpu.VMEM((128, 768), WIDE)] * 2
    scratch += [pltpu.VMEM(s, LOW) for s in [(128, 768), (128, 768), (128, 768), (384, 768), (384, 768)]]
    scratch += [pltpu.VMEM((16, 768), WIDE), pltpu.VMEM((8, 3072), WIDE)]
    scratch += [
        pltpu.VMEM((12, 2, 4, 2, 48, 768), LOW),
        pltpu.VMEM((4, 2, 4, 2, 48, 768), LOW),
        pltpu.VMEM((4, 2, 4, 48, 768), LOW),
        pltpu.VMEM((4, 4, 2, 48, 768), LOW),
        pltpu.VMEM((8, 4, 48, 768), LOW),
        pltpu.VMEM((2, 2, 4, 2, 16, 128), WIDE),
        pltpu.VMEM((2, 4, 2, 16, 128), WIDE),
        pltpu.VMEM((2, 4, 16, 128), WIDE),
        pltpu.VMEM((4, 16, 128), WIDE),
        pltpu.VMEM((128, 768), LOW),
        pltpu.VMEM((3, 128, 768), LOW),
        pltpu.VMEM((128, 768), LOW),
        pltpu.VMEM((128, 768), LOW),
        pltpu.VMEM((128, 768), LOW),
        pltpu.SemaphoreType.REGULAR,
        pltpu.SemaphoreType.DMA((80,)),
        pltpu.SemaphoreType.DMA((80,)),
    ]
    return pl.pallas_call(
        layer_kernel,
        out_shape=shapes,
        in_specs=[vmem()] * 8,
        out_specs=[vmem(), pl.BlockSpec(memory_space=pl.ANY)] + [vmem()] * 5,
        scratch_shapes=scratch,
        compiler_params=pltpu.CompilerParams(
            collective_id=1, has_side_effects=True, vmem_limit_bytes=VMEM_BYTES
        ),
    )(mats, outer, vectors, tokens, memory, cotangent, mask_self, mask_cross)


def final_kernel(parts, mine, vparts, left, memory_low, tokens_part, *outs):
    tokens_grad, memory_grad, small = outs[:3]
    squares, inner, outer = outs[3:11], outs[11], outs[12]
    b, s = lax.axis_index(BATCH), lax.axis_index(SEQ)
    even = lax.rem(s, 2) == 0
    tokens_grad[...] = tokens_part[...] + left[...].astype(WIDE)
    memory_grad[...] = memory_low[...].astype(WIDE)

    def summed(unit):
        return (
            mine[unit].astype(WIDE) + parts[unit, 0].astype(WIDE)
            + parts[unit, 1].astype(WIDE) + parts[unit, 2].astype(WIDE)
        )

    for unit in range(6):
        total = summed(unit)
        for k in range(2):
            body, rest = total[16 * k : 16 * k + 16], total[32 + 8 * k : 40 + 8 * k]
            matrix = jnp.where(
                even, jnp.concatenate([body, rest], axis=0), jnp.concatenate([rest, body], axis=0)
            )
            m = 2 * unit + k
            if m < 8:
                squares[m][...] = matrix
            else:
                inner[:, 768 * (m - 8) : 768 * (m - 7)] = matrix
    outer[0:48, :] = summed(6)
    outer[48:96, :] = summed(7)
    index = 8 * b + s
    vectors = vparts[0] + vparts[1] + vparts[2] + vparts[3]
    row = lax.broadcasted_iota(jnp.int32, (16, 128), 0)
    by24 = pltpu.roll(vectors, lax.rem(128 * 24 - 24 * index, 128), 1)
    by96 = pltpu.roll(vectors, lax.rem(128 * 96 - 96 * index, 128), 1)
    small[...] = jnp.where(row == 13, by96, by24)


def final_call(parts, mine, vparts, left, memory_low, tokens_part):
    shapes = [
        jax.ShapeDtypeStruct((128, 768), WIDE),
        jax.ShapeDtypeStruct((128, 768), WIDE),
        jax.ShapeDtypeStruct((16, 128), WIDE),
    ]
    shapes += [jax.ShapeDtypeStruct((24, 768), WIDE)] * 8
    shapes += [jax.ShapeDtypeStruct((24, 3072), WIDE), jax.ShapeDtypeStruct((96, 768), WIDE)]
    return pl.pallas_call(
        final_kernel,
        out_shape=shapes,
        in_specs=[vmem()] * 6,
        out_specs=[vmem()] * 13,
        compiler_params=pltpu.CompilerParams(vmem_limit_bytes=32 << 20),
    )(parts, mine, vparts, left, memory_low, tokens_part)


def masks(target_ids, source_ids):
    first = lax.axis_index(SEQ) * 128
    query_ids = lax.dynamic_slice_in_dim(target_ids, first, 128, 0)
    padded = jnp.concatenate([jnp.full((128,), -1, jnp.int32), target_ids])
    key_ids = lax.dynamic_slice_in_dim(padded, first, 256, 0)
    offset = jnp.arange(256, dtype=jnp.int32)[None, :] - 128
    causal = offset <= jnp.arange(128, dtype=jnp.int32)[:, None]
    allowed = jnp.logical_and(query_ids[:, None] == key_ids[None, :], causal)
    begin = lax.rem(6 + 8 - lax.axis_index(SEQ), 8) * 128
    doubled = jnp.concatenate([source_ids, source_ids])
    cross_ids = lax.dynamic_slice_in_dim(doubled, begin, 384, 0)
    crossed = query_ids[:, None] == cross_ids[None, :]
    return (
        jnp.where(allowed, 0.0, NEGATIVE).astype(WIDE),
        jnp.where(crossed, 0.0, NEGATIVE).astype(WIDE),
    )


def fast_shards(tokens, memory, target_segments, memory_segments, cotangent, *weights):
    squares = weights[0:4] + weights[9:13]
    inner, inner_bias, outer = weights[18:21]
    smalls = list(weights[4:9]) + list(weights[13:18]) + list(weights[21:24])
    packed = jnp.zeros((16, 128), LOW)
    packed = jnp.concatenate(
        [
            jnp.pad(jnp.stack(smalls), ((0, 0), (0, 104))),
            jnp.pad(inner_bias[None], ((0, 0), (0, 32))),
            jnp.zeros((2, 128), LOW),
        ]
    )
    mask_self, mask_cross = masks(target_segments[0], memory_segments[0])
    mats, whole_outer, vectors, tokens_two, memory_three = gather_call(
        squares, inner, outer, packed, tokens[0], memory[0]
    )
    output, parts, mine, vparts, left, memory_low, tokens_part = layer_call(
        mats, whole_outer, vectors, tokens_two, memory_three.reshape(384, 768), cotangent[0], mask_self, mask_cross
    )
    results = final_call(parts, mine, vparts, left, memory_low, tokens_part)
    tokens_grad, memory_grad, small = results[:3]
    matrices, inner_grad, outer_grad = results[3:11], results[11], results[12]
    vector = [small[j, 0:24] for j in range(13)]
    return (
        (output[None], tokens_grad[None], memory_grad[None])
        + tuple(matrices[0:4]) + tuple(vector[0:5])
        + tuple(matrices[4:8]) + tuple(vector[5:10])
        + (inner_grad, small[13, 0:96], outer_grad) + tuple(vector[10:13])
    )


def fits(mesh):
    return mesh.shape[BATCH] == 4 and mesh.shape[SEQ] == 8


def solution(mesh):
    in_specs = (
        P(BATCH, SEQ, None),
        P(BATCH, SEQ, None),
        P(BATCH, None),
        P(BATCH, None),
        P(BATCH, SEQ, None),
        P(BOTH, None),
        P(BOTH, None),
        P(BOTH, None),
        P(BOTH, None),
        P(BOTH),
        P(BOTH),
        P(BOTH),
        P(BOTH),
        P(BOTH),
        P(BOTH, None),
        P(BOTH, None),
        P(BOTH, None),
        P(BOTH, None),
        P(BOTH),
        P(BOTH),
        P(BOTH),
        P(BOTH),
        P(BOTH),
        P(BOTH, None),
        P(BOTH),
        P(BOTH, None),
        P(BOTH),
        P(BOTH),
        P(BOTH),
    )
    out_specs = (
        P(BATCH, SEQ, None),
        P(BATCH, SEQ, None),
        P(BATCH, SEQ, None),
        P(BOTH, None),
        P(BOTH, None),
        P(BOTH, None),
        P(BOTH, None),
        P(BOTH),
        P(BOTH),
        P(BOTH),
        P(BOTH),
        P(BOTH),
        P(BOTH, None),
        P(BOTH, None),
        P(BOTH, None),
        P(BOTH, None),
        P(BOTH),
        P(BOTH),
        P(BOTH),
        P(BOTH),
        P(BOTH),
        P(BOTH, None),
        P(BOTH),
        P(BOTH, None),
        P(BOTH),
        P(BOTH),
        P(BOTH),
    )
    quick = fits(mesh)
    return jax.shard_map(fast_shards if quick else shards, mesh=mesh, in_specs=in_specs, out_specs=out_specs, check_vma=False)
```

```python
from functools import partial

import jax
import jax.numpy as jnp
from jax import lax
from jax.experimental import pallas as pl
from jax.experimental.pallas import tpu as pltpu
from jax.sharding import PartitionSpec as P

BATCH, SEQ = ("batch", "seq")
BOTH = (BATCH, SEQ)
HD = 64
SCALE = 0.125
NEGATIVE = -1e30
EPSILON = 1e-05
block_limit = 1024


def spans(total):
    if total > block_limit and total % block_limit == 0:
        return (block_limit, total // block_limit)
    return (total, 1)


def heads_of(matrix):
    return matrix.reshape(matrix.shape[0], -1, HD)


def normalize(values, gain, shift):
    center = values - jnp.mean(values, axis=-1, keepdims=True)
    spread = jnp.mean(center * center, axis=-1, keepdims=True)
    return center * lax.rsqrt(spread + EPSILON) * gain + shift


def norm_back(values, gain, shift, grad):
    _, pullback = jax.vjp(normalize, values, gain, shift)
    return pullback(grad)


def matmul(left, right):
    return jnp.dot(left, right, preferred_element_type=jnp.float32)


def left_product(left, right):
    return lax.dot_general(
        left, right, (((0,), (0,)), ((), ())), preferred_element_type=jnp.float32
    )


def right_product(left, right):
    return lax.dot_general(
        left, right, (((1,), (1,)), ((), ())), preferred_element_type=jnp.float32
    )


def row_total(matrix):
    return jnp.sum(matrix.astype(jnp.float32), axis=0)


def allowed_mask(query_seg, query_pos, key_seg, key_pos, causal):
    same = query_seg[:, None] == key_seg[None, :]
    if causal:
        same = jnp.logical_and(same, key_pos[None, :] <= query_pos[:, None])
    return same


def block_terms(
    query_block, upstream_block, logsum_block, delta_block, allowed, key_block, value_block
):
    scores = (
        jnp.einsum("qhd,khd->hqk", query_block, key_block, preferred_element_type=jnp.float32)
        * SCALE
    )
    scores = jnp.where(allowed[None], scores, NEGATIVE)
    probs = jnp.where(allowed[None], jnp.exp(scores - logsum_block[:, :, None]), 0.0)
    dprobs = jnp.einsum(
        "qhd,khd->hqk", upstream_block, value_block, preferred_element_type=jnp.float32
    )
    dscores = (probs * (dprobs - delta_block[:, :, None]) * SCALE).astype(jnp.bfloat16)
    return (probs.astype(jnp.bfloat16), dscores)


def attend(queries, keys, values, query_seg, query_pos, key_ids, causal):
    row_count = queries.shape[0]
    head_count = queries.shape[1] // HD
    query_heads = heads_of(queries)
    all_keys, all_values = (
        lax.all_gather(keys, SEQ, axis=0, tiled=True),
        lax.all_gather(values, SEQ, axis=0, tiled=True),
    )
    block_rows, block_count = spans(all_keys.shape[0])

    def scored(index):
        offset = index * block_rows
        key_block = heads_of(lax.dynamic_slice_in_dim(all_keys, offset, block_rows, 0))
        key_pos = offset + jnp.arange(block_rows, dtype=jnp.int32)
        key_seg = lax.dynamic_slice_in_dim(key_ids, offset, block_rows, 0)
        allowed = allowed_mask(query_seg, query_pos, key_seg, key_pos, causal)[None]
        scores = (
            jnp.einsum("qhd,khd->hqk", query_heads, key_block, preferred_element_type=jnp.float32)
            * SCALE
        )
        return (jnp.where(allowed, scores, NEGATIVE), allowed)

    def stat_step(index, state):
        run_max, run_sum = state
        scores, allowed = scored(index)
        new_max = jnp.maximum(run_max, jnp.max(scores, axis=2))
        weights = jnp.where(allowed, jnp.exp(scores - new_max[:, :, None]), 0.0)
        run_sum = run_sum * jnp.exp(run_max - new_max) + jnp.sum(weights, axis=2)
        return (new_max, run_sum)

    run_max, run_sum = lax.fori_loop(
        0,
        block_count,
        stat_step,
        (
            jnp.full((head_count, row_count), NEGATIVE, jnp.float32),
            jnp.zeros((head_count, row_count), jnp.float32),
        ),
    )
    logsum = run_max + jnp.log(run_sum)

    def value_step(index, accum):
        scores, allowed = scored(index)
        probs = jnp.where(allowed, jnp.exp(scores - logsum[:, :, None]), 0.0).astype(jnp.bfloat16)
        value_block = heads_of(
            lax.dynamic_slice_in_dim(all_values, index * block_rows, block_rows, 0)
        )
        return accum + jnp.einsum(
            "hqk,khd->qhd", probs, value_block, preferred_element_type=jnp.float32
        )

    accum = lax.fori_loop(
        0, block_count, value_step, jnp.zeros((row_count, head_count, HD), jnp.float32)
    )
    outcome = accum.reshape(row_count, head_count * HD)
    return (outcome, logsum)


def head_delta(upstream, context):
    row_count = upstream.shape[0]
    return jnp.sum((upstream.astype(jnp.float32) * context).reshape(row_count, -1, HD), axis=2).T


def attend_back(queries, keys, values, upstream, logsum, delta, query_ids, key_ids, causal):
    row_count = queries.shape[0]
    head_count = queries.shape[1] // HD
    own_first = lax.axis_index(SEQ) * row_count
    own_pos = own_first + jnp.arange(row_count, dtype=jnp.int32)
    query_seg = lax.dynamic_slice_in_dim(query_ids, own_first, row_count, 0)
    key_seg = lax.dynamic_slice_in_dim(key_ids, own_first, row_count, 0)
    query_heads = heads_of(queries)
    upstream_heads = heads_of(upstream)
    empty = jnp.zeros((row_count, head_count, HD), jnp.float32)
    key_source = lax.all_gather(keys, SEQ, axis=0, tiled=True)
    value_source = lax.all_gather(values, SEQ, axis=0, tiled=True)
    block_rows, block_count = spans(key_source.shape[0])

    def key_step(index, running):
        local = index * block_rows
        key_block = heads_of(lax.dynamic_slice_in_dim(key_source, local, block_rows, 0))
        value_block = heads_of(lax.dynamic_slice_in_dim(value_source, local, block_rows, 0))
        block_seg = lax.dynamic_slice_in_dim(key_ids, local, block_rows, 0)
        block_pos = local + jnp.arange(block_rows, dtype=jnp.int32)
        allowed = allowed_mask(query_seg, own_pos, block_seg, block_pos, causal)
        probs, dscores = block_terms(
            query_heads, upstream_heads, logsum, delta, allowed, key_block, value_block
        )
        return running + jnp.einsum(
            "hqk,khd->qhd", dscores, key_block, preferred_element_type=jnp.float32
        )

    dqueries = lax.fori_loop(0, block_count, key_step, empty)
    all_logsum, all_delta = (
        lax.all_gather(logsum, SEQ, axis=1, tiled=True),
        lax.all_gather(delta, SEQ, axis=1, tiled=True),
    )
    key_heads = heads_of(keys)
    value_heads = heads_of(values)
    piece_queries = lax.all_gather(queries, SEQ, axis=0, tiled=True)
    piece_upstream = lax.all_gather(upstream, SEQ, axis=0, tiled=True)
    query_block_rows, block_count = spans(piece_queries.shape[0])

    def query_step(index, running):
        key_total, value_total = running
        local = index * query_block_rows
        query_block = heads_of(lax.dynamic_slice_in_dim(piece_queries, local, query_block_rows, 0))
        upstream_block = heads_of(
            lax.dynamic_slice_in_dim(piece_upstream, local, query_block_rows, 0)
        )
        logsum_block = lax.dynamic_slice_in_dim(all_logsum, local, query_block_rows, 1)
        delta_block = lax.dynamic_slice_in_dim(all_delta, local, query_block_rows, 1)
        block_seg = lax.dynamic_slice_in_dim(query_ids, local, query_block_rows, 0)
        block_pos = local + jnp.arange(query_block_rows, dtype=jnp.int32)
        allowed = allowed_mask(block_seg, block_pos, key_seg, own_pos, causal)
        probs, dscores = block_terms(
            query_block, upstream_block, logsum_block, delta_block, allowed, key_heads, value_heads
        )
        key_total = key_total + jnp.einsum(
            "hqk,qhd->khd", dscores, query_block, preferred_element_type=jnp.float32
        )
        value_total = value_total + jnp.einsum(
            "hqk,qhd->khd", probs, upstream_block, preferred_element_type=jnp.float32
        )
        return (key_total, value_total)

    key_grad, value_grad = lax.fori_loop(0, block_count, query_step, (empty, empty))
    key_grad = key_grad.reshape(row_count, -1)
    value_grad = value_grad.reshape(row_count, -1)
    return (dqueries.reshape(row_count, -1), key_grad, value_grad)


def shards(
    tokens,
    memory,
    target_segments,
    memory_segments,
    cotangent,
    selfquery,
    selfkey,
    selfvalue,
    selfout,
    selfqbias,
    selfvbias,
    selfobias,
    selfgain,
    selfshift,
    crossquery,
    crosskey,
    crossvalue,
    crossout,
    crossqbias,
    crossvbias,
    crossobias,
    crossgain,
    crossshift,
    innerweight,
    innerbias,
    outerweight,
    outerbias,
    finalgain,
    finalshift,
):
    inputs = tokens[0]
    source = memory[0]
    target_ids = target_segments[0]
    source_ids = memory_segments[0]
    row_count = inputs.shape[0]
    own_first = lax.axis_index(SEQ) * row_count
    own_pos = own_first + jnp.arange(row_count, dtype=jnp.int32)
    query_seg = lax.dynamic_slice_in_dim(target_ids, own_first, row_count, 0)
    (
        query_full,
        key_full,
        value_full,
        out_full,
        qbias_full,
        vbias_full,
        obias_full,
        sgain_full,
        sshift_full,
    ) = (
        lax.all_gather(selfquery, BOTH, axis=0, tiled=True),
        lax.all_gather(selfkey, BOTH, axis=0, tiled=True),
        lax.all_gather(selfvalue, BOTH, axis=0, tiled=True),
        lax.all_gather(selfout, BOTH, axis=0, tiled=True),
        lax.all_gather(selfqbias, BOTH, axis=0, tiled=True),
        lax.all_gather(selfvbias, BOTH, axis=0, tiled=True),
        lax.all_gather(selfobias, BOTH, axis=0, tiled=True),
        lax.all_gather(selfgain, BOTH, axis=0, tiled=True),
        lax.all_gather(selfshift, BOTH, axis=0, tiled=True),
    )
    sgain = sgain_full.astype(jnp.float32)
    sshift = sshift_full.astype(jnp.float32)
    query_self = (matmul(inputs, query_full) + qbias_full.astype(jnp.float32)).astype(jnp.bfloat16)
    key_self = matmul(inputs, key_full).astype(jnp.bfloat16)
    value_self = (matmul(inputs, value_full) + vbias_full.astype(jnp.float32)).astype(jnp.bfloat16)
    attn_self, logsum_self = attend(
        query_self, key_self, value_self, query_seg, own_pos, target_ids, True
    )
    self_low = attn_self.astype(jnp.bfloat16)
    hidden_one = (
        inputs.astype(jnp.float32) + matmul(self_low, out_full) + obias_full.astype(jnp.float32)
    )
    first = normalize(hidden_one, sgain, sshift)
    first_low = first.astype(jnp.bfloat16)
    (
        cquery_full,
        ckey_full,
        cvalue_full,
        cout_full,
        cqbias_full,
        cvbias_full,
        cobias_full,
        cgain_full,
        cshift_full,
    ) = (
        lax.all_gather(crossquery, BOTH, axis=0, tiled=True),
        lax.all_gather(crosskey, BOTH, axis=0, tiled=True),
        lax.all_gather(crossvalue, BOTH, axis=0, tiled=True),
        lax.all_gather(crossout, BOTH, axis=0, tiled=True),
        lax.all_gather(crossqbias, BOTH, axis=0, tiled=True),
        lax.all_gather(crossvbias, BOTH, axis=0, tiled=True),
        lax.all_gather(crossobias, BOTH, axis=0, tiled=True),
        lax.all_gather(crossgain, BOTH, axis=0, tiled=True),
        lax.all_gather(crossshift, BOTH, axis=0, tiled=True),
    )
    cgain = cgain_full.astype(jnp.float32)
    cshift = cshift_full.astype(jnp.float32)
    query_cross = (matmul(first_low, cquery_full) + cqbias_full.astype(jnp.float32)).astype(
        jnp.bfloat16
    )
    key_cross = matmul(source, ckey_full).astype(jnp.bfloat16)
    value_cross = (matmul(source, cvalue_full) + cvbias_full.astype(jnp.float32)).astype(
        jnp.bfloat16
    )
    attn_cross, logsum_cross = attend(
        query_cross, key_cross, value_cross, query_seg, own_pos, source_ids, False
    )
    cross_low = attn_cross.astype(jnp.bfloat16)
    hidden_two = first + matmul(cross_low, cout_full) + cobias_full.astype(jnp.float32)
    second = normalize(hidden_two, cgain, cshift)
    second_low = second.astype(jnp.bfloat16)
    inner_full, ibias_full, outer_full, obias_feed, fgain_full, fshift_full = (
        lax.all_gather(innerweight, BOTH, axis=0, tiled=True),
        lax.all_gather(innerbias, BOTH, axis=0, tiled=True),
        lax.all_gather(outerweight, BOTH, axis=0, tiled=True),
        lax.all_gather(outerbias, BOTH, axis=0, tiled=True),
        lax.all_gather(finalgain, BOTH, axis=0, tiled=True),
        lax.all_gather(finalshift, BOTH, axis=0, tiled=True),
    )
    fgain = fgain_full.astype(jnp.float32)
    fshift = fshift_full.astype(jnp.float32)
    smooth = partial(jax.nn.gelu, approximate=False)
    inner_pre = matmul(second_low, inner_full) + ibias_full.astype(jnp.float32)
    activation = smooth(inner_pre).astype(jnp.bfloat16)
    hidden_three = second + matmul(activation, outer_full) + obias_feed.astype(jnp.float32)
    output = normalize(hidden_three, fgain, fshift).astype(jnp.bfloat16)
    grad_hidden3, grad_fgain, grad_fshift = norm_back(
        hidden_three, fgain, fshift, cotangent[0].astype(jnp.float32)
    )
    branch_grad = grad_hidden3.astype(jnp.bfloat16)
    grad_outer = left_product(activation, branch_grad)
    grad_obias_feed = row_total(branch_grad)
    _, gelu_back = jax.vjp(smooth, inner_pre)
    inner_grad = gelu_back(right_product(branch_grad, outer_full))[0].astype(jnp.bfloat16)
    grad_inner = left_product(second_low, inner_grad)
    grad_ibias = row_total(inner_grad)
    grad_second = grad_hidden3 + right_product(inner_grad, inner_full)
    feed_grads = (
        lax.psum_scatter(grad_inner, BOTH, scatter_dimension=0, tiled=True),
        lax.psum_scatter(grad_ibias, BOTH, scatter_dimension=0, tiled=True),
        lax.psum_scatter(grad_outer, BOTH, scatter_dimension=0, tiled=True),
        lax.psum_scatter(grad_obias_feed, BOTH, scatter_dimension=0, tiled=True),
        lax.psum_scatter(grad_fgain, BOTH, scatter_dimension=0, tiled=True),
        lax.psum_scatter(grad_fshift, BOTH, scatter_dimension=0, tiled=True),
    )
    grad_hidden2, grad_cgain, grad_cshift = norm_back(hidden_two, cgain, cshift, grad_second)
    cross_branch = grad_hidden2.astype(jnp.bfloat16)
    grad_cout = left_product(cross_low, cross_branch)
    grad_cobias = row_total(cross_branch)
    cross_up = right_product(cross_branch, cout_full).astype(jnp.bfloat16)
    cross_delta = head_delta(cross_up, attn_cross)
    cq_grad, ck_grad, cv_grad = attend_back(
        query_cross,
        key_cross,
        value_cross,
        cross_up,
        logsum_cross,
        cross_delta,
        target_ids,
        source_ids,
        False,
    )
    cq_low = cq_grad.astype(jnp.bfloat16)
    ck_low = ck_grad.astype(jnp.bfloat16)
    cv_low = cv_grad.astype(jnp.bfloat16)
    grad_cquery = left_product(first_low, cq_low)
    grad_cqbias = row_total(cq_low)
    grad_ckey = left_product(source, ck_low)
    grad_cvalue = left_product(source, cv_low)
    grad_cvbias = row_total(cv_low)
    memory_grad = right_product(ck_low, ckey_full) + right_product(cv_low, cvalue_full)
    grad_first = grad_hidden2 + right_product(cq_low, cquery_full)
    cross_grads = (
        lax.psum_scatter(grad_cquery, BOTH, scatter_dimension=0, tiled=True),
        lax.psum_scatter(grad_ckey, BOTH, scatter_dimension=0, tiled=True),
        lax.psum_scatter(grad_cvalue, BOTH, scatter_dimension=0, tiled=True),
        lax.psum_scatter(grad_cout, BOTH, scatter_dimension=0, tiled=True),
        lax.psum_scatter(grad_cqbias, BOTH, scatter_dimension=0, tiled=True),
        lax.psum_scatter(grad_cvbias, BOTH, scatter_dimension=0, tiled=True),
        lax.psum_scatter(grad_cobias, BOTH, scatter_dimension=0, tiled=True),
        lax.psum_scatter(grad_cgain, BOTH, scatter_dimension=0, tiled=True),
        lax.psum_scatter(grad_cshift, BOTH, scatter_dimension=0, tiled=True),
    )
    grad_hidden1, grad_sgain, grad_sshift = norm_back(hidden_one, sgain, sshift, grad_first)
    self_branch = grad_hidden1.astype(jnp.bfloat16)
    grad_out = left_product(self_low, self_branch)
    grad_obias = row_total(self_branch)
    self_up = right_product(self_branch, out_full).astype(jnp.bfloat16)
    self_delta = head_delta(self_up, attn_self)
    sq_grad, sk_grad, sv_grad = attend_back(
        query_self,
        key_self,
        value_self,
        self_up,
        logsum_self,
        self_delta,
        target_ids,
        target_ids,
        True,
    )
    sq_low = sq_grad.astype(jnp.bfloat16)
    sk_low = sk_grad.astype(jnp.bfloat16)
    sv_low = sv_grad.astype(jnp.bfloat16)
    grad_query = left_product(inputs, sq_low)
    grad_qbias = row_total(sq_low)
    grad_key = left_product(inputs, sk_low)
    grad_value = left_product(inputs, sv_low)
    grad_vbias = row_total(sv_low)
    tokens_grad = (
        grad_hidden1
        + right_product(sq_low, query_full)
        + right_product(sk_low, key_full)
        + right_product(sv_low, value_full)
    )
    self_grads = (
        lax.psum_scatter(grad_query, BOTH, scatter_dimension=0, tiled=True),
        lax.psum_scatter(grad_key, BOTH, scatter_dimension=0, tiled=True),
        lax.psum_scatter(grad_value, BOTH, scatter_dimension=0, tiled=True),
        lax.psum_scatter(grad_out, BOTH, scatter_dimension=0, tiled=True),
        lax.psum_scatter(grad_qbias, BOTH, scatter_dimension=0, tiled=True),
        lax.psum_scatter(grad_vbias, BOTH, scatter_dimension=0, tiled=True),
        lax.psum_scatter(grad_obias, BOTH, scatter_dimension=0, tiled=True),
        lax.psum_scatter(grad_sgain, BOTH, scatter_dimension=0, tiled=True),
        lax.psum_scatter(grad_sshift, BOTH, scatter_dimension=0, tiled=True),
    )
    return (
        (output[None], tokens_grad[None], memory_grad[None])
        + tuple(self_grads)
        + tuple(cross_grads)
        + tuple(feed_grads)
    )


LOW = jnp.bfloat16
WIDE = jnp.float32
MESH = pl.DeviceIdType.MESH
VMEM_BYTES = 64 << 20
ALL2 = pl.ds(0, 2)
ALL4 = pl.ds(0, 4)


def place():
    b, s = lax.axis_index(BATCH), lax.axis_index(SEQ)
    return (lax.div(b, 2), lax.rem(b, 2), lax.rem(s, 2), lax.div(s, 2))


def device(x, c, y, z):
    return (2 * x + c, 2 * z + y)


class Peers:
    def __init__(self):
        self.x, self.c, self.y, self.z = place()
        x, c, y, z = self.x, self.c, self.y, self.z
        b, s = lax.axis_index(BATCH), lax.axis_index(SEQ)
        self.across_x = device(1 - x, c, y, z)
        self.across_y = device(x, c, 1 - y, z)
        self.sibling = device(x, 1 - c, y, z)
        self.along_z = [device(x, c, y, lax.rem(z + k, 4)) for k in (1, 2, 3)]
        self.s = s
        self.after = (b, lax.rem(s + 1, 8))
        self.before = (b, lax.rem(s + 7, 8))
        self.mirror = (b, 7 - s)
        self.folds = [(b, lax.rem(14 - s, 8)), (b, lax.rem(16 - s, 8))]
        self.alone = [self.folds[k][1] == s for k in range(2)]

    def greet(self):
        barrier = pltpu.get_barrier_semaphore()
        always = [
            self.across_x, self.across_y, self.sibling, *self.along_z, self.after, self.before, self.mirror,
        ]
        for peer in always:
            pl.semaphore_signal(barrier, inc=1, device_id=peer, device_id_type=MESH)
        for peer, alone in zip(self.folds, self.alone):
            @pl.when(jnp.logical_not(alone))
            def _():
                pl.semaphore_signal(barrier, inc=1, device_id=peer, device_id_type=MESH)

    def meet(self):
        barrier = pltpu.get_barrier_semaphore()
        others = [jnp.where(alone, 0, 1) for alone in self.alone]
        pl.semaphore_wait(barrier, 9 + others[0] + others[1])


class Wires:
    def __init__(self, send, recv):
        self.send, self.recv, self.used = send, recv, 0

    def copies(self, pairs, target):
        made = []
        for source, landing in pairs:
            made.append(
                pltpu.make_async_remote_copy(
                    src_ref=source,
                    dst_ref=landing,
                    send_sem=self.send.at[self.used],
                    recv_sem=self.recv.at[self.used],
                    device_id=target,
                    device_id_type=MESH,
                )
            )
            self.used += 1
        return made


def start(copies):
    for copy in copies:
        copy.start()


def landed(copies):
    for copy in copies:
        copy.wait_recv()


def sent(copies):
    for copy in copies:
        copy.wait_send()


class Gather:
    def __init__(self, peers, wires, mats, pool, outer, vectors):
        self.peers, self.wires = peers, wires
        self.mats, self.pool, self.outer, self.vectors = mats, pool, outer, vectors
        self.steps = [{} for _ in range(8)]

    def parts(self, unit, x, c, z, y):
        both = y is None
        if unit >= 6:
            rows = pl.ds(48 * (unit - 6), 48)
            return [self.outer.at[x, c, z, ALL2 if both else y, rows]]
        mats = pl.ds(2 * unit, 2)
        if both:
            refs = [self.mats.at[mats, x, c, z, pl.ds(0, 16)], self.mats.at[mats, x, c, z, pl.ds(32, 16)]]
        else:
            refs = [self.mats.at[mats, x, c, z, pl.ds(pl.multiple_of(32 * y, 16), 16)]]
        depth = pl.ds(4 * c, 4) if z is ALL4 else 4 * c + z
        side = 2 * (unit % 2)
        refs.append(self.pool.at[depth, x, pl.ds(side, 2) if both else side + y, unit // 2])
        if unit == 0:
            refs.append(self.vectors.at[x, c, z, ALL2 if both else y])
        return refs

    def send(self, unit, name, spot, target):
        pairs = [(part, part) for part in self.parts(unit, *spot)]
        copies = self.wires.copies(pairs, target)
        start(copies)
        self.steps[unit][name] = copies

    def z_start(self, unit):
        p = self.peers
        for k, peer in enumerate(p.along_z):
            self.send(unit, ("z", k), (p.x, p.c, p.z, p.y), peer)

    def first(self, unit):
        p = self.peers
        for k in range(3):
            landed(self.steps[unit]["z", k])
        self.send(unit, "first", (p.x, p.c, ALL4, p.y), p.across_y if unit % 2 else p.across_x)

    def second(self, unit):
        p = self.peers
        landed(self.steps[unit]["first"])
        if unit % 2:
            self.send(unit, "second", (p.x, p.c, ALL4, None), p.across_x)
            self.send(unit, "near", (p.x, p.c, ALL4, None), p.sibling)
        else:
            self.send(unit, "second", (ALL2, p.c, ALL4, p.y), p.across_y)
            self.send(unit, "near", (ALL2, p.c, ALL4, p.y), p.sibling)

    def third(self, unit):
        p = self.peers
        landed(self.steps[unit]["second"])
        if unit % 2:
            self.send(unit, "far", (1 - p.x, p.c, ALL4, None), p.sibling)
        else:
            self.send(unit, "far", (ALL2, p.c, ALL4, 1 - p.y), p.sibling)

    def last(self, unit):
        landed(self.steps[unit]["near"])
        landed(self.steps[unit]["far"])

    def close(self, units):
        for unit in units:
            for copies in self.steps[unit].values():
                sent(copies)


def gather_pack(unit, peers, squares, inner, outer, mats, pool, whole_outer):
    x, c, y, z = peers.x, peers.c, peers.y, peers.z
    if unit >= 6:
        half = slice(48 * (unit - 6), 48 * (unit - 6) + 48)
        whole_outer[x, c, z, y, half] = outer[half]
        return
    rests = []
    for k in range(2):
        m = 2 * unit + k
        values = squares[m][...] if m < 8 else inner[:, 768 * (m - 8) : 768 * (m - 7)]
        values = values.astype(WIDE)
        body = jnp.where(y == 0, values[0:16], values[8:24])
        rests.append(jnp.where(y == 0, values[16:24], values[0:8]))
        mats[m, x, c, z, pl.ds(pl.multiple_of(32 * y, 16), 16), :] = body.astype(LOW)
    pool[4 * c + z, x, 2 * (unit % 2) + y, unit // 2] = jnp.concatenate(rests, axis=0).astype(LOW)


def gather_vectors(peers, smalls, board, vectors):
    board[...] = jnp.zeros((16, 128), WIDE)
    for j, small in enumerate(smalls):
        board[j : j + 1, 0 : small.shape[1]] = small[...].astype(WIDE)
    index = (2 * peers.x + peers.c) * 8 + peers.s
    wide = board[...]
    row = lax.broadcasted_iota(jnp.int32, (16, 128), 0)
    by24 = pltpu.roll(wide, lax.rem(24 * index, 128), 1)
    by96 = pltpu.roll(wide, lax.rem(96 * index, 128), 1)
    rolled = jnp.where(row == 13, by96, by24).astype(LOW)
    vectors[peers.x, peers.c, peers.z, peers.y] = rolled


def merge_rests(unit, mats, pool):
    def one(step, carry):
        x, c, z = lax.div(step, 8), lax.rem(lax.div(step, 4), 2), lax.rem(step, 4)
        side = 2 * (unit % 2)
        low_half = pool[4 * c + z, x, side, unit // 2].astype(WIDE)
        high_half = pool[4 * c + z, x, side + 1, unit // 2].astype(WIDE)
        mats[2 * unit, x, c, z, 16:32, :] = jnp.concatenate(
            [low_half[0:8], high_half[0:8]], axis=0
        ).astype(LOW)
        mats[2 * unit + 1, x, c, z, 16:32, :] = jnp.concatenate(
            [low_half[8:16], high_half[8:16]], axis=0
        ).astype(LOW)
        return carry

    lax.fori_loop(0, 16, one, 0)


def vmem():
    return pl.BlockSpec(memory_space=pltpu.VMEM)


def dot(left, right):
    return jnp.dot(left, right, preferred_element_type=WIDE)


def dot_nt(left, right):
    return lax.dot_general(left, right, (((1,), (1,)), ((), ())), preferred_element_type=WIDE)


def dot_tn(left, right):
    return lax.dot_general(left, right, (((0,), (0,)), ((), ())), preferred_element_type=WIDE)


def strip(n):
    return slice(256 * n, 256 * n + 256)


def columns(mats, m, n):
    return mats[m, :, :, :, :, strip(n)].reshape(768, 256)


def rows(mats, m, x):
    return mats[m, x].reshape(384, 768)


def outer_columns(outer, j, n):
    return outer[j // 2, j % 2, :, :, :, strip(n)].reshape(768, 256)


def outer_rows(outer, j, half):
    return outer[j // 2, j % 2, 2 * half : 2 * half + 2].reshape(384, 768)


def unpack_vectors(vectors, vec, inner_bias):
    lane = lax.broadcasted_iota(jnp.int32, (16, 128), 1)

    def shard(d):
        b, s = d // 8, d % 8
        return vectors[b // 2, b % 2, s // 2, s % 2].astype(WIDE)

    for width, tiles, ref in ((24, 6, vec), (96, 24, inner_bias)):
        for t in range(tiles):
            first = (128 * t) // width
            final = (128 * t + 127) // width
            total = shard(first)
            for d in range(first + 1, final + 1):
                total = jnp.where(lane >= width * d - 128 * t, shard(d), total)
            if width == 24:
                ref[:, 128 * t : 128 * t + 128] = total
            else:
                ref[0:1, 128 * t : 128 * t + 128] = total[13:14]


def pack_vectors(vec, inner_bias, c, place_at):
    lane = lax.broadcasted_iota(jnp.int32, (16, 128), 1)
    row = lax.broadcasted_iota(jnp.int32, (16, 128), 0)

    def shard(ref, width, d):
        t, offset = width * d // 128, width * d % 128
        block = ref[:, 128 * t : 128 * t + 128]
        if offset + width > 128:
            block = jnp.where(lane >= offset, block, ref[:, 128 * t + 128 : 128 * t + 256])
        return block

    for d in range(32):
        b, s = d // 8, d % 8
        block = shard(vec, 24, d)
        t, offset = 96 * d // 128, 96 * d % 128
        bias = inner_bias[0:1, 128 * t : 128 * t + 128]
        if offset + 96 > 128:
            bias = jnp.where(lane[0:1] >= offset, bias, inner_bias[0:1, 128 * t + 128 : 128 * t + 256])
        place_at(b % 2, b // 2, s // 2, s % 2, jnp.where(row == 13, jnp.broadcast_to(bias, (16, 128)), block))


def centered(values):
    center = values - jnp.mean(values, axis=-1, keepdims=True)
    scale = lax.rsqrt(jnp.mean(center * center, axis=-1, keepdims=True) + EPSILON)
    return (center * scale, scale)


def norm_grad(unit_values, scale, gain, grad):
    scaled = grad * gain
    mean = jnp.mean(scaled, axis=-1, keepdims=True)
    along = jnp.mean(scaled * unit_values, axis=-1, keepdims=True)
    return (scaled - mean - unit_values * along) * scale


def total_rows(values):
    return jnp.sum(values.astype(WIDE), axis=0, keepdims=True)


def lane_halves():
    lane = lax.broadcasted_iota(jnp.int32, (128, 128), 1)
    low_half = jnp.where(lane < 64, 1.0, 0.0).astype(LOW)
    high_half = jnp.where(lane < 64, 0.0, 1.0).astype(LOW)
    return (lane < 64, low_half, high_half)


def pair_rows(block, low_half, high_half):
    return jnp.concatenate([block * low_half, block * high_half], axis=0)


def attention(queries, keys, values, mask, probs, context):
    pick, low_half, high_half = lane_halves()

    def heads(h, carry):
        here = pl.ds(pl.multiple_of(128 * h, 128), 128)
        both = pair_rows(queries[:, here], low_half, high_half)
        bias = mask[...]
        scores = dot_nt(both, keys[:, here]) * SCALE + jnp.concatenate([bias, bias], axis=0)
        weights = jnp.exp(scores - jnp.max(scores, axis=1, keepdims=True))
        weights = weights * (1.0 / jnp.sum(weights, axis=1, keepdims=True))
        rounded = weights.astype(LOW)
        probs[h] = rounded
        mixed = dot(rounded, values[:, here])
        context[:, here] = jnp.where(pick, mixed[:128], mixed[128:]).astype(LOW)
        return carry

    lax.fori_loop(0, 6, heads, 0)


def attention_back(queries, keys, values, upstream, probs, dqueries, dkeys, dvalues, count):
    pick, low_half, high_half = lane_halves()

    def heads(h, carry):
        here = pl.ds(pl.multiple_of(128 * h, 128), 128)
        both = pair_rows(queries[:, here], low_half, high_half)
        both_up = pair_rows(upstream[:, here], low_half, high_half)
        dprobs = dot_nt(both_up, values[:, here])
        weights = probs[h].astype(WIDE)
        delta = jnp.sum(weights * dprobs, axis=1, keepdims=True)
        dscores = (weights * (dprobs - delta) * SCALE).astype(LOW)
        mixed = dot(dscores, keys[:, here])
        dqueries[:, here] = jnp.where(pick, mixed[:128], mixed[128:]).astype(LOW)
        dkeys[0:count, here] = dot_tn(dscores, both).astype(LOW)
        dvalues[0:count, here] = dot_tn(probs[h], both_up).astype(LOW)
        return carry

    lax.fori_loop(0, 6, heads, 0)


class Grads:
    ORDER = (6, 7, 4, 5, 2, 3, 0, 1)

    def __init__(self, peers, wires, held, r0, pool, r2, out, mine, credit):
        self.peers, self.wires, self.held = peers, wires, held
        self.r0, self.pool, self.r2, self.out = r0, pool, r2, out
        self.mine, self.credit = mine, credit
        self.stage = {}
        self.open = []
        self.first_sends = {}

    def at(self, unit):
        return self.ORDER.index(unit)

    def slot(self, unit, c):
        return jnp.where(c == self.peers.c, unit, 8 + self.at(unit) % 4)

    def ready(self, unit):
        turn = self.at(unit)
        if turn >= 4:
            sent(self.first_sends.pop(self.ORDER[turn - 4]))

    def ship(self, pairs, target):
        copies = self.wires.copies(pairs, target)
        start(copies)
        self.open += copies
        return copies

    def step0(self, unit):
        turn = self.at(unit)
        if turn >= 4:
            pl.semaphore_wait(self.credit, 1)
        ring = turn % 4
        copies = self.wires.copies([(self.held.at[8 + ring], self.r0.at[ring])], self.peers.sibling)
        start(copies)
        self.first_sends[unit] = copies
        self.stage[unit] = copies

    def step1(self, unit):
        p, held = self.peers, self.held
        landed(self.stage[unit])
        turn = self.at(unit)
        ring = turn % 4

        def add(i, carry):
            j, k = lax.div(i, 4), lax.rem(i, 4)
            held[unit, j, k] = held[unit, j, k] + self.r0[ring, j, k]
            return carry

        lax.fori_loop(0, 8, add, 0)
        if turn < 4:
            pl.semaphore_signal(self.credit, inc=1, device_id=p.sibling, device_id_type=MESH)
        if unit % 2:
            pairs = [(held.at[unit, 1 - p.x, ALL4, k], self.pool.at[unit, k]) for k in range(2)]
            self.stage[unit] = self.ship(pairs, p.across_x)
        else:
            pairs = [(held.at[unit, ALL2, ALL4, 1 - p.y], self.pool.at[unit])]
            self.stage[unit] = self.ship(pairs, p.across_y)

    def step2(self, unit):
        p, held = self.peers, self.held
        landed(self.stage[unit])

        def add(i, carry):
            if unit % 2:
                for k in range(2):
                    held[unit, p.x, i, k] = held[unit, p.x, i, k] + self.pool[unit, k, i]
            else:
                for j in range(2):
                    held[unit, j, i, p.y] = held[unit, j, i, p.y] + self.pool[unit, j, i]
            return carry

        lax.fori_loop(0, 4, add, 0)
        if unit % 2:
            pairs = [(held.at[unit, p.x, ALL4, 1 - p.y], self.r2.at[unit])]
            self.stage[unit] = self.ship(pairs, p.across_y)
        else:
            pairs = [(held.at[unit, 1 - p.x, ALL4, p.y], self.r2.at[unit])]
            self.stage[unit] = self.ship(pairs, p.across_x)

    def step3(self, unit):
        p, held = self.peers, self.held
        landed(self.stage[unit])

        def add(i, carry):
            held[unit, p.x, i, p.y] = held[unit, p.x, i, p.y] + self.r2[unit, i]
            return carry

        lax.fori_loop(0, 4, add, 0)
        copies = []
        for k in (1, 2, 3):
            source = held.at[unit, p.x, lax.rem(p.z + k, 4), p.y]
            copies += self.ship([(source, self.out.at[unit, k - 1])], p.along_z[k - 1])
        self.stage[unit] = copies
        self.mine[unit] = held[unit, p.x, p.z, p.y]

    def finish(self):
        for unit in self.ORDER:
            landed(self.stage[unit])
        for copies in self.first_sends.values():
            sent(copies)
        sent(self.open)

    def pair_grad(self, unit, first_left, first_right, second_left, second_right):
        self.ready(unit)
        for x in range(2):
            here = slice(384 * x, 384 * x + 384)
            one_left = jnp.transpose(first_left[:, here])
            two_left = jnp.transpose(second_left[:, here])
            for n in range(3):
                s = strip(n)
                one = dot(one_left, first_right[:, s])
                two = dot(two_left, second_right[:, s])
                for c in range(2):
                    slot = self.slot(unit, c)
                    for z in range(4):
                        for y in range(2):
                            base = 24 * (8 * c + 2 * z + y)
                            body = base + 8 * y
                            rest = base + 16 * (1 - y)
                            self.held[slot, x, z, y, 0, :, s] = one[body : body + 16].astype(LOW)
                            self.held[slot, x, z, y, 1, :, s] = two[body : body + 16].astype(LOW)
                            self.held[slot, x, z, y, 2, :, s] = jnp.concatenate(
                                [one[rest : rest + 8], two[rest : rest + 8]], axis=0
                            ).astype(LOW)

    def outer_grad(self, hidden, upstream):
        for j in range(4):
            x, c = j // 2, j % 2
            for half in range(2):
                here = slice(768 * j + 384 * half, 768 * j + 384 * half + 384)
                left = jnp.transpose(hidden[:, here])
                for n in range(3):
                    s = strip(n)
                    one = dot(left, upstream[:, s])
                    for unit in (6, 7):
                        slot = self.slot(unit, c)
                        for k in range(4):
                            base = 96 * k + 48 * (unit - 6)
                            z, y = 2 * half + k // 2, k % 2
                            block = one[base : base + 48].reshape(3, 16, 256)
                            self.held[slot, x, z, y, :, :, s] = block.astype(LOW)


def layer_kernel(*refs):
    squares, inner_own, outer_own, smalls = refs[0:8], refs[8], refs[9], refs[10:24]
    tokens_own, memory_own, cotangent, target_ids, source_ids = refs[24:29]
    output, out, mine, vout, left_out, memory_out, tokens_part = refs[29:36]
    (
        mats, outer, vectors, tokens, memory, board, mask_self, mask_cross,
        vec, inner_bias, query, key, value, probs, context, unit1, first_low,
        query2, key2, value2, probs2, context2, unit2, second_low,
        hidden, slope, total, grad, branch, upstream, dquery, dkey, dvalue,
        gvec, ginner,
        held, r0, pool, r2, vheld, v0, v1, v2, left_part, memory_parts,
        credit, free, send, recv, local,
    ) = refs[36:]
    peers = Peers()
    peers.greet()
    wires = Wires(send, recv)
    weights = Gather(peers, wires, mats, pool, outer, vectors)
    grads = Grads(peers, wires, held, r0, pool, r2, out, mine, credit)
    own = slice(128, 256)

    def pack(unit):
        gather_pack(unit, peers, squares, inner_own, outer_own, mats, pool, outer)

    pack(0)
    gather_vectors(peers, smalls, board, vectors)
    peers.meet()
    weights.z_start(0)
    pack(1)
    weights.z_start(1)
    tokens[own, :] = tokens_own[...]
    left = wires.copies([(tokens_own, tokens.at[pl.ds(0, 128)])], peers.after)
    mirrored = wires.copies([(memory_own, memory.at[pl.ds(128, 128)])], peers.mirror)
    start(left + mirrored)
    folds = [
        wires.copies([(memory_own, memory.at[pl.ds(256 * k, 128)])], peers.folds[k]) for k in range(2)
    ]
    for k in range(2):
        @pl.when(jnp.logical_not(peers.alone[k]))
        def _():
            start(folds[k])

        @pl.when(peers.alone[k])
        def _():
            memory[pl.ds(256 * k, 128), :] = memory_own[...]

    for unit in range(2, 8):
        pack(unit)
    fill_masks(peers, target_ids, source_ids, mask_self, mask_cross)

    def turn(t):
        if t < 4:
            weights.first(2 * t)
            weights.first(2 * t + 1)
            if t < 3:
                weights.z_start(2 * t + 2)
                weights.z_start(2 * t + 3)
        if 1 <= t < 5:
            weights.second(2 * t - 2)
            weights.second(2 * t - 1)
        if t >= 2:
            weights.third(2 * t - 4)
            weights.third(2 * t - 3)

    def arrive(pair):
        for unit in (2 * pair, 2 * pair + 1):
            weights.last(unit)
            if unit < 6:
                merge_rests(unit, mats, pool)

    def vector(j):
        return vec[j : j + 1, :]

    turn(0)
    turn(1)
    turn(2)
    arrive(0)
    unpack_vectors(vectors, vec, inner_bias)
    landed(left)
    for n in range(3):
        s = strip(n)
        query[:, s] = (dot(tokens[own, :], columns(mats, 0, n)) + vec[0:1, s]).astype(LOW)
        key[:, s] = dot(tokens[...], columns(mats, 1, n)).astype(LOW)
        value[:, s] = (dot(tokens[...], columns(mats, 2, n)) + vec[1:2, s]).astype(LOW)
    attention(query, key, value, mask_self, probs, context)
    for n in range(3):
        s = strip(n)
        total[:, s] = (
            tokens[own, s].astype(WIDE) + dot(context[...], columns(mats, 3, n)) + vec[2:3, s]
        )
    unit, scale1 = centered(total[...])
    unit1[...] = unit
    first = unit * vector(3) + vector(4)
    total[...] = first
    first_low[...] = first.astype(LOW)
    turn(3)
    arrive(1)
    landed(mirrored)
    for k in range(2):
        @pl.when(jnp.logical_not(peers.alone[k]))
        def _():
            landed(folds[k])
            sent(folds[k])

    for n in range(3):
        s = strip(n)
        query2[:, s] = (dot(first_low[...], columns(mats, 4, n)) + vec[5:6, s]).astype(LOW)
        key2[:, s] = dot(memory[...], columns(mats, 5, n)).astype(LOW)
        value2[:, s] = (dot(memory[...], columns(mats, 6, n)) + vec[6:7, s]).astype(LOW)
    attention(query2, key2, value2, mask_cross, probs2, context2)
    for n in range(3):
        s = strip(n)
        total[:, s] = total[:, s] + dot(context2[...], columns(mats, 7, n)) + vec[7:8, s]
    unit, scale2 = centered(total[...])
    unit2[...] = unit
    second = unit * vector(8) + vector(9)
    total[...] = second + vector(10)
    second_low[...] = second.astype(LOW)
    turn(4)
    arrive(2)
    weights.close(range(6))
    for peer in (peers.across_x, peers.across_y):
        pl.semaphore_signal(free, inc=1, device_id=peer, device_id_type=MESH)
    for j in range(4):
        for n in range(3):
            s = slice(768 * j + 256 * n, 768 * j + 256 * n + 256)
            pre = dot(second_low[...], columns(mats, 8 + j, n)) + inner_bias[0:1, s]
            normal = 0.5 + 0.5 * lax.erf(pre * 0.7071067811865476)
            hidden[:, s] = (pre * normal).astype(LOW)
            slope[:, s] = (
                normal + pre * (0.3989422804014327 * jnp.exp(-0.5 * pre * pre))
            ).astype(LOW)
    turn(5)
    arrive(3)
    weights.close(range(6, 8))
    sent(left + mirrored)
    for n in range(3):
        s = strip(n)
        summed = total[:, s]
        for j in range(4):
            here = slice(768 * j, 768 * j + 768)
            summed = summed + dot(hidden[:, here], outer_columns(outer, j, n))
        total[:, s] = summed
    unit, scale3 = centered(total[...])
    output[...] = (unit * vector(11) + vector(12)).astype(LOW)
    arrived = cotangent[...].astype(WIDE)
    gvec[11:12, :] = total_rows(arrived * unit)
    gvec[12:13, :] = total_rows(arrived)
    dhidden = norm_grad(unit, scale3, vector(11), arrived)
    grad[...] = dhidden
    branch[...] = dhidden.astype(LOW)
    gvec[10:11, :] = total_rows(branch[...])
    grads.outer_grad(hidden, branch)
    grads.step0(6)
    grads.step0(7)
    for j in range(4):
        for half in range(2):
            s = slice(768 * j + 384 * half, 768 * j + 384 * half + 384)
            raised = dot_nt(branch[...], outer_rows(outer, j, half)) * slope[:, s].astype(WIDE)
            raised = raised.astype(LOW)
            slope[:, s] = raised
            ginner[0:1, s] = total_rows(raised)
    for unit in (4, 5):
        spans_of = [slope.at[:, pl.ds(768 * j, 768)] for j in (2 * unit - 8, 2 * unit - 7)]
        grads.pair_grad(unit, second_low, spans_of[0], second_low, spans_of[1])
        grads.step0(unit)
    for x in range(2):
        s = slice(384 * x, 384 * x + 384)
        summed = grad[:, s]
        for j in range(4):
            summed = summed + dot_nt(slope[:, 768 * j : 768 * j + 768], rows(mats, 8 + j, x))
        grad[:, s] = summed
    pl.semaphore_wait(free, 2)
    grads.step1(6)
    grads.step1(7)
    arrived = grad[...]
    unit = unit2[...]
    gvec[8:9, :] = total_rows(arrived * unit)
    gvec[9:10, :] = total_rows(arrived)
    dhidden = norm_grad(unit, scale2, vector(8), arrived)
    grad[...] = dhidden
    branch[...] = dhidden.astype(LOW)
    gvec[7:8, :] = total_rows(branch[...])
    for x in range(2):
        upstream[:, 384 * x : 384 * x + 384] = dot_nt(branch[...], rows(mats, 7, x)).astype(LOW)
    grads.step1(4)
    grads.step1(5)
    attention_back(query2, key2, value2, upstream, probs2, dquery, dkey, dvalue, 384)
    grads.step2(6)
    grads.step2(7)
    gvec[5:6, :] = total_rows(dquery[...])
    gvec[6:7, :] = total_rows(dvalue[...])
    for x in range(2):
        s = slice(384 * x, 384 * x + 384)
        grad[:, s] = grad[:, s] + dot_nt(dquery[...], rows(mats, 4, x))
        backed = dot_nt(dkey[...], rows(mats, 5, x)) + dot_nt(dvalue[...], rows(mats, 6, x))
        for block in range(3):
            memory_parts[block, :, s] = backed[128 * block : 128 * block + 128].astype(LOW)
    home = grads.ship([(memory_parts.at[1], memory_out.at[1])], peers.mirror)
    back = [
        wires.copies([(memory_parts.at[2 * k], memory_out.at[2 * k])], peers.folds[k]) for k in range(2)
    ]
    stay = [
        pltpu.make_async_copy(memory_parts.at[2 * k], memory_out.at[2 * k], local.at[k]) for k in range(2)
    ]
    for k in range(2):
        @pl.when(jnp.logical_not(peers.alone[k]))
        def _():
            start(back[k])

        @pl.when(peers.alone[k])
        def _():
            stay[k].start()

    grads.pair_grad(2, first_low, dquery, memory, dkey)
    grads.step0(2)
    grads.pair_grad(3, memory, dvalue, context2, branch)
    grads.step0(3)
    grads.step2(4)
    grads.step2(5)
    grads.step3(6)
    grads.step3(7)
    arrived = grad[...]
    unit = unit1[...]
    gvec[3:4, :] = total_rows(arrived * unit)
    gvec[4:5, :] = total_rows(arrived)
    dhidden = norm_grad(unit, scale1, vector(3), arrived)
    grad[...] = dhidden
    branch[...] = dhidden.astype(LOW)
    gvec[2:3, :] = total_rows(branch[...])
    for x in range(2):
        upstream[:, 384 * x : 384 * x + 384] = dot_nt(branch[...], rows(mats, 3, x)).astype(LOW)
    grads.step1(2)
    grads.step1(3)
    attention_back(query, key, value, upstream, probs, dquery, dkey, dvalue, 256)
    dkey_two, dvalue_two = dkey.at[pl.ds(0, 256)], dvalue.at[pl.ds(0, 256)]
    grads.pair_grad(0, tokens.at[pl.ds(128, 128)], dquery, tokens, dkey_two)
    grads.step0(0)
    grads.pair_grad(1, tokens, dvalue_two, context, branch)
    grads.step0(1)
    gvec[0:1, :] = total_rows(dquery[...])
    gvec[1:2, :] = total_rows(dvalue_two[...])
    gvec[13:16, :] = jnp.zeros((3, 768), WIDE)

    def put(c, x, z, y, block):
        vheld[c, x, z, y] = block

    pack_vectors(gvec, ginner, peers.c, put)
    c, x, y, z = peers.c, peers.x, peers.y, peers.z
    vstage = grads.ship([(vheld.at[1 - c], v0)], peers.sibling)
    grads.step3(4)
    grads.step3(5)
    grads.step2(2)
    grads.step2(3)
    for x_ in range(2):
        s = slice(384 * x_, 384 * x_ + 384)
        backed = dot_nt(dkey_two[...], rows(mats, 1, x_)) + dot_nt(dvalue_two[...], rows(mats, 2, x_))
        left_part[:, s] = backed[0:128].astype(LOW)
        tokens_part[:, s] = grad[:, s] + dot_nt(dquery[...], rows(mats, 0, x_)) + backed[128:256]
    left = grads.ship([(left_part, left_out)], peers.before)
    grads.step1(0)
    grads.step1(1)
    landed(vstage)
    vheld[c] = vheld[c] + v0[...]
    vstage = grads.ship([(vheld.at[c, ALL2, ALL4, 1 - y], v1)], peers.across_y)
    grads.step3(2)
    grads.step3(3)
    grads.step2(0)
    grads.step2(1)
    landed(vstage)
    for j in range(2):
        for k in range(4):
            vheld[c, j, k, y] = vheld[c, j, k, y] + v1[j, k]
    vstage = grads.ship([(vheld.at[c, 1 - x, ALL4, y], v2)], peers.across_x)
    grads.step3(0)
    grads.step3(1)
    landed(vstage)
    for k in range(4):
        vheld[c, x, k, y] = vheld[c, x, k, y] + v2[k]
    vstage = []
    for k in (1, 2, 3):
        source = vheld.at[c, x, lax.rem(z + k, 4), y]
        vstage += grads.ship([(source, vout.at[k])], peers.along_z[k - 1])
    vout[0] = vheld[c, x, z, y]
    landed(vstage + left + home)
    for k in range(2):
        @pl.when(jnp.logical_not(peers.alone[k]))
        def _():
            landed(back[k])
            sent(back[k])

        @pl.when(peers.alone[k])
        def _():
            stay[k].wait()

    grads.finish()


def fill_masks(peers, target_ids, source_ids, mask_self, mask_cross):
    def ids(ref, block):
        here = pl.ds(pl.multiple_of(128 * block, 128), 128)
        return jnp.broadcast_to(ref[:, here].astype(WIDE), (128, 128))

    s = peers.s
    here = ids(target_ids, s)
    queries = jnp.transpose(here)
    row = lax.broadcasted_iota(jnp.int32, (128, 128), 0)
    column = lax.broadcasted_iota(jnp.int32, (128, 128), 1)
    before = jnp.where(s > 0, ids(target_ids, lax.rem(s + 7, 8)), -1.0)
    mask_self[:, 0:128] = jnp.where(queries == before, 0.0, NEGATIVE)
    seen = jnp.where(queries == here, 0.0, NEGATIVE)
    mask_self[:, 128:256] = jnp.where(column <= row, seen, NEGATIVE)
    for k in range(3):
        block = ids(source_ids, lax.rem(14 + k - s, 8))
        mask_cross[:, 128 * k : 128 * k + 128] = jnp.where(queries == block, 0.0, NEGATIVE)


def layer_call(*inputs):
    shapes = [
        jax.ShapeDtypeStruct((128, 768), LOW),
        jax.ShapeDtypeStruct((8, 3, 3, 16, 768), LOW),
        jax.ShapeDtypeStruct((8, 3, 16, 768), LOW),
        jax.ShapeDtypeStruct((4, 16, 128), WIDE),
        jax.ShapeDtypeStruct((128, 768), LOW),
        jax.ShapeDtypeStruct((3, 128, 768), LOW),
        jax.ShapeDtypeStruct((128, 768), WIDE),
    ]

    def low(*shape):
        return pltpu.VMEM(shape, LOW)

    def wide(*shape):
        return pltpu.VMEM(shape, WIDE)

    scratch = [
        low(12, 2, 2, 4, 48, 768),
        low(2, 2, 4, 2, 96, 768),
        low(2, 2, 4, 2, 16, 128),
        low(256, 768),
        low(384, 768),
        wide(16, 128),
        wide(128, 256),
        wide(128, 384),
        wide(16, 768),
        wide(8, 3072),
        low(128, 768),
        low(256, 768),
        low(256, 768),
        low(6, 256, 256),
        low(128, 768),
        wide(128, 768),
        low(128, 768),
        low(128, 768),
        low(384, 768),
        low(384, 768),
        low(6, 256, 384),
        low(128, 768),
        wide(128, 768),
        low(128, 768),
        low(128, 3072),
        low(128, 3072),
        wide(128, 768),
        wide(128, 768),
        low(128, 768),
        low(128, 768),
        low(128, 768),
        low(384, 768),
        low(384, 768),
        wide(16, 768),
        wide(8, 3072),
        low(12, 2, 4, 2, 3, 16, 768),
        low(4, 2, 4, 2, 3, 16, 768),
        low(8, 2, 4, 3, 16, 768),
        low(8, 4, 3, 16, 768),
        wide(2, 2, 4, 2, 16, 128),
        wide(2, 4, 2, 16, 128),
        wide(2, 4, 16, 128),
        wide(4, 16, 128),
        low(128, 768),
        low(3, 128, 768),
        pltpu.SemaphoreType.REGULAR,
        pltpu.SemaphoreType.REGULAR,
        pltpu.SemaphoreType.DMA((240,)),
        pltpu.SemaphoreType.DMA((240,)),
        pltpu.SemaphoreType.DMA((2,)),
    ]
    anywhere = pl.BlockSpec(memory_space=pl.ANY)
    return pl.pallas_call(
        layer_kernel,
        out_shape=shapes,
        in_specs=[vmem()] * 29,
        out_specs=[vmem(), anywhere, vmem(), vmem(), anywhere, anywhere, vmem()],
        scratch_shapes=scratch,
        compiler_params=pltpu.CompilerParams(
            collective_id=0, has_side_effects=True, vmem_limit_bytes=VMEM_BYTES
        ),
    )(*inputs)


def final_kernel(output_low, parts, mine, vparts, left, memory_low, tokens_part, *outs):
    output, tokens_grad, memory_grad, small = outs[:4]
    squares, inner, outer = outs[4:12], outs[12], outs[13]
    output[...] = output_low[...]
    b, s = lax.axis_index(BATCH), lax.axis_index(SEQ)
    even = lax.rem(s, 2) == 0
    tokens_grad[...] = tokens_part[...] + left[...].astype(WIDE)
    memory_grad[...] = (
        memory_low[0].astype(WIDE) + memory_low[1].astype(WIDE) + memory_low[2].astype(WIDE)
    )

    def summed(unit):
        total = (
            mine[unit].astype(WIDE) + parts[unit, 0].astype(WIDE)
            + parts[unit, 1].astype(WIDE) + parts[unit, 2].astype(WIDE)
        )
        return total.reshape(48, 768)

    for unit in range(6):
        total = summed(unit)
        for k in range(2):
            body, rest = total[16 * k : 16 * k + 16], total[32 + 8 * k : 40 + 8 * k]
            matrix = jnp.where(
                even, jnp.concatenate([body, rest], axis=0), jnp.concatenate([rest, body], axis=0)
            )
            m = 2 * unit + k
            if m < 8:
                squares[m][...] = matrix
            else:
                inner[:, 768 * (m - 8) : 768 * (m - 7)] = matrix
    outer[0:48, :] = summed(6)
    outer[48:96, :] = summed(7)
    index = 8 * b + s
    vectors = vparts[0] + vparts[1] + vparts[2] + vparts[3]
    row = lax.broadcasted_iota(jnp.int32, (16, 128), 0)
    by24 = pltpu.roll(vectors, lax.rem(128 * 24 - 24 * index, 128), 1)
    by96 = pltpu.roll(vectors, lax.rem(128 * 96 - 96 * index, 128), 1)
    small[...] = jnp.where(row == 13, by96, by24)


def final_call(*inputs):
    shapes = [
        jax.ShapeDtypeStruct((128, 768), LOW),
        jax.ShapeDtypeStruct((128, 768), WIDE),
        jax.ShapeDtypeStruct((128, 768), WIDE),
        jax.ShapeDtypeStruct((16, 128), WIDE),
    ]
    shapes += [jax.ShapeDtypeStruct((24, 768), WIDE)] * 8
    shapes += [jax.ShapeDtypeStruct((24, 3072), WIDE), jax.ShapeDtypeStruct((96, 768), WIDE)]
    return pl.pallas_call(
        final_kernel,
        out_shape=shapes,
        in_specs=[vmem()] * 7,
        out_specs=[vmem()] * 14,
        compiler_params=pltpu.CompilerParams(vmem_limit_bytes=VMEM_BYTES),
    )(*inputs)


def fast_shards(tokens, memory, target_segments, memory_segments, cotangent, *weights):
    squares = weights[0:4] + weights[9:13]
    inner, inner_bias, outer = weights[18:21]
    smalls = list(weights[4:9]) + list(weights[13:18]) + list(weights[21:24]) + [inner_bias]
    results = layer_call(
        *squares,
        inner,
        outer,
        *[small[None] for small in smalls],
        tokens[0],
        memory[0],
        cotangent[0],
        target_segments,
        memory_segments,
    )
    results = final_call(*results)
    output, tokens_grad, memory_grad, small = results[:4]
    matrices, inner_grad, outer_grad = results[4:12], results[12], results[13]
    vector = [small[j, 0:24] for j in range(13)]
    return (
        (output[None], tokens_grad[None], memory_grad[None])
        + tuple(matrices[0:4])
        + tuple(vector[0:5])
        + tuple(matrices[4:8])
        + tuple(vector[5:10])
        + (inner_grad, small[13, 0:96], outer_grad)
        + tuple(vector[10:13])
    )


def fits(mesh):
    return mesh.shape[BATCH] == 4 and mesh.shape[SEQ] == 8


def solution(mesh):
    in_specs = (
        P(BATCH, SEQ, None),
        P(BATCH, SEQ, None),
        P(BATCH, None),
        P(BATCH, None),
        P(BATCH, SEQ, None),
        P(BOTH, None),
        P(BOTH, None),
        P(BOTH, None),
        P(BOTH, None),
        P(BOTH),
        P(BOTH),
        P(BOTH),
        P(BOTH),
        P(BOTH),
        P(BOTH, None),
        P(BOTH, None),
        P(BOTH, None),
        P(BOTH, None),
        P(BOTH),
        P(BOTH),
        P(BOTH),
        P(BOTH),
        P(BOTH),
        P(BOTH, None),
        P(BOTH),
        P(BOTH, None),
        P(BOTH),
        P(BOTH),
        P(BOTH),
    )
    out_specs = (
        P(BATCH, SEQ, None),
        P(BATCH, SEQ, None),
        P(BATCH, SEQ, None),
        P(BOTH, None),
        P(BOTH, None),
        P(BOTH, None),
        P(BOTH, None),
        P(BOTH),
        P(BOTH),
        P(BOTH),
        P(BOTH),
        P(BOTH),
        P(BOTH, None),
        P(BOTH, None),
        P(BOTH, None),
        P(BOTH, None),
        P(BOTH),
        P(BOTH),
        P(BOTH),
        P(BOTH),
        P(BOTH),
        P(BOTH, None),
        P(BOTH),
        P(BOTH, None),
        P(BOTH),
        P(BOTH),
        P(BOTH),
    )
    quick = fits(mesh)
    return jax.shard_map(fast_shards if quick else shards, mesh=mesh, in_specs=in_specs, out_specs=out_specs, check_vma=False)
```

```python
from functools import partial

import jax
import jax.numpy as jnp
from jax import lax
from jax.experimental import pallas as pl
from jax.experimental.pallas import tpu as pltpu
from jax.sharding import PartitionSpec as P

BATCH, SEQ = ("batch", "seq")
BOTH = (BATCH, SEQ)
HD = 64
SCALE = 0.125
NEGATIVE = -1e30
EPSILON = 1e-05
block_limit = 1024


def spans(total):
    if total > block_limit and total % block_limit == 0:
        return (block_limit, total // block_limit)
    return (total, 1)


def heads_of(matrix):
    return matrix.reshape(matrix.shape[0], -1, HD)


def normalize(values, gain, shift):
    center = values - jnp.mean(values, axis=-1, keepdims=True)
    spread = jnp.mean(center * center, axis=-1, keepdims=True)
    return center * lax.rsqrt(spread + EPSILON) * gain + shift


def norm_back(values, gain, shift, grad):
    _, pullback = jax.vjp(normalize, values, gain, shift)
    return pullback(grad)


def matmul(left, right):
    return jnp.dot(left, right, preferred_element_type=jnp.float32)


def left_product(left, right):
    return lax.dot_general(
        left, right, (((0,), (0,)), ((), ())), preferred_element_type=jnp.float32
    )


def right_product(left, right):
    return lax.dot_general(
        left, right, (((1,), (1,)), ((), ())), preferred_element_type=jnp.float32
    )


def row_total(matrix):
    return jnp.sum(matrix.astype(jnp.float32), axis=0)


def allowed_mask(query_seg, query_pos, key_seg, key_pos, causal):
    same = query_seg[:, None] == key_seg[None, :]
    if causal:
        same = jnp.logical_and(same, key_pos[None, :] <= query_pos[:, None])
    return same


def block_terms(
    query_block, upstream_block, logsum_block, delta_block, allowed, key_block, value_block
):
    scores = (
        jnp.einsum("qhd,khd->hqk", query_block, key_block, preferred_element_type=jnp.float32)
        * SCALE
    )
    scores = jnp.where(allowed[None], scores, NEGATIVE)
    probs = jnp.where(allowed[None], jnp.exp(scores - logsum_block[:, :, None]), 0.0)
    dprobs = jnp.einsum(
        "qhd,khd->hqk", upstream_block, value_block, preferred_element_type=jnp.float32
    )
    dscores = (probs * (dprobs - delta_block[:, :, None]) * SCALE).astype(jnp.bfloat16)
    return (probs.astype(jnp.bfloat16), dscores)


def attend(queries, keys, values, query_seg, query_pos, key_ids, causal):
    row_count = queries.shape[0]
    head_count = queries.shape[1] // HD
    query_heads = heads_of(queries)
    all_keys, all_values = (
        lax.all_gather(keys, SEQ, axis=0, tiled=True),
        lax.all_gather(values, SEQ, axis=0, tiled=True),
    )
    block_rows, block_count = spans(all_keys.shape[0])

    def scored(index):
        offset = index * block_rows
        key_block = heads_of(lax.dynamic_slice_in_dim(all_keys, offset, block_rows, 0))
        key_pos = offset + jnp.arange(block_rows, dtype=jnp.int32)
        key_seg = lax.dynamic_slice_in_dim(key_ids, offset, block_rows, 0)
        allowed = allowed_mask(query_seg, query_pos, key_seg, key_pos, causal)[None]
        scores = (
            jnp.einsum("qhd,khd->hqk", query_heads, key_block, preferred_element_type=jnp.float32)
            * SCALE
        )
        return (jnp.where(allowed, scores, NEGATIVE), allowed)

    def stat_step(index, state):
        run_max, run_sum = state
        scores, allowed = scored(index)
        new_max = jnp.maximum(run_max, jnp.max(scores, axis=2))
        weights = jnp.where(allowed, jnp.exp(scores - new_max[:, :, None]), 0.0)
        run_sum = run_sum * jnp.exp(run_max - new_max) + jnp.sum(weights, axis=2)
        return (new_max, run_sum)

    run_max, run_sum = lax.fori_loop(
        0,
        block_count,
        stat_step,
        (
            jnp.full((head_count, row_count), NEGATIVE, jnp.float32),
            jnp.zeros((head_count, row_count), jnp.float32),
        ),
    )
    logsum = run_max + jnp.log(run_sum)

    def value_step(index, accum):
        scores, allowed = scored(index)
        probs = jnp.where(allowed, jnp.exp(scores - logsum[:, :, None]), 0.0).astype(jnp.bfloat16)
        value_block = heads_of(
            lax.dynamic_slice_in_dim(all_values, index * block_rows, block_rows, 0)
        )
        return accum + jnp.einsum(
            "hqk,khd->qhd", probs, value_block, preferred_element_type=jnp.float32
        )

    accum = lax.fori_loop(
        0, block_count, value_step, jnp.zeros((row_count, head_count, HD), jnp.float32)
    )
    outcome = accum.reshape(row_count, head_count * HD)
    return (outcome, logsum)


def head_delta(upstream, context):
    row_count = upstream.shape[0]
    return jnp.sum((upstream.astype(jnp.float32) * context).reshape(row_count, -1, HD), axis=2).T


def attend_back(queries, keys, values, upstream, logsum, delta, query_ids, key_ids, causal):
    row_count = queries.shape[0]
    head_count = queries.shape[1] // HD
    own_first = lax.axis_index(SEQ) * row_count
    own_pos = own_first + jnp.arange(row_count, dtype=jnp.int32)
    query_seg = lax.dynamic_slice_in_dim(query_ids, own_first, row_count, 0)
    key_seg = lax.dynamic_slice_in_dim(key_ids, own_first, row_count, 0)
    query_heads = heads_of(queries)
    upstream_heads = heads_of(upstream)
    empty = jnp.zeros((row_count, head_count, HD), jnp.float32)
    key_source = lax.all_gather(keys, SEQ, axis=0, tiled=True)
    value_source = lax.all_gather(values, SEQ, axis=0, tiled=True)
    block_rows, block_count = spans(key_source.shape[0])

    def key_step(index, running):
        local = index * block_rows
        key_block = heads_of(lax.dynamic_slice_in_dim(key_source, local, block_rows, 0))
        value_block = heads_of(lax.dynamic_slice_in_dim(value_source, local, block_rows, 0))
        block_seg = lax.dynamic_slice_in_dim(key_ids, local, block_rows, 0)
        block_pos = local + jnp.arange(block_rows, dtype=jnp.int32)
        allowed = allowed_mask(query_seg, own_pos, block_seg, block_pos, causal)
        probs, dscores = block_terms(
            query_heads, upstream_heads, logsum, delta, allowed, key_block, value_block
        )
        return running + jnp.einsum(
            "hqk,khd->qhd", dscores, key_block, preferred_element_type=jnp.float32
        )

    dqueries = lax.fori_loop(0, block_count, key_step, empty)
    all_logsum, all_delta = (
        lax.all_gather(logsum, SEQ, axis=1, tiled=True),
        lax.all_gather(delta, SEQ, axis=1, tiled=True),
    )
    key_heads = heads_of(keys)
    value_heads = heads_of(values)
    piece_queries = lax.all_gather(queries, SEQ, axis=0, tiled=True)
    piece_upstream = lax.all_gather(upstream, SEQ, axis=0, tiled=True)
    query_block_rows, block_count = spans(piece_queries.shape[0])

    def query_step(index, running):
        key_total, value_total = running
        local = index * query_block_rows
        query_block = heads_of(lax.dynamic_slice_in_dim(piece_queries, local, query_block_rows, 0))
        upstream_block = heads_of(
            lax.dynamic_slice_in_dim(piece_upstream, local, query_block_rows, 0)
        )
        logsum_block = lax.dynamic_slice_in_dim(all_logsum, local, query_block_rows, 1)
        delta_block = lax.dynamic_slice_in_dim(all_delta, local, query_block_rows, 1)
        block_seg = lax.dynamic_slice_in_dim(query_ids, local, query_block_rows, 0)
        block_pos = local + jnp.arange(query_block_rows, dtype=jnp.int32)
        allowed = allowed_mask(block_seg, block_pos, key_seg, own_pos, causal)
        probs, dscores = block_terms(
            query_block, upstream_block, logsum_block, delta_block, allowed, key_heads, value_heads
        )
        key_total = key_total + jnp.einsum(
            "hqk,qhd->khd", dscores, query_block, preferred_element_type=jnp.float32
        )
        value_total = value_total + jnp.einsum(
            "hqk,qhd->khd", probs, upstream_block, preferred_element_type=jnp.float32
        )
        return (key_total, value_total)

    key_grad, value_grad = lax.fori_loop(0, block_count, query_step, (empty, empty))
    key_grad = key_grad.reshape(row_count, -1)
    value_grad = value_grad.reshape(row_count, -1)
    return (dqueries.reshape(row_count, -1), key_grad, value_grad)


def shards(
    tokens,
    memory,
    target_segments,
    memory_segments,
    cotangent,
    selfquery,
    selfkey,
    selfvalue,
    selfout,
    selfqbias,
    selfvbias,
    selfobias,
    selfgain,
    selfshift,
    crossquery,
    crosskey,
    crossvalue,
    crossout,
    crossqbias,
    crossvbias,
    crossobias,
    crossgain,
    crossshift,
    innerweight,
    innerbias,
    outerweight,
    outerbias,
    finalgain,
    finalshift,
):
    inputs = tokens[0]
    source = memory[0]
    target_ids = target_segments[0]
    source_ids = memory_segments[0]
    row_count = inputs.shape[0]
    own_first = lax.axis_index(SEQ) * row_count
    own_pos = own_first + jnp.arange(row_count, dtype=jnp.int32)
    query_seg = lax.dynamic_slice_in_dim(target_ids, own_first, row_count, 0)
    (
        query_full,
        key_full,
        value_full,
        out_full,
        qbias_full,
        vbias_full,
        obias_full,
        sgain_full,
        sshift_full,
    ) = (
        lax.all_gather(selfquery, BOTH, axis=0, tiled=True),
        lax.all_gather(selfkey, BOTH, axis=0, tiled=True),
        lax.all_gather(selfvalue, BOTH, axis=0, tiled=True),
        lax.all_gather(selfout, BOTH, axis=0, tiled=True),
        lax.all_gather(selfqbias, BOTH, axis=0, tiled=True),
        lax.all_gather(selfvbias, BOTH, axis=0, tiled=True),
        lax.all_gather(selfobias, BOTH, axis=0, tiled=True),
        lax.all_gather(selfgain, BOTH, axis=0, tiled=True),
        lax.all_gather(selfshift, BOTH, axis=0, tiled=True),
    )
    sgain = sgain_full.astype(jnp.float32)
    sshift = sshift_full.astype(jnp.float32)
    query_self = (matmul(inputs, query_full) + qbias_full.astype(jnp.float32)).astype(jnp.bfloat16)
    key_self = matmul(inputs, key_full).astype(jnp.bfloat16)
    value_self = (matmul(inputs, value_full) + vbias_full.astype(jnp.float32)).astype(jnp.bfloat16)
    attn_self, logsum_self = attend(
        query_self, key_self, value_self, query_seg, own_pos, target_ids, True
    )
    self_low = attn_self.astype(jnp.bfloat16)
    hidden_one = (
        inputs.astype(jnp.float32) + matmul(self_low, out_full) + obias_full.astype(jnp.float32)
    )
    first = normalize(hidden_one, sgain, sshift)
    first_low = first.astype(jnp.bfloat16)
    (
        cquery_full,
        ckey_full,
        cvalue_full,
        cout_full,
        cqbias_full,
        cvbias_full,
        cobias_full,
        cgain_full,
        cshift_full,
    ) = (
        lax.all_gather(crossquery, BOTH, axis=0, tiled=True),
        lax.all_gather(crosskey, BOTH, axis=0, tiled=True),
        lax.all_gather(crossvalue, BOTH, axis=0, tiled=True),
        lax.all_gather(crossout, BOTH, axis=0, tiled=True),
        lax.all_gather(crossqbias, BOTH, axis=0, tiled=True),
        lax.all_gather(crossvbias, BOTH, axis=0, tiled=True),
        lax.all_gather(crossobias, BOTH, axis=0, tiled=True),
        lax.all_gather(crossgain, BOTH, axis=0, tiled=True),
        lax.all_gather(crossshift, BOTH, axis=0, tiled=True),
    )
    cgain = cgain_full.astype(jnp.float32)
    cshift = cshift_full.astype(jnp.float32)
    query_cross = (matmul(first_low, cquery_full) + cqbias_full.astype(jnp.float32)).astype(
        jnp.bfloat16
    )
    key_cross = matmul(source, ckey_full).astype(jnp.bfloat16)
    value_cross = (matmul(source, cvalue_full) + cvbias_full.astype(jnp.float32)).astype(
        jnp.bfloat16
    )
    attn_cross, logsum_cross = attend(
        query_cross, key_cross, value_cross, query_seg, own_pos, source_ids, False
    )
    cross_low = attn_cross.astype(jnp.bfloat16)
    hidden_two = first + matmul(cross_low, cout_full) + cobias_full.astype(jnp.float32)
    second = normalize(hidden_two, cgain, cshift)
    second_low = second.astype(jnp.bfloat16)
    inner_full, ibias_full, outer_full, obias_feed, fgain_full, fshift_full = (
        lax.all_gather(innerweight, BOTH, axis=0, tiled=True),
        lax.all_gather(innerbias, BOTH, axis=0, tiled=True),
        lax.all_gather(outerweight, BOTH, axis=0, tiled=True),
        lax.all_gather(outerbias, BOTH, axis=0, tiled=True),
        lax.all_gather(finalgain, BOTH, axis=0, tiled=True),
        lax.all_gather(finalshift, BOTH, axis=0, tiled=True),
    )
    fgain = fgain_full.astype(jnp.float32)
    fshift = fshift_full.astype(jnp.float32)
    smooth = partial(jax.nn.gelu, approximate=False)
    inner_pre = matmul(second_low, inner_full) + ibias_full.astype(jnp.float32)
    activation = smooth(inner_pre).astype(jnp.bfloat16)
    hidden_three = second + matmul(activation, outer_full) + obias_feed.astype(jnp.float32)
    output = normalize(hidden_three, fgain, fshift).astype(jnp.bfloat16)
    grad_hidden3, grad_fgain, grad_fshift = norm_back(
        hidden_three, fgain, fshift, cotangent[0].astype(jnp.float32)
    )
    branch_grad = grad_hidden3.astype(jnp.bfloat16)
    grad_outer = left_product(activation, branch_grad)
    grad_obias_feed = row_total(branch_grad)
    _, gelu_back = jax.vjp(smooth, inner_pre)
    inner_grad = gelu_back(right_product(branch_grad, outer_full))[0].astype(jnp.bfloat16)
    grad_inner = left_product(second_low, inner_grad)
    grad_ibias = row_total(inner_grad)
    grad_second = grad_hidden3 + right_product(inner_grad, inner_full)
    feed_grads = (
        lax.psum_scatter(grad_inner, BOTH, scatter_dimension=0, tiled=True),
        lax.psum_scatter(grad_ibias, BOTH, scatter_dimension=0, tiled=True),
        lax.psum_scatter(grad_outer, BOTH, scatter_dimension=0, tiled=True),
        lax.psum_scatter(grad_obias_feed, BOTH, scatter_dimension=0, tiled=True),
        lax.psum_scatter(grad_fgain, BOTH, scatter_dimension=0, tiled=True),
        lax.psum_scatter(grad_fshift, BOTH, scatter_dimension=0, tiled=True),
    )
    grad_hidden2, grad_cgain, grad_cshift = norm_back(hidden_two, cgain, cshift, grad_second)
    cross_branch = grad_hidden2.astype(jnp.bfloat16)
    grad_cout = left_product(cross_low, cross_branch)
    grad_cobias = row_total(cross_branch)
    cross_up = right_product(cross_branch, cout_full).astype(jnp.bfloat16)
    cross_delta = head_delta(cross_up, attn_cross)
    cq_grad, ck_grad, cv_grad = attend_back(
        query_cross,
        key_cross,
        value_cross,
        cross_up,
        logsum_cross,
        cross_delta,
        target_ids,
        source_ids,
        False,
    )
    cq_low = cq_grad.astype(jnp.bfloat16)
    ck_low = ck_grad.astype(jnp.bfloat16)
    cv_low = cv_grad.astype(jnp.bfloat16)
    grad_cquery = left_product(first_low, cq_low)
    grad_cqbias = row_total(cq_low)
    grad_ckey = left_product(source, ck_low)
    grad_cvalue = left_product(source, cv_low)
    grad_cvbias = row_total(cv_low)
    memory_grad = right_product(ck_low, ckey_full) + right_product(cv_low, cvalue_full)
    grad_first = grad_hidden2 + right_product(cq_low, cquery_full)
    cross_grads = (
        lax.psum_scatter(grad_cquery, BOTH, scatter_dimension=0, tiled=True),
        lax.psum_scatter(grad_ckey, BOTH, scatter_dimension=0, tiled=True),
        lax.psum_scatter(grad_cvalue, BOTH, scatter_dimension=0, tiled=True),
        lax.psum_scatter(grad_cout, BOTH, scatter_dimension=0, tiled=True),
        lax.psum_scatter(grad_cqbias, BOTH, scatter_dimension=0, tiled=True),
        lax.psum_scatter(grad_cvbias, BOTH, scatter_dimension=0, tiled=True),
        lax.psum_scatter(grad_cobias, BOTH, scatter_dimension=0, tiled=True),
        lax.psum_scatter(grad_cgain, BOTH, scatter_dimension=0, tiled=True),
        lax.psum_scatter(grad_cshift, BOTH, scatter_dimension=0, tiled=True),
    )
    grad_hidden1, grad_sgain, grad_sshift = norm_back(hidden_one, sgain, sshift, grad_first)
    self_branch = grad_hidden1.astype(jnp.bfloat16)
    grad_out = left_product(self_low, self_branch)
    grad_obias = row_total(self_branch)
    self_up = right_product(self_branch, out_full).astype(jnp.bfloat16)
    self_delta = head_delta(self_up, attn_self)
    sq_grad, sk_grad, sv_grad = attend_back(
        query_self,
        key_self,
        value_self,
        self_up,
        logsum_self,
        self_delta,
        target_ids,
        target_ids,
        True,
    )
    sq_low = sq_grad.astype(jnp.bfloat16)
    sk_low = sk_grad.astype(jnp.bfloat16)
    sv_low = sv_grad.astype(jnp.bfloat16)
    grad_query = left_product(inputs, sq_low)
    grad_qbias = row_total(sq_low)
    grad_key = left_product(inputs, sk_low)
    grad_value = left_product(inputs, sv_low)
    grad_vbias = row_total(sv_low)
    tokens_grad = (
        grad_hidden1
        + right_product(sq_low, query_full)
        + right_product(sk_low, key_full)
        + right_product(sv_low, value_full)
    )
    self_grads = (
        lax.psum_scatter(grad_query, BOTH, scatter_dimension=0, tiled=True),
        lax.psum_scatter(grad_key, BOTH, scatter_dimension=0, tiled=True),
        lax.psum_scatter(grad_value, BOTH, scatter_dimension=0, tiled=True),
        lax.psum_scatter(grad_out, BOTH, scatter_dimension=0, tiled=True),
        lax.psum_scatter(grad_qbias, BOTH, scatter_dimension=0, tiled=True),
        lax.psum_scatter(grad_vbias, BOTH, scatter_dimension=0, tiled=True),
        lax.psum_scatter(grad_obias, BOTH, scatter_dimension=0, tiled=True),
        lax.psum_scatter(grad_sgain, BOTH, scatter_dimension=0, tiled=True),
        lax.psum_scatter(grad_sshift, BOTH, scatter_dimension=0, tiled=True),
    )
    return (
        (output[None], tokens_grad[None], memory_grad[None])
        + tuple(self_grads)
        + tuple(cross_grads)
        + tuple(feed_grads)
    )


LOW = jnp.bfloat16
WIDE = jnp.float32
MESH = pl.DeviceIdType.MESH
VMEM_BYTES = 64 << 20
WIRES = 192
ALL2 = pl.ds(0, 2)
ALL3 = pl.ds(0, 3)
ALL4 = pl.ds(0, 4)
ALL16 = pl.ds(0, 16)
ALL768 = pl.ds(0, 768)
SHARED = (2, 3, 4, 5)


def shares(unit):
    cut = 384 if unit in SHARED else 512
    return (pl.ds(0, cut), pl.ds(cut, 768 - cut))


def place():
    b, s = lax.axis_index(BATCH), lax.axis_index(SEQ)
    return (lax.div(b, 2), lax.rem(b, 2), lax.rem(s, 2), lax.div(s, 2))


def device(x, c, y, z):
    return (2 * x + c, 2 * z + y)


FORWARD = (
    0, "prepare", 10, 1, 20, 11, 2, 30, 21, 12, 3, "tokens", 40, 31, 22, 13, 4, 50, 41, 32, 23, 14,
    "memory", 60, 51, 42, 33, 24, 70, 61, 52, 43, 34, 25, "self", 71, 62, 53, 44, 35, 72, "project",
    63, "cross", 54, 45, 73, 55, "feed1", "feed2", 64, 74,
)
BACKWARD = (
    "slopes", 60, 70, "inner4", 61, 40, "inner5", 50, 41, 51, 71, "inner", "norm2", "cross",
    "grads2", 20, 30, 42, 52, 62, 72, "inputs2", "norm1", 21, 31, "home", "self", "grads1", 0, 10,
    22, 32, "v", "vy", "inputs1", 63, 73, 1, 11, 43, 53, "vx", 23, 33, 44, 54, "vp", 24, 2, 34,
    "vm", 12, 3, 13,
)


class Peers:
    def __init__(self):
        self.x, self.c, self.y, self.z = place()
        x, c, y, z = self.x, self.c, self.y, self.z
        b, s = lax.axis_index(BATCH), lax.axis_index(SEQ)
        self.across_x = device(1 - x, c, y, z)
        self.across_y = device(x, c, 1 - y, z)
        self.sibling = device(x, 1 - c, y, z)
        odd = lax.rem(z, 2)
        self.twin = z + 1 - 2 * odd
        self.share_z = pl.ds(2 * odd, 2)
        self.twin_share_z = pl.ds(2 - 2 * odd, 2)
        self.across_z = device(x, c, y, 3 - z)
        self.beside_z = device(x, c, y, self.twin)
        self.s = s
        self.after = (b, lax.rem(s + 1, 8))
        self.before = (b, lax.rem(s + 7, 8))
        self.mirror = (b, 7 - s)
        self.folds = [(b, lax.rem(14 - s, 8)), (b, lax.rem(16 - s, 8))]
        self.alone = [self.folds[k][1] == s for k in range(2)]

    def greet(self):
        barrier = pltpu.get_barrier_semaphore()
        always = [
            self.across_x, self.across_y, self.across_z, self.beside_z, self.sibling, self.after, self.before, self.mirror,
        ]
        for peer in always:
            pl.semaphore_signal(barrier, inc=1, device_id=peer, device_id_type=MESH)
        for peer, alone in zip(self.folds, self.alone):
            @pl.when(jnp.logical_not(alone))
            def _():
                pl.semaphore_signal(barrier, inc=1, device_id=peer, device_id_type=MESH)

    def meet(self):
        barrier = pltpu.get_barrier_semaphore()
        others = [jnp.where(alone, 0, 1) for alone in self.alone]
        pl.semaphore_wait(barrier, 8 + others[0] + others[1])


class Wires:
    def __init__(self, send, recv):
        self.send, self.recv, self.used = send, recv, 0

    def copies(self, pairs, target):
        made = []
        assert self.used + len(pairs) <= WIRES
        for source, landing in pairs:
            made.append(
                pltpu.make_async_remote_copy(
                    src_ref=source,
                    dst_ref=landing,
                    send_sem=self.send.at[self.used],
                    recv_sem=self.recv.at[self.used],
                    device_id=target,
                    device_id_type=MESH,
                )
            )
            self.used += 1
        return made


def start(copies):
    for copy in copies:
        copy.start()


def landed(copies):
    for copy in copies:
        copy.wait_recv()


def sent(copies):
    for copy in copies:
        copy.wait_send()


class Gather:
    def __init__(self, peers, wires, held, outer, vectors):
        self.peers, self.wires = peers, wires
        self.held, self.outer, self.vectors = held, outer, vectors
        self.steps = [{} for _ in range(8)]

    def parts(self, unit, x, c, z, y, columns=ALL768):
        both = y is None
        if unit >= 6:
            rows = pl.ds(48 * (unit - 6), 48)
            return [self.outer.at[x, c, z, ALL2 if both else y, rows, columns]]
        refs = [self.held.at[2 * unit + c, x, z, ALL2 if both else y, ALL3, ALL16, columns]]
        if unit == 0 and columns.start == 0:
            refs.append(self.vectors.at[x, c, z, ALL2 if both else y])
        return refs

    def send(self, unit, k, routes):
        made = []
        for target, spot in routes:
            pairs = [(part, part) for part in self.parts(unit, *spot)]
            made += self.wires.copies(pairs, target)
        start(made)
        self.steps[unit][k] = made

    def hop(self, unit, k):
        p = self.peers
        x, c, y, z = p.x, p.c, p.y, p.z
        if k > 0:
            landed(self.steps[unit][k - 1])
        if k == 0:
            self.send(unit, 0, [(p.across_z, (x, c, z, y))])
        elif k == 1:
            self.send(unit, 1, [(p.beside_z, (x, c, z, y)), (p.beside_z, (x, c, 3 - z, y))])
        elif k == 2:
            column = (x, c, ALL4, y)
            self.send(unit, 2, [(p.across_x, column), (p.across_y, column)])
        elif k == 3:
            over_x, over_y = shares(unit)
            depth = p.share_z if unit in SHARED else ALL4
            routes = [(p.across_x, (x, c, depth, 1 - y, over_x))]
            routes += [(p.across_y, (1 - x, c, depth, y, over_y))]
            self.send(unit, 3, routes)
            self.send(unit, 6, [(p.sibling, (x, c, ALL4, None)), (p.sibling, (1 - x, c, ALL4, y))])
        elif k == 4 and unit in SHARED:
            self.send(unit, 4, [(p.beside_z, (1 - x, c, p.share_z, 1 - y))])
        else:
            self.send(unit, 5, [(p.sibling, (1 - x, c, ALL4, 1 - y))])

    def last(self, unit):
        landed(self.steps[unit][5])
        landed(self.steps[unit][6])

    def close(self, units):
        for unit in units:
            for copies in self.steps[unit].values():
                sent(copies)


def gather_pack(unit, peers, squares, inner, held):
    x, c, y, z = peers.x, peers.c, peers.y, peers.z
    rests = []
    for k in range(2):
        m = 2 * unit + k
        values = squares[m][...] if m < 8 else inner[:, 768 * (m - 8) : 768 * (m - 7)]
        values = values.astype(WIDE)
        body = jnp.where(y == 0, values[0:16], values[8:24])
        rests.append(jnp.where(y == 0, values[16:24], values[0:8]))
        held[2 * unit + c, x, z, y, k] = body.astype(LOW)
    held[2 * unit + c, x, z, y, 2] = jnp.concatenate(rests, axis=0).astype(LOW)


def gather_vectors(peers, smalls, board, vectors):
    board[...] = jnp.zeros((16, 128), WIDE)
    for j, small in enumerate(smalls):
        board[j : j + 1, 0 : small.shape[1]] = small[...].astype(WIDE)
    index = (2 * peers.x + peers.c) * 8 + peers.s
    wide = board[...]
    row = lax.broadcasted_iota(jnp.int32, (16, 128), 0)
    by24 = pltpu.roll(wide, lax.rem(24 * index, 128), 1)
    by96 = pltpu.roll(wide, lax.rem(96 * index, 128), 1)
    rolled = jnp.where(row == 13, by96, by24).astype(LOW)
    vectors[peers.x, peers.c, peers.z, peers.y] = rolled


def assemble(unit, held, mats):
    def one(step, carry):
        x, c, z = lax.div(step, 8), lax.rem(lax.div(step, 4), 2), lax.rem(step, 4)
        low_half = held[2 * unit + c, x, z, 0, 2].astype(WIDE)
        high_half = held[2 * unit + c, x, z, 1, 2].astype(WIDE)
        for k in range(2):
            part = slice(8 * k, 8 * k + 8)
            middle = jnp.concatenate([low_half[part], high_half[part]], axis=0)
            mats[2 * unit + k, x, c, z, 0:16, :] = held[2 * unit + c, x, z, 0, k]
            mats[2 * unit + k, x, c, z, 16:32, :] = middle.astype(LOW)
            mats[2 * unit + k, x, c, z, 32:48, :] = held[2 * unit + c, x, z, 1, k]
        return carry

    lax.fori_loop(0, 16, one, 0)


def vmem():
    return pl.BlockSpec(memory_space=pltpu.VMEM)


def dot(left, right):
    return jnp.dot(left, right, preferred_element_type=WIDE)


def dot_nt(left, right):
    return lax.dot_general(left, right, (((1,), (1,)), ((), ())), preferred_element_type=WIDE)


def dot_tn(left, right):
    return lax.dot_general(left, right, (((0,), (0,)), ((), ())), preferred_element_type=WIDE)


def strip(n):
    return slice(256 * n, 256 * n + 256)


def columns(mats, m, n):
    return mats[m, :, :, :, :, strip(n)].reshape(768, 256)


def rows(mats, m, x):
    return mats[m, x].reshape(384, 768)


def outer_columns(outer, j, n):
    return outer[j // 2, j % 2, :, :, :, strip(n)].reshape(768, 256)


def outer_rows(outer, j, half):
    return outer[j // 2, j % 2, 2 * half : 2 * half + 2].reshape(384, 768)


def unpack_vectors(vectors, vec, inner_bias):
    lane = lax.broadcasted_iota(jnp.int32, (16, 128), 1)

    def shard(d):
        b, s = d // 8, d % 8
        return vectors[b // 2, b % 2, s // 2, s % 2].astype(WIDE)

    for width, tiles, ref in ((24, 6, vec), (96, 24, inner_bias)):
        for t in range(tiles):
            first = (128 * t) // width
            final = (128 * t + 127) // width
            total = shard(first)
            for d in range(first + 1, final + 1):
                total = jnp.where(lane >= width * d - 128 * t, shard(d), total)
            if width == 24:
                ref[:, 128 * t : 128 * t + 128] = total
            else:
                ref[0:1, 128 * t : 128 * t + 128] = total[13:14]


def pack_vectors(vec, inner_bias, c, place_at):
    lane = lax.broadcasted_iota(jnp.int32, (16, 128), 1)
    row = lax.broadcasted_iota(jnp.int32, (16, 128), 0)

    def shard(ref, width, d):
        t, offset = width * d // 128, width * d % 128
        block = ref[:, 128 * t : 128 * t + 128]
        if offset + width > 128:
            block = jnp.where(lane >= offset, block, ref[:, 128 * t + 128 : 128 * t + 256])
        return block

    for d in range(32):
        b, s = d // 8, d % 8
        block = shard(vec, 24, d)
        t, offset = 96 * d // 128, 96 * d % 128
        bias = inner_bias[0:1, 128 * t : 128 * t + 128]
        if offset + 96 > 128:
            bias = jnp.where(lane[0:1] >= offset, bias, inner_bias[0:1, 128 * t + 128 : 128 * t + 256])
        place_at(b % 2, b // 2, s // 2, s % 2, jnp.where(row == 13, jnp.broadcast_to(bias, (16, 128)), block))


def centered(values):
    center = values - jnp.mean(values, axis=-1, keepdims=True)
    scale = lax.rsqrt(jnp.mean(center * center, axis=-1, keepdims=True) + EPSILON)
    return (center * scale, scale)


def norm_grad(unit_values, scale, gain, grad):
    scaled = grad * gain
    mean = jnp.mean(scaled, axis=-1, keepdims=True)
    along = jnp.mean(scaled * unit_values, axis=-1, keepdims=True)
    return (scaled - mean - unit_values * along) * scale


def total_rows(values):
    return jnp.sum(values.astype(WIDE), axis=0, keepdims=True)


def lane_halves():
    lane = lax.broadcasted_iota(jnp.int32, (128, 128), 1)
    low_half = jnp.where(lane < 64, 1.0, 0.0).astype(LOW)
    high_half = jnp.where(lane < 64, 0.0, 1.0).astype(LOW)
    return (lane < 64, low_half, high_half)


def pair_rows(block, low_half, high_half):
    return jnp.concatenate([block * low_half, block * high_half], axis=0)


def attention(queries, keys, values, mask, probs, context):
    pick, low_half, high_half = lane_halves()

    def heads(h, carry):
        here = pl.ds(pl.multiple_of(128 * h, 128), 128)
        both = pair_rows(queries[:, here], low_half, high_half)
        bias = mask[...]
        scores = dot_nt(both, keys[:, here]) * SCALE + jnp.concatenate([bias, bias], axis=0)
        weights = jnp.exp(scores - jnp.max(scores, axis=1, keepdims=True))
        weights = weights * (1.0 / jnp.sum(weights, axis=1, keepdims=True))
        rounded = weights.astype(LOW)
        probs[h] = rounded
        mixed = dot(rounded, values[:, here])
        context[:, here] = jnp.where(pick, mixed[:128], mixed[128:]).astype(LOW)
        return carry

    lax.fori_loop(0, 6, heads, 0)


def attention_back(queries, keys, values, upstream, probs, dqueries, dkeys, dvalues, count):
    pick, low_half, high_half = lane_halves()

    def heads(h, carry):
        here = pl.ds(pl.multiple_of(128 * h, 128), 128)
        both = pair_rows(queries[:, here], low_half, high_half)
        both_up = pair_rows(upstream[:, here], low_half, high_half)
        dprobs = dot_nt(both_up, values[:, here])
        weights = probs[h].astype(WIDE)
        delta = jnp.sum(weights * dprobs, axis=1, keepdims=True)
        dscores = (weights * (dprobs - delta) * SCALE).astype(LOW)
        mixed = dot(dscores, keys[:, here])
        dqueries[:, here] = jnp.where(pick, mixed[:128], mixed[128:]).astype(LOW)
        dkeys[0:count, here] = dot_tn(dscores, both).astype(LOW)
        dvalues[0:count, here] = dot_tn(probs[h], both_up).astype(LOW)
        return carry

    lax.fori_loop(0, 6, heads, 0)


class Grads:
    ORDER = (6, 7, 4, 5, 2, 3, 0, 1)

    def __init__(self, peers, wires, held, r0, shared, pool, r2, r3, out, mine, credit, move):
        self.peers, self.wires, self.held = peers, wires, held
        self.r0, self.pool, self.r2, self.r3, self.out = r0, pool, r2, r3, out
        self.shared, self.mine, self.credit, self.move = shared, mine, credit, move
        self.kept = []
        self.stage = {}
        self.open = []
        self.first_sends = {}

    def at(self, unit):
        return self.ORDER.index(unit)

    def slot(self, unit, c):
        return jnp.where(c == self.peers.c, unit, 8 + self.at(unit) % 4)

    def ready(self, unit):
        turn = self.at(unit)
        if turn >= 4:
            sent(self.first_sends.pop(self.ORDER[turn - 4]))

    def ship(self, pairs, target):
        copies = self.wires.copies(pairs, target)
        start(copies)
        self.open += copies
        return copies

    def step0(self, unit):
        turn = self.at(unit)
        if turn >= 4:
            pl.semaphore_wait(self.credit, 1)
        ring = turn % 4
        copies = self.wires.copies([(self.held.at[8 + ring], self.r0.at[ring])], self.peers.sibling)
        start(copies)
        self.first_sends[unit] = copies
        self.stage[unit] = copies

    def corner(self, unit, depth):
        p, landing = self.peers, self.r2.at[unit, pl.ds(0, depth.size)]
        self.stage[unit] = []
        for columns, target in zip(shares(unit), (p.across_x, p.across_y)):
            source = self.held.at[unit, 1 - p.x, depth, 1 - p.y, ALL3, ALL16, columns]
            self.stage[unit] += self.ship([(source, landing.at[:, :, :, columns])], target)

    def hop(self, unit, k):
        p, held = self.peers, self.held
        x, y, z = p.x, p.y, p.z
        landed(self.stage[unit])
        if k == 0:
            turn = self.at(unit)
            ring = turn % 4

            def add(i, carry):
                j, d = lax.div(i, 4), lax.rem(i, 4)
                held[unit, j, d] = held[unit, j, d] + self.r0[ring, j, d]
                return carry

            lax.fori_loop(0, 8, add, 0)
            if turn < 4:
                pl.semaphore_signal(self.credit, inc=1, device_id=p.sibling, device_id_type=MESH)
            if unit in SHARED:
                pairs = [(held.at[unit, 1 - x, p.twin_share_z, 1 - y], self.shared.at[unit - SHARED[0]])]
                self.stage[unit] = self.ship(pairs, p.beside_z)
            else:
                self.corner(unit, ALL4)
        elif k == 0.5:
            for i in range(2):
                d = p.share_z.start + i
                block = held[unit, 1 - x, d, 1 - y] + self.shared[unit - SHARED[0], i]
                held[unit, 1 - x, d, 1 - y] = block
            self.corner(unit, p.share_z)
        elif k == 1:
            over_x, over_y = shares(unit)
            depth = p.share_z if unit in SHARED else ALL4
            for i in range(depth.size):
                d = depth.start + i
                here = (unit, x, d, 1 - y, ALL3, ALL16, over_x)
                held[here] = held[here] + self.r2[unit, i, :, :, over_x]
                here = (unit, 1 - x, d, y, ALL3, ALL16, over_y)
                held[here] = held[here] + self.r2[unit, i, :, :, over_y]
            pairs = [(held.at[unit, 1 - x, ALL4, y], self.pool.at[unit, 0])]
            self.stage[unit] = self.ship(pairs, p.across_x)
            pairs = [(held.at[unit, x, ALL4, 1 - y], self.pool.at[unit, 1])]
            self.stage[unit] += self.ship(pairs, p.across_y)
        elif k == 2:
            for d in range(4):
                total = held[unit, x, d, y].astype(WIDE) + self.pool[unit, 0, d].astype(WIDE)
                held[unit, x, d, y] = (total + self.pool[unit, 1, d].astype(WIDE)).astype(LOW)
            pairs = [(held.at[unit, x, d, y], self.r3.at[unit, i]) for i, d in enumerate((p.twin, 3 - p.twin))]
            self.stage[unit] = self.ship(pairs, p.beside_z)
        else:
            for i, d in enumerate((z, 3 - z)):
                held[unit, x, d, y] = held[unit, x, d, y] + self.r3[unit, i]
            pairs = [(held.at[unit, x, 3 - z, y], self.out.at[unit])]
            self.stage[unit] = self.ship(pairs, p.across_z)
            self.kept.append(self.move(held.at[unit, x, z, y], self.mine.at[unit]))
            start(self.kept[-1:])

    def finish(self):
        for unit in self.ORDER:
            landed(self.stage[unit])
        for copies in self.first_sends.values():
            sent(copies)
        sent(self.open)
        for copy in self.kept:
            copy.wait()

    def pair_grad(self, unit, first_left, first_right, second_left, second_right):
        self.ready(unit)
        for x in range(2):
            here = slice(384 * x, 384 * x + 384)
            one_left = jnp.transpose(first_left[:, here])
            two_left = jnp.transpose(second_left[:, here])
            for n in range(3):
                s = strip(n)
                one = dot(one_left, first_right[:, s])
                two = dot(two_left, second_right[:, s])
                for c in range(2):
                    slot = self.slot(unit, c)
                    for z in range(4):
                        for y in range(2):
                            base = 24 * (8 * c + 2 * z + y)
                            body = base + 8 * y
                            rest = base + 16 * (1 - y)
                            self.held[slot, x, z, y, 0, :, s] = one[body : body + 16].astype(LOW)
                            self.held[slot, x, z, y, 1, :, s] = two[body : body + 16].astype(LOW)
                            self.held[slot, x, z, y, 2, :, s] = jnp.concatenate(
                                [one[rest : rest + 8], two[rest : rest + 8]], axis=0
                            ).astype(LOW)

    def outer_grad(self, hidden, upstream):
        for j in range(4):
            x, c = j // 2, j % 2
            for half in range(2):
                here = slice(768 * j + 384 * half, 768 * j + 384 * half + 384)
                left = jnp.transpose(hidden[:, here])
                for n in range(3):
                    s = strip(n)
                    one = dot(left, upstream[:, s])
                    for unit in (6, 7):
                        slot = self.slot(unit, c)
                        for k in range(4):
                            base = 96 * k + 48 * (unit - 6)
                            z, y = 2 * half + k // 2, k % 2
                            block = one[base : base + 48].reshape(3, 16, 256)
                            self.held[slot, x, z, y, :, :, s] = block.astype(LOW)


def layer_kernel(*refs):
    squares_in, inner_in, outer_in, smalls_in = refs[0:8], refs[8], refs[9], refs[10:24]
    tokens_in, memory_in, cotangent_in, target_in, source_in = refs[24:29]
    output, out, mine, vout, left_out, memory_out, tokens_part = refs[29:36]
    squares, inner_own, smalls, refs = refs[36:44], refs[44], refs[45:59], refs[59:]
    (
        cotangent, target_ids, source_ids, output_low, tokens_sum,
        mats, outer, vectors, tokens, memory, board, mask_self, mask_cross,
        vec, inner_bias, query, key, value, probs, context, unit1, first_low,
        query2, key2, value2, probs2, context2, unit2, second_low,
        hidden, slope, total, grad, branch, upstream, dquery, dkey, dvalue,
        gvec, ginner,
        held, r0, shared, pool, r2, r3, vheld, v0, v1, v2, v3, left_part, memory_parts,
        credit, send, recv, local,
    ) = refs
    peers = Peers()
    peers.greet()
    c, x, y, z = peers.c, peers.x, peers.y, peers.z
    wires = Wires(send, recv)
    weights = Gather(peers, wires, held, outer, vectors)
    moves = []

    def move(source, target):
        copy = pltpu.make_async_copy(source, target, local.at[len(moves)])
        moves.append(copy)
        return copy

    grads = Grads(peers, wires, held, r0, shared, pool, r2, r3, out, mine, credit, move)
    own = slice(128, 256)
    early = [move(a, b) for a, b in zip(squares_in[0:2], squares[0:2])]
    early += [move(a, b) for a, b in zip(smalls_in, smalls)]
    loads = [move(a, b) for a, b in zip(squares_in[2:], squares[2:])]
    loads += [move(inner_in, inner_own), move(outer_in, outer.at[x, c, z, y])]
    loads += [move(target_in, target_ids), move(source_in, source_ids)]
    loads += [move(tokens_in, tokens.at[pl.ds(128, 128)]), move(cotangent_in, cotangent)]
    start(early + loads)
    state = {}

    def reduce_hop(unit, k):
        grads.hop(unit, (0, 0.5, 1, 2, 3)[k] if unit in SHARED else k)

    def follow(plan, hop, chunks):
        for step in plan:
            if step in chunks:
                chunks[step]()
            else:
                hop(step // 10, step % 10)

    def vector(j):
        return vec[j : j + 1, :]

    def pack(unit):
        gather_pack(unit, peers, squares, inner_own, held)

    def arrive(*units):
        for unit in units:
            weights.last(unit)
            if unit < 6:
                assemble(unit, held, mats)

    left = wires.copies([(tokens_in, tokens.at[pl.ds(0, 128)])], peers.after)
    mirrored = wires.copies([(memory_in, memory.at[pl.ds(128, 128)])], peers.mirror)
    folds = [
        wires.copies([(memory_in, memory.at[pl.ds(256 * k, 128)])], peers.folds[k]) for k in range(2)
    ]
    kept = [move(memory_in, memory.at[pl.ds(256 * k, 128)]) for k in range(2)]

    def prepare():
        for copy in loads:
            copy.wait()
        for unit in range(1, 6):
            pack(unit)
        fill_masks(peers, target_ids, source_ids, mask_self, mask_cross)

    def exchange_tokens():
        start(left)

    def exchange_memory():
        start(mirrored)
        for k in range(2):
            @pl.when(jnp.logical_not(peers.alone[k]))
            def _():
                start(folds[k])

            @pl.when(peers.alone[k])
            def _():
                kept[k].start()

    def self_attention():
        arrive(0, 1)
        unpack_vectors(vectors, vec, inner_bias)
        landed(left)
        for n in range(3):
            s = strip(n)
            query[:, s] = (dot(tokens[own, :], columns(mats, 0, n)) + vec[0:1, s]).astype(LOW)
            key[:, s] = dot(tokens[...], columns(mats, 1, n)).astype(LOW)
            value[:, s] = (dot(tokens[...], columns(mats, 2, n)) + vec[1:2, s]).astype(LOW)
        attention(query, key, value, mask_self, probs, context)
        for n in range(3):
            s = strip(n)
            total[:, s] = (
                tokens[own, s].astype(WIDE) + dot(context[...], columns(mats, 3, n)) + vec[2:3, s]
            )
        unit, state[1] = centered(total[...])
        unit1[...] = unit
        first = unit * vector(3) + vector(4)
        total[...] = first
        first_low[...] = first.astype(LOW)

    def cross_projections():
        arrive(2, 3)
        for n in range(3):
            s = strip(n)
            query2[:, s] = (dot(first_low[...], columns(mats, 4, n)) + vec[5:6, s]).astype(LOW)
        landed(mirrored)
        for k in range(2):
            @pl.when(jnp.logical_not(peers.alone[k]))
            def _():
                landed(folds[k])
                sent(folds[k])

            @pl.when(peers.alone[k])
            def _():
                kept[k].wait()

        for n in range(3):
            s = strip(n)
            key2[:, s] = dot(memory[...], columns(mats, 5, n)).astype(LOW)
            value2[:, s] = (dot(memory[...], columns(mats, 6, n)) + vec[6:7, s]).astype(LOW)

    def cross_attention():
        attention(query2, key2, value2, mask_cross, probs2, context2)
        for n in range(3):
            s = strip(n)
            total[:, s] = total[:, s] + dot(context2[...], columns(mats, 7, n)) + vec[7:8, s]
        unit, state[2] = centered(total[...])
        unit2[...] = unit
        second = unit * vector(8) + vector(9)
        total[...] = second + vector(10)
        second_low[...] = second.astype(LOW)

    def feed(j):
        for n in range(3):
            s = slice(768 * j + 256 * n, 768 * j + 256 * n + 256)
            pre = dot(second_low[...], columns(mats, 8 + j, n)) + inner_bias[0:1, s]
            normal = 0.5 + 0.5 * lax.erf(pre * 0.7071067811865476)
            hidden[:, s] = (pre * normal).astype(LOW)
            slope[:, s] = (
                normal + pre * (0.3989422804014327 * jnp.exp(-0.5 * pre * pre))
            ).astype(LOW)

    def feed_one():
        arrive(4)
        feed(0)
        feed(1)

    def feed_two():
        arrive(5)
        feed(2)
        feed(3)
        weights.close(range(6))

    forward = {
        "prepare": prepare,
        "tokens": exchange_tokens,
        "memory": exchange_memory,
        "self": self_attention,
        "project": cross_projections,
        "cross": cross_attention,
        "feed1": feed_one,
        "feed2": feed_two,
    }
    for copy in early:
        copy.wait()
    pack(0)
    gather_vectors(peers, smalls, board, vectors)
    peers.meet()
    follow(FORWARD, weights.hop, forward)
    arrive(6, 7)
    for n in range(3):
        s = strip(n)
        summed = total[:, s]
        for j in range(4):
            here = slice(768 * j, 768 * j + 768)
            summed = summed + dot(hidden[:, here], outer_columns(outer, j, n))
        total[:, s] = summed
    unit, scale3 = centered(total[...])
    arrived = cotangent[...].astype(WIDE)
    dhidden = norm_grad(unit, scale3, vector(11), arrived)
    grad[...] = dhidden
    branch[...] = dhidden.astype(LOW)
    grads.outer_grad(hidden, branch)
    grads.step0(6)
    grads.step0(7)
    output_low[...] = (unit * vector(11) + vector(12)).astype(LOW)
    ends = [move(output_low, output)]
    start(ends)
    gvec[11:12, :] = total_rows(arrived * unit)
    gvec[12:13, :] = total_rows(arrived)
    gvec[10:11, :] = total_rows(branch[...])
    weights.close(range(6, 8))
    sent(left + mirrored)

    def slopes():
        for j in range(4):
            for half in range(2):
                s = slice(768 * j + 384 * half, 768 * j + 384 * half + 384)
                raised = dot_nt(branch[...], outer_rows(outer, j, half)) * slope[:, s].astype(WIDE)
                raised = raised.astype(LOW)
                slope[:, s] = raised
                ginner[0:1, s] = total_rows(raised)

    def inner_grad(unit):
        one, two = [slope.at[:, pl.ds(768 * j, 768)] for j in (2 * unit - 8, 2 * unit - 7)]
        grads.pair_grad(unit, second_low, one, second_low, two)
        grads.step0(unit)

    def inner_back():
        for x in range(2):
            s = slice(384 * x, 384 * x + 384)
            summed = grad[:, s]
            for j in range(4):
                summed = summed + dot_nt(slope[:, 768 * j : 768 * j + 768], rows(mats, 8 + j, x))
            grad[:, s] = summed

    def norm_back_at(held_unit, scale, gain, gain_row):
        arrived = grad[...]
        unit = held_unit[...]
        gvec[gain_row : gain_row + 1, :] = total_rows(arrived * unit)
        gvec[gain_row + 1 : gain_row + 2, :] = total_rows(arrived)
        dhidden = norm_grad(unit, scale, gain, arrived)
        grad[...] = dhidden
        branch[...] = dhidden.astype(LOW)
        gvec[gain_row - 1 : gain_row, :] = total_rows(branch[...])

    def cross_norm():
        norm_back_at(unit2, state[2], vector(8), 8)
        for x in range(2):
            upstream[:, 384 * x : 384 * x + 384] = dot_nt(branch[...], rows(mats, 7, x)).astype(LOW)

    def cross_back():
        attention_back(query2, key2, value2, upstream, probs2, dquery, dkey, dvalue, 384)

    def cross_grads():
        grads.pair_grad(2, first_low, dquery, memory, dkey)
        grads.step0(2)
        grads.pair_grad(3, memory, dvalue, context2, branch)
        grads.step0(3)

    def cross_inputs():
        gvec[5:6, :] = total_rows(dquery[...])
        gvec[6:7, :] = total_rows(dvalue[...])
        for x in range(2):
            s = slice(384 * x, 384 * x + 384)
            grad[:, s] = grad[:, s] + dot_nt(dquery[...], rows(mats, 4, x))
            backed = dot_nt(dkey[...], rows(mats, 5, x)) + dot_nt(dvalue[...], rows(mats, 6, x))
            for block in range(3):
                memory_parts[block, :, s] = backed[128 * block : 128 * block + 128].astype(LOW)

    back = [
        wires.copies([(memory_parts.at[2 * k], memory_out.at[2 * k])], peers.folds[k]) for k in range(2)
    ]
    stay = [
        move(memory_parts.at[2 * k], memory_out.at[2 * k]) for k in range(2)
    ]

    def memory_home():
        state["home"] = grads.ship([(memory_parts.at[1], memory_out.at[1])], peers.mirror)
        for k in range(2):
            @pl.when(jnp.logical_not(peers.alone[k]))
            def _():
                start(back[k])

            @pl.when(peers.alone[k])
            def _():
                stay[k].start()

    def self_norm():
        norm_back_at(unit1, state[1], vector(3), 3)
        for x in range(2):
            upstream[:, 384 * x : 384 * x + 384] = dot_nt(branch[...], rows(mats, 3, x)).astype(LOW)

    dkey_two, dvalue_two = dkey.at[pl.ds(0, 256)], dvalue.at[pl.ds(0, 256)]

    def self_back():
        attention_back(query, key, value, upstream, probs, dquery, dkey, dvalue, 256)

    def self_grads():
        grads.pair_grad(0, tokens.at[pl.ds(128, 128)], dquery, tokens, dkey_two)
        grads.step0(0)
        grads.pair_grad(1, tokens, dvalue_two, context, branch)
        grads.step0(1)

    def vectors_near():
        gvec[0:1, :] = total_rows(dquery[...])
        gvec[1:2, :] = total_rows(dvalue_two[...])
        gvec[13:16, :] = jnp.zeros((3, 768), WIDE)

        def put(c, x, z, y, block):
            vheld[c, x, z, y] = block

        pack_vectors(gvec, ginner, peers.c, put)
        state["v"] = grads.ship([(vheld.at[1 - c], v0)], peers.sibling)

    def vectors_y():
        landed(state["v"])
        vheld[c] = vheld[c] + v0[...]
        state["v"] = grads.ship([(vheld.at[c, ALL2, ALL4, 1 - y], v1)], peers.across_y)

    def vectors_x():
        landed(state["v"])
        for j in range(2):
            for k in range(4):
                vheld[c, j, k, y] = vheld[c, j, k, y] + v1[j, k]
        state["v"] = grads.ship([(vheld.at[c, 1 - x, ALL4, y], v2)], peers.across_x)

    def vectors_p():
        landed(state["v"])
        for k in range(4):
            vheld[c, x, k, y] = vheld[c, x, k, y] + v2[k]
        twin = peers.twin
        pairs = [(vheld.at[c, x, twin, y], v3.at[0]), (vheld.at[c, x, 3 - twin, y], v3.at[1])]
        state["v"] = grads.ship(pairs, peers.beside_z)

    def vectors_m():
        landed(state["v"])
        vheld[c, x, z, y] = vheld[c, x, z, y] + v3[0]
        vheld[c, x, 3 - z, y] = vheld[c, x, 3 - z, y] + v3[1]
        state["v"] = grads.ship([(vheld.at[c, x, 3 - z, y], vout.at[1])], peers.across_z)
        ends.append(move(vheld.at[c, x, z, y], vout.at[0]))
        start(ends[-1:])

    def self_inputs():
        for k in range(2):
            s = slice(384 * k, 384 * k + 384)
            backed = dot_nt(dkey_two[...], rows(mats, 1, k)) + dot_nt(dvalue_two[...], rows(mats, 2, k))
            left_part[:, s] = backed[0:128].astype(LOW)
            tokens_sum[:, s] = grad[:, s] + dot_nt(dquery[...], rows(mats, 0, k)) + backed[128:256]
        ends.append(move(tokens_sum, tokens_part))
        start(ends[-1:])
        state["left"] = grads.ship([(left_part, left_out)], peers.before)

    backward = {
        "slopes": slopes,
        "inner4": partial(inner_grad, 4),
        "inner5": partial(inner_grad, 5),
        "inner": inner_back,
        "norm2": cross_norm,
        "cross": cross_back,
        "grads2": cross_grads,
        "inputs2": cross_inputs,
        "home": memory_home,
        "norm1": self_norm,
        "self": self_back,
        "grads1": self_grads,
        "inputs1": self_inputs,
        "v": vectors_near,
        "vy": vectors_y,
        "vx": vectors_x,
        "vp": vectors_p,
        "vm": vectors_m,
    }
    follow(BACKWARD, reduce_hop, backward)
    landed(state["v"] + state["left"] + state["home"])
    for k in range(2):
        @pl.when(jnp.logical_not(peers.alone[k]))
        def _():
            landed(back[k])
            sent(back[k])

        @pl.when(peers.alone[k])
        def _():
            stay[k].wait()

    grads.finish()
    for copy in ends:
        copy.wait()


def fill_masks(peers, target_ids, source_ids, mask_self, mask_cross):
    def ids(ref, block):
        here = pl.ds(pl.multiple_of(128 * block, 128), 128)
        return jnp.broadcast_to(ref[:, here].astype(WIDE), (128, 128))

    s = peers.s
    here = ids(target_ids, s)
    queries = jnp.transpose(here)
    row = lax.broadcasted_iota(jnp.int32, (128, 128), 0)
    column = lax.broadcasted_iota(jnp.int32, (128, 128), 1)
    before = jnp.where(s > 0, ids(target_ids, lax.rem(s + 7, 8)), -1.0)
    mask_self[:, 0:128] = jnp.where(queries == before, 0.0, NEGATIVE)
    seen = jnp.where(queries == here, 0.0, NEGATIVE)
    mask_self[:, 128:256] = jnp.where(column <= row, seen, NEGATIVE)
    for k in range(3):
        block = ids(source_ids, lax.rem(14 + k - s, 8))
        mask_cross[:, 128 * k : 128 * k + 128] = jnp.where(queries == block, 0.0, NEGATIVE)


def layer_call(*inputs):
    shapes = [
        jax.ShapeDtypeStruct((128, 768), LOW),
        jax.ShapeDtypeStruct((8, 3, 16, 768), LOW),
        jax.ShapeDtypeStruct((8, 3, 16, 768), LOW),
        jax.ShapeDtypeStruct((2, 16, 128), WIDE),
        jax.ShapeDtypeStruct((128, 768), LOW),
        jax.ShapeDtypeStruct((3, 128, 768), LOW),
        jax.ShapeDtypeStruct((128, 768), WIDE),
    ]

    def low(*shape):
        return pltpu.VMEM(shape, LOW)

    def wide(*shape):
        return pltpu.VMEM(shape, WIDE)

    scratch = [low(24, 768)] * 8 + [low(24, 3072)] + [low(1, 24)] * 13 + [low(1, 96)]
    scratch += [
        low(128, 768),
        pltpu.VMEM((1, 1024), jnp.int32),
        pltpu.VMEM((1, 1024), jnp.int32),
        low(128, 768),
        wide(128, 768),
        low(12, 2, 2, 4, 48, 768),
        low(2, 2, 4, 2, 96, 768),
        low(2, 2, 4, 2, 16, 128),
        low(256, 768),
        low(384, 768),
        wide(16, 128),
        wide(128, 256),
        wide(128, 384),
        wide(16, 768),
        wide(8, 3072),
        low(128, 768),
        low(256, 768),
        low(256, 768),
        low(6, 256, 256),
        low(128, 768),
        wide(128, 768),
        low(128, 768),
        low(128, 768),
        low(384, 768),
        low(384, 768),
        low(6, 256, 384),
        low(128, 768),
        wide(128, 768),
        low(128, 768),
        low(128, 3072),
        low(128, 3072),
        wide(128, 768),
        wide(128, 768),
        low(128, 768),
        low(128, 768),
        low(128, 768),
        low(384, 768),
        low(384, 768),
        wide(16, 768),
        wide(8, 3072),
        low(12, 2, 4, 2, 3, 16, 768),
        low(4, 2, 4, 2, 3, 16, 768),
        low(4, 2, 3, 16, 768),
        low(8, 2, 4, 3, 16, 768),
        low(8, 4, 3, 16, 768),
        low(8, 2, 3, 16, 768),
        wide(2, 2, 4, 2, 16, 128),
        wide(2, 4, 2, 16, 128),
        wide(2, 4, 16, 128),
        wide(4, 16, 128),
        wide(2, 16, 128),
        low(128, 768),
        low(3, 128, 768),
        pltpu.SemaphoreType.REGULAR,
        pltpu.SemaphoreType.DMA((WIRES,)),
        pltpu.SemaphoreType.DMA((WIRES,)),
        pltpu.SemaphoreType.DMA((44,)),
    ]
    anywhere = pl.BlockSpec(memory_space=pl.ANY)
    return pl.pallas_call(
        layer_kernel,
        out_shape=shapes,
        in_specs=[anywhere] * 29,
        out_specs=[anywhere] * 7,
        scratch_shapes=scratch,
        compiler_params=pltpu.CompilerParams(
            collective_id=0, has_side_effects=True, vmem_limit_bytes=VMEM_BYTES
        ),
    )(*inputs)


def final_kernel(output_low, parts, mine, vparts, left, memory_low, tokens_part, *outs):
    output, tokens_grad, memory_grad = outs[:3]
    squares, inner, outer, smalls = outs[3:11], outs[11], outs[12], outs[13:]
    output[...] = output_low[...]
    b, s = lax.axis_index(BATCH), lax.axis_index(SEQ)
    even = lax.rem(s, 2) == 0
    tokens_grad[...] = tokens_part[...] + left[...].astype(WIDE)
    memory_grad[...] = (
        memory_low[0].astype(WIDE) + memory_low[1].astype(WIDE) + memory_low[2].astype(WIDE)
    )

    def summed(unit):
        total = (
            mine[unit].astype(WIDE) + parts[unit].astype(WIDE)
        )
        return total.reshape(48, 768)

    for unit in range(6):
        total = summed(unit)
        for k in range(2):
            body, rest = total[16 * k : 16 * k + 16], total[32 + 8 * k : 40 + 8 * k]
            matrix = jnp.where(
                even, jnp.concatenate([body, rest], axis=0), jnp.concatenate([rest, body], axis=0)
            )
            m = 2 * unit + k
            if m < 8:
                squares[m][...] = matrix
            else:
                inner[:, 768 * (m - 8) : 768 * (m - 7)] = matrix
    outer[0:48, :] = summed(6)
    outer[48:96, :] = summed(7)
    index = 8 * b + s
    vectors = vparts[0] + vparts[1]
    row = lax.broadcasted_iota(jnp.int32, (16, 128), 0)
    by24 = pltpu.roll(vectors, lax.rem(128 * 24 - 24 * index, 128), 1)
    by96 = pltpu.roll(vectors, lax.rem(128 * 96 - 96 * index, 128), 1)
    small = jnp.where(row == 13, by96, by24)
    for j, ref in enumerate(smalls):
        ref[...] = small[j : j + 1, 0 : ref.shape[1]]


def final_call(*inputs):
    shapes = [
        jax.ShapeDtypeStruct((128, 768), LOW),
        jax.ShapeDtypeStruct((128, 768), WIDE),
        jax.ShapeDtypeStruct((128, 768), WIDE),
    ]
    shapes += [jax.ShapeDtypeStruct((24, 768), WIDE)] * 8
    shapes += [jax.ShapeDtypeStruct((24, 3072), WIDE), jax.ShapeDtypeStruct((96, 768), WIDE)]
    shapes += [jax.ShapeDtypeStruct((1, 24), WIDE)] * 13 + [jax.ShapeDtypeStruct((1, 96), WIDE)]
    return pl.pallas_call(
        final_kernel,
        out_shape=shapes,
        in_specs=[vmem()] * 7,
        out_specs=[vmem()] * 27,
        compiler_params=pltpu.CompilerParams(vmem_limit_bytes=VMEM_BYTES),
    )(*inputs)


def fast_shards(tokens, memory, target_segments, memory_segments, cotangent, *weights):
    squares = weights[0:4] + weights[9:13]
    inner, inner_bias, outer = weights[18:21]
    smalls = list(weights[4:9]) + list(weights[13:18]) + list(weights[21:24]) + [inner_bias]
    results = layer_call(
        *squares,
        inner,
        outer,
        *[small[None] for small in smalls],
        tokens[0],
        memory[0],
        cotangent[0],
        target_segments,
        memory_segments,
    )
    results = final_call(*results)
    output, tokens_grad, memory_grad = results[:3]
    matrices, inner_grad, outer_grad = results[3:11], results[11], results[12]
    vector = [small.reshape(-1) for small in results[13:]]
    return (
        (output[None], tokens_grad[None], memory_grad[None])
        + tuple(matrices[0:4])
        + tuple(vector[0:5])
        + tuple(matrices[4:8])
        + tuple(vector[5:10])
        + (inner_grad, vector[13], outer_grad)
        + tuple(vector[10:13])
    )


def fits(mesh):
    return mesh.shape[BATCH] == 4 and mesh.shape[SEQ] == 8


def solution(mesh):
    in_specs = (
        P(BATCH, SEQ, None),
        P(BATCH, SEQ, None),
        P(BATCH, None),
        P(BATCH, None),
        P(BATCH, SEQ, None),
        P(BOTH, None),
        P(BOTH, None),
        P(BOTH, None),
        P(BOTH, None),
        P(BOTH),
        P(BOTH),
        P(BOTH),
        P(BOTH),
        P(BOTH),
        P(BOTH, None),
        P(BOTH, None),
        P(BOTH, None),
        P(BOTH, None),
        P(BOTH),
        P(BOTH),
        P(BOTH),
        P(BOTH),
        P(BOTH),
        P(BOTH, None),
        P(BOTH),
        P(BOTH, None),
        P(BOTH),
        P(BOTH),
        P(BOTH),
    )
    out_specs = (
        P(BATCH, SEQ, None),
        P(BATCH, SEQ, None),
        P(BATCH, SEQ, None),
        P(BOTH, None),
        P(BOTH, None),
        P(BOTH, None),
        P(BOTH, None),
        P(BOTH),
        P(BOTH),
        P(BOTH),
        P(BOTH),
        P(BOTH),
        P(BOTH, None),
        P(BOTH, None),
        P(BOTH, None),
        P(BOTH, None),
        P(BOTH),
        P(BOTH),
        P(BOTH),
        P(BOTH),
        P(BOTH),
        P(BOTH, None),
        P(BOTH),
        P(BOTH, None),
        P(BOTH),
        P(BOTH),
        P(BOTH),
    )
    quick = fits(mesh)
    return jax.shard_map(fast_shards if quick else shards, mesh=mesh, in_specs=in_specs, out_specs=out_specs, check_vma=False)
```

```python
from functools import partial

import jax
import jax.numpy as jnp
from jax import lax
from jax.experimental import pallas as pl
from jax.experimental.pallas import tpu as pltpu
from jax.sharding import PartitionSpec as P

BATCH, SEQ = ("batch", "seq")
BOTH = (BATCH, SEQ)
HD = 64
SCALE = 0.125
NEGATIVE = -1e30
EPSILON = 1e-05
block_limit = 1024


def spans(total):
    if total > block_limit and total % block_limit == 0:
        return (block_limit, total // block_limit)
    return (total, 1)


def heads_of(matrix):
    return matrix.reshape(matrix.shape[0], -1, HD)


def normalize(values, gain, shift):
    center = values - jnp.mean(values, axis=-1, keepdims=True)
    spread = jnp.mean(center * center, axis=-1, keepdims=True)
    return center * lax.rsqrt(spread + EPSILON) * gain + shift


def norm_back(values, gain, shift, grad):
    _, pullback = jax.vjp(normalize, values, gain, shift)
    return pullback(grad)


def matmul(left, right):
    return jnp.dot(left, right, preferred_element_type=jnp.float32)


def left_product(left, right):
    return lax.dot_general(
        left, right, (((0,), (0,)), ((), ())), preferred_element_type=jnp.float32
    )


def right_product(left, right):
    return lax.dot_general(
        left, right, (((1,), (1,)), ((), ())), preferred_element_type=jnp.float32
    )


def row_total(matrix):
    return jnp.sum(matrix.astype(jnp.float32), axis=0)


def allowed_mask(query_seg, query_pos, key_seg, key_pos, causal):
    same = query_seg[:, None] == key_seg[None, :]
    if causal:
        same = jnp.logical_and(same, key_pos[None, :] <= query_pos[:, None])
    return same


def block_terms(
    query_block, upstream_block, logsum_block, delta_block, allowed, key_block, value_block
):
    scores = (
        jnp.einsum("qhd,khd->hqk", query_block, key_block, preferred_element_type=jnp.float32)
        * SCALE
    )
    scores = jnp.where(allowed[None], scores, NEGATIVE)
    probs = jnp.where(allowed[None], jnp.exp(scores - logsum_block[:, :, None]), 0.0)
    dprobs = jnp.einsum(
        "qhd,khd->hqk", upstream_block, value_block, preferred_element_type=jnp.float32
    )
    dscores = (probs * (dprobs - delta_block[:, :, None]) * SCALE).astype(jnp.bfloat16)
    return (probs.astype(jnp.bfloat16), dscores)


def attend(queries, keys, values, query_seg, query_pos, key_ids, causal):
    row_count = queries.shape[0]
    head_count = queries.shape[1] // HD
    query_heads = heads_of(queries)
    all_keys, all_values = (
        lax.all_gather(keys, SEQ, axis=0, tiled=True),
        lax.all_gather(values, SEQ, axis=0, tiled=True),
    )
    block_rows, block_count = spans(all_keys.shape[0])

    def scored(index):
        offset = index * block_rows
        key_block = heads_of(lax.dynamic_slice_in_dim(all_keys, offset, block_rows, 0))
        key_pos = offset + jnp.arange(block_rows, dtype=jnp.int32)
        key_seg = lax.dynamic_slice_in_dim(key_ids, offset, block_rows, 0)
        allowed = allowed_mask(query_seg, query_pos, key_seg, key_pos, causal)[None]
        scores = (
            jnp.einsum("qhd,khd->hqk", query_heads, key_block, preferred_element_type=jnp.float32)
            * SCALE
        )
        return (jnp.where(allowed, scores, NEGATIVE), allowed)

    def stat_step(index, state):
        run_max, run_sum = state
        scores, allowed = scored(index)
        new_max = jnp.maximum(run_max, jnp.max(scores, axis=2))
        weights = jnp.where(allowed, jnp.exp(scores - new_max[:, :, None]), 0.0)
        run_sum = run_sum * jnp.exp(run_max - new_max) + jnp.sum(weights, axis=2)
        return (new_max, run_sum)

    run_max, run_sum = lax.fori_loop(
        0,
        block_count,
        stat_step,
        (
            jnp.full((head_count, row_count), NEGATIVE, jnp.float32),
            jnp.zeros((head_count, row_count), jnp.float32),
        ),
    )
    logsum = run_max + jnp.log(run_sum)

    def value_step(index, accum):
        scores, allowed = scored(index)
        probs = jnp.where(allowed, jnp.exp(scores - logsum[:, :, None]), 0.0).astype(jnp.bfloat16)
        value_block = heads_of(
            lax.dynamic_slice_in_dim(all_values, index * block_rows, block_rows, 0)
        )
        return accum + jnp.einsum(
            "hqk,khd->qhd", probs, value_block, preferred_element_type=jnp.float32
        )

    accum = lax.fori_loop(
        0, block_count, value_step, jnp.zeros((row_count, head_count, HD), jnp.float32)
    )
    outcome = accum.reshape(row_count, head_count * HD)
    return (outcome, logsum)


def head_delta(upstream, context):
    row_count = upstream.shape[0]
    return jnp.sum((upstream.astype(jnp.float32) * context).reshape(row_count, -1, HD), axis=2).T


def attend_back(queries, keys, values, upstream, logsum, delta, query_ids, key_ids, causal):
    row_count = queries.shape[0]
    head_count = queries.shape[1] // HD
    own_first = lax.axis_index(SEQ) * row_count
    own_pos = own_first + jnp.arange(row_count, dtype=jnp.int32)
    query_seg = lax.dynamic_slice_in_dim(query_ids, own_first, row_count, 0)
    key_seg = lax.dynamic_slice_in_dim(key_ids, own_first, row_count, 0)
    query_heads = heads_of(queries)
    upstream_heads = heads_of(upstream)
    empty = jnp.zeros((row_count, head_count, HD), jnp.float32)
    key_source = lax.all_gather(keys, SEQ, axis=0, tiled=True)
    value_source = lax.all_gather(values, SEQ, axis=0, tiled=True)
    block_rows, block_count = spans(key_source.shape[0])

    def key_step(index, running):
        local = index * block_rows
        key_block = heads_of(lax.dynamic_slice_in_dim(key_source, local, block_rows, 0))
        value_block = heads_of(lax.dynamic_slice_in_dim(value_source, local, block_rows, 0))
        block_seg = lax.dynamic_slice_in_dim(key_ids, local, block_rows, 0)
        block_pos = local + jnp.arange(block_rows, dtype=jnp.int32)
        allowed = allowed_mask(query_seg, own_pos, block_seg, block_pos, causal)
        probs, dscores = block_terms(
            query_heads, upstream_heads, logsum, delta, allowed, key_block, value_block
        )
        return running + jnp.einsum(
            "hqk,khd->qhd", dscores, key_block, preferred_element_type=jnp.float32
        )

    dqueries = lax.fori_loop(0, block_count, key_step, empty)
    all_logsum, all_delta = (
        lax.all_gather(logsum, SEQ, axis=1, tiled=True),
        lax.all_gather(delta, SEQ, axis=1, tiled=True),
    )
    key_heads = heads_of(keys)
    value_heads = heads_of(values)
    piece_queries = lax.all_gather(queries, SEQ, axis=0, tiled=True)
    piece_upstream = lax.all_gather(upstream, SEQ, axis=0, tiled=True)
    query_block_rows, block_count = spans(piece_queries.shape[0])

    def query_step(index, running):
        key_total, value_total = running
        local = index * query_block_rows
        query_block = heads_of(lax.dynamic_slice_in_dim(piece_queries, local, query_block_rows, 0))
        upstream_block = heads_of(
            lax.dynamic_slice_in_dim(piece_upstream, local, query_block_rows, 0)
        )
        logsum_block = lax.dynamic_slice_in_dim(all_logsum, local, query_block_rows, 1)
        delta_block = lax.dynamic_slice_in_dim(all_delta, local, query_block_rows, 1)
        block_seg = lax.dynamic_slice_in_dim(query_ids, local, query_block_rows, 0)
        block_pos = local + jnp.arange(query_block_rows, dtype=jnp.int32)
        allowed = allowed_mask(block_seg, block_pos, key_seg, own_pos, causal)
        probs, dscores = block_terms(
            query_block, upstream_block, logsum_block, delta_block, allowed, key_heads, value_heads
        )
        key_total = key_total + jnp.einsum(
            "hqk,qhd->khd", dscores, query_block, preferred_element_type=jnp.float32
        )
        value_total = value_total + jnp.einsum(
            "hqk,qhd->khd", probs, upstream_block, preferred_element_type=jnp.float32
        )
        return (key_total, value_total)

    key_grad, value_grad = lax.fori_loop(0, block_count, query_step, (empty, empty))
    key_grad = key_grad.reshape(row_count, -1)
    value_grad = value_grad.reshape(row_count, -1)
    return (dqueries.reshape(row_count, -1), key_grad, value_grad)


def shards(
    tokens,
    memory,
    target_segments,
    memory_segments,
    cotangent,
    selfquery,
    selfkey,
    selfvalue,
    selfout,
    selfqbias,
    selfvbias,
    selfobias,
    selfgain,
    selfshift,
    crossquery,
    crosskey,
    crossvalue,
    crossout,
    crossqbias,
    crossvbias,
    crossobias,
    crossgain,
    crossshift,
    innerweight,
    innerbias,
    outerweight,
    outerbias,
    finalgain,
    finalshift,
):
    inputs = tokens[0]
    source = memory[0]
    target_ids = target_segments[0]
    source_ids = memory_segments[0]
    row_count = inputs.shape[0]
    own_first = lax.axis_index(SEQ) * row_count
    own_pos = own_first + jnp.arange(row_count, dtype=jnp.int32)
    query_seg = lax.dynamic_slice_in_dim(target_ids, own_first, row_count, 0)
    (
        query_full,
        key_full,
        value_full,
        out_full,
        qbias_full,
        vbias_full,
        obias_full,
        sgain_full,
        sshift_full,
    ) = (
        lax.all_gather(selfquery, BOTH, axis=0, tiled=True),
        lax.all_gather(selfkey, BOTH, axis=0, tiled=True),
        lax.all_gather(selfvalue, BOTH, axis=0, tiled=True),
        lax.all_gather(selfout, BOTH, axis=0, tiled=True),
        lax.all_gather(selfqbias, BOTH, axis=0, tiled=True),
        lax.all_gather(selfvbias, BOTH, axis=0, tiled=True),
        lax.all_gather(selfobias, BOTH, axis=0, tiled=True),
        lax.all_gather(selfgain, BOTH, axis=0, tiled=True),
        lax.all_gather(selfshift, BOTH, axis=0, tiled=True),
    )
    sgain = sgain_full.astype(jnp.float32)
    sshift = sshift_full.astype(jnp.float32)
    query_self = (matmul(inputs, query_full) + qbias_full.astype(jnp.float32)).astype(jnp.bfloat16)
    key_self = matmul(inputs, key_full).astype(jnp.bfloat16)
    value_self = (matmul(inputs, value_full) + vbias_full.astype(jnp.float32)).astype(jnp.bfloat16)
    attn_self, logsum_self = attend(
        query_self, key_self, value_self, query_seg, own_pos, target_ids, True
    )
    self_low = attn_self.astype(jnp.bfloat16)
    hidden_one = (
        inputs.astype(jnp.float32) + matmul(self_low, out_full) + obias_full.astype(jnp.float32)
    )
    first = normalize(hidden_one, sgain, sshift)
    first_low = first.astype(jnp.bfloat16)
    (
        cquery_full,
        ckey_full,
        cvalue_full,
        cout_full,
        cqbias_full,
        cvbias_full,
        cobias_full,
        cgain_full,
        cshift_full,
    ) = (
        lax.all_gather(crossquery, BOTH, axis=0, tiled=True),
        lax.all_gather(crosskey, BOTH, axis=0, tiled=True),
        lax.all_gather(crossvalue, BOTH, axis=0, tiled=True),
        lax.all_gather(crossout, BOTH, axis=0, tiled=True),
        lax.all_gather(crossqbias, BOTH, axis=0, tiled=True),
        lax.all_gather(crossvbias, BOTH, axis=0, tiled=True),
        lax.all_gather(crossobias, BOTH, axis=0, tiled=True),
        lax.all_gather(crossgain, BOTH, axis=0, tiled=True),
        lax.all_gather(crossshift, BOTH, axis=0, tiled=True),
    )
    cgain = cgain_full.astype(jnp.float32)
    cshift = cshift_full.astype(jnp.float32)
    query_cross = (matmul(first_low, cquery_full) + cqbias_full.astype(jnp.float32)).astype(
        jnp.bfloat16
    )
    key_cross = matmul(source, ckey_full).astype(jnp.bfloat16)
    value_cross = (matmul(source, cvalue_full) + cvbias_full.astype(jnp.float32)).astype(
        jnp.bfloat16
    )
    attn_cross, logsum_cross = attend(
        query_cross, key_cross, value_cross, query_seg, own_pos, source_ids, False
    )
    cross_low = attn_cross.astype(jnp.bfloat16)
    hidden_two = first + matmul(cross_low, cout_full) + cobias_full.astype(jnp.float32)
    second = normalize(hidden_two, cgain, cshift)
    second_low = second.astype(jnp.bfloat16)
    inner_full, ibias_full, outer_full, obias_feed, fgain_full, fshift_full = (
        lax.all_gather(innerweight, BOTH, axis=0, tiled=True),
        lax.all_gather(innerbias, BOTH, axis=0, tiled=True),
        lax.all_gather(outerweight, BOTH, axis=0, tiled=True),
        lax.all_gather(outerbias, BOTH, axis=0, tiled=True),
        lax.all_gather(finalgain, BOTH, axis=0, tiled=True),
        lax.all_gather(finalshift, BOTH, axis=0, tiled=True),
    )
    fgain = fgain_full.astype(jnp.float32)
    fshift = fshift_full.astype(jnp.float32)
    smooth = partial(jax.nn.gelu, approximate=False)
    inner_pre = matmul(second_low, inner_full) + ibias_full.astype(jnp.float32)
    activation = smooth(inner_pre).astype(jnp.bfloat16)
    hidden_three = second + matmul(activation, outer_full) + obias_feed.astype(jnp.float32)
    output = normalize(hidden_three, fgain, fshift).astype(jnp.bfloat16)
    grad_hidden3, grad_fgain, grad_fshift = norm_back(
        hidden_three, fgain, fshift, cotangent[0].astype(jnp.float32)
    )
    branch_grad = grad_hidden3.astype(jnp.bfloat16)
    grad_outer = left_product(activation, branch_grad)
    grad_obias_feed = row_total(branch_grad)
    _, gelu_back = jax.vjp(smooth, inner_pre)
    inner_grad = gelu_back(right_product(branch_grad, outer_full))[0].astype(jnp.bfloat16)
    grad_inner = left_product(second_low, inner_grad)
    grad_ibias = row_total(inner_grad)
    grad_second = grad_hidden3 + right_product(inner_grad, inner_full)
    feed_grads = (
        lax.psum_scatter(grad_inner, BOTH, scatter_dimension=0, tiled=True),
        lax.psum_scatter(grad_ibias, BOTH, scatter_dimension=0, tiled=True),
        lax.psum_scatter(grad_outer, BOTH, scatter_dimension=0, tiled=True),
        lax.psum_scatter(grad_obias_feed, BOTH, scatter_dimension=0, tiled=True),
        lax.psum_scatter(grad_fgain, BOTH, scatter_dimension=0, tiled=True),
        lax.psum_scatter(grad_fshift, BOTH, scatter_dimension=0, tiled=True),
    )
    grad_hidden2, grad_cgain, grad_cshift = norm_back(hidden_two, cgain, cshift, grad_second)
    cross_branch = grad_hidden2.astype(jnp.bfloat16)
    grad_cout = left_product(cross_low, cross_branch)
    grad_cobias = row_total(cross_branch)
    cross_up = right_product(cross_branch, cout_full).astype(jnp.bfloat16)
    cross_delta = head_delta(cross_up, attn_cross)
    cq_grad, ck_grad, cv_grad = attend_back(
        query_cross,
        key_cross,
        value_cross,
        cross_up,
        logsum_cross,
        cross_delta,
        target_ids,
        source_ids,
        False,
    )
    cq_low = cq_grad.astype(jnp.bfloat16)
    ck_low = ck_grad.astype(jnp.bfloat16)
    cv_low = cv_grad.astype(jnp.bfloat16)
    grad_cquery = left_product(first_low, cq_low)
    grad_cqbias = row_total(cq_low)
    grad_ckey = left_product(source, ck_low)
    grad_cvalue = left_product(source, cv_low)
    grad_cvbias = row_total(cv_low)
    memory_grad = right_product(ck_low, ckey_full) + right_product(cv_low, cvalue_full)
    grad_first = grad_hidden2 + right_product(cq_low, cquery_full)
    cross_grads = (
        lax.psum_scatter(grad_cquery, BOTH, scatter_dimension=0, tiled=True),
        lax.psum_scatter(grad_ckey, BOTH, scatter_dimension=0, tiled=True),
        lax.psum_scatter(grad_cvalue, BOTH, scatter_dimension=0, tiled=True),
        lax.psum_scatter(grad_cout, BOTH, scatter_dimension=0, tiled=True),
        lax.psum_scatter(grad_cqbias, BOTH, scatter_dimension=0, tiled=True),
        lax.psum_scatter(grad_cvbias, BOTH, scatter_dimension=0, tiled=True),
        lax.psum_scatter(grad_cobias, BOTH, scatter_dimension=0, tiled=True),
        lax.psum_scatter(grad_cgain, BOTH, scatter_dimension=0, tiled=True),
        lax.psum_scatter(grad_cshift, BOTH, scatter_dimension=0, tiled=True),
    )
    grad_hidden1, grad_sgain, grad_sshift = norm_back(hidden_one, sgain, sshift, grad_first)
    self_branch = grad_hidden1.astype(jnp.bfloat16)
    grad_out = left_product(self_low, self_branch)
    grad_obias = row_total(self_branch)
    self_up = right_product(self_branch, out_full).astype(jnp.bfloat16)
    self_delta = head_delta(self_up, attn_self)
    sq_grad, sk_grad, sv_grad = attend_back(
        query_self,
        key_self,
        value_self,
        self_up,
        logsum_self,
        self_delta,
        target_ids,
        target_ids,
        True,
    )
    sq_low = sq_grad.astype(jnp.bfloat16)
    sk_low = sk_grad.astype(jnp.bfloat16)
    sv_low = sv_grad.astype(jnp.bfloat16)
    grad_query = left_product(inputs, sq_low)
    grad_qbias = row_total(sq_low)
    grad_key = left_product(inputs, sk_low)
    grad_value = left_product(inputs, sv_low)
    grad_vbias = row_total(sv_low)
    tokens_grad = (
        grad_hidden1
        + right_product(sq_low, query_full)
        + right_product(sk_low, key_full)
        + right_product(sv_low, value_full)
    )
    self_grads = (
        lax.psum_scatter(grad_query, BOTH, scatter_dimension=0, tiled=True),
        lax.psum_scatter(grad_key, BOTH, scatter_dimension=0, tiled=True),
        lax.psum_scatter(grad_value, BOTH, scatter_dimension=0, tiled=True),
        lax.psum_scatter(grad_out, BOTH, scatter_dimension=0, tiled=True),
        lax.psum_scatter(grad_qbias, BOTH, scatter_dimension=0, tiled=True),
        lax.psum_scatter(grad_vbias, BOTH, scatter_dimension=0, tiled=True),
        lax.psum_scatter(grad_obias, BOTH, scatter_dimension=0, tiled=True),
        lax.psum_scatter(grad_sgain, BOTH, scatter_dimension=0, tiled=True),
        lax.psum_scatter(grad_sshift, BOTH, scatter_dimension=0, tiled=True),
    )
    return (
        (output[None], tokens_grad[None], memory_grad[None])
        + tuple(self_grads)
        + tuple(cross_grads)
        + tuple(feed_grads)
    )


LOW = jnp.bfloat16
WIDE = jnp.float32
MESH = pl.DeviceIdType.MESH
VMEM_BYTES = 64 << 20
WIRES = 192
ALL2 = pl.ds(0, 2)
ALL3 = pl.ds(0, 3)
ALL4 = pl.ds(0, 4)
ALL16 = pl.ds(0, 16)
ALL768 = pl.ds(0, 768)
SHARED = (2, 3, 4, 5)


def shares(unit):
    cut = 384 if unit in SHARED else 512
    return (pl.ds(0, cut), pl.ds(cut, 768 - cut))


def place():
    b, s = lax.axis_index(BATCH), lax.axis_index(SEQ)
    return (lax.div(b, 2), lax.rem(b, 2), lax.rem(s, 2), lax.div(s, 2))


def device(x, c, y, z):
    return (2 * x + c, 2 * z + y)


FORWARD = (
    0, "prepare", 10, 1, 20, 11, 2, 30, 21, 12, 3, "tokens", 40, 31, 22, 13, 4, 50, "memory", 41,
    32, 23, 14, 60, 51, 42, 33, 24, 70, 61, 52, 43, 34, 25, "self", 71, 62, 53, 44, 35, 72,
    "project", 63, "cross", 54, 45, 73, 55, "feed1", "feed2", 64, 74,
)
BACKWARD = (
    "slopes", 60, 70, "inner4", 61, 40, "inner5", 50, 41, 51, 71, "inner", "norm2", "cross",
    "grads2", 20, 30, 42, 52, 62, 72, "inputs2", "norm1", 21, 31, "home", "self", "grads1", 0, 10,
    22, 32, "v", "vy", "inputs1", 63, 73, 1, 11, 43, 53, "vx", 23, 33, 44, 54, "vp", 24, 2, 34,
    "vm", 12, 3, 13,
)


class Peers:
    def __init__(self):
        self.x, self.c, self.y, self.z = place()
        x, c, y, z = self.x, self.c, self.y, self.z
        b, s = lax.axis_index(BATCH), lax.axis_index(SEQ)
        self.across_x = device(1 - x, c, y, z)
        self.across_y = device(x, c, 1 - y, z)
        self.sibling = device(x, 1 - c, y, z)
        odd = lax.rem(z, 2)
        self.twin = z + 1 - 2 * odd
        self.share_z = pl.ds(2 * odd, 2)
        self.twin_share_z = pl.ds(2 - 2 * odd, 2)
        self.across_z = device(x, c, y, 3 - z)
        self.beside_z = device(x, c, y, self.twin)
        self.s = s
        self.after = (b, lax.rem(s + 1, 8))
        self.before = (b, lax.rem(s + 7, 8))
        self.mirror = (b, 7 - s)
        self.folds = [(b, lax.rem(14 - s, 8)), (b, lax.rem(16 - s, 8))]
        self.alone = [self.folds[k][1] == s for k in range(2)]

    def greet(self):
        barrier = pltpu.get_barrier_semaphore()
        always = [
            self.across_x, self.across_y, self.across_z, self.beside_z, self.sibling, self.after, self.before, self.mirror,
        ]
        for peer in always:
            pl.semaphore_signal(barrier, inc=1, device_id=peer, device_id_type=MESH)
        for peer, alone in zip(self.folds, self.alone):
            @pl.when(jnp.logical_not(alone))
            def _():
                pl.semaphore_signal(barrier, inc=1, device_id=peer, device_id_type=MESH)

    def meet(self):
        barrier = pltpu.get_barrier_semaphore()
        others = [jnp.where(alone, 0, 1) for alone in self.alone]
        pl.semaphore_wait(barrier, 8 + others[0] + others[1])


class Wires:
    def __init__(self, send, recv):
        self.send, self.recv, self.used = send, recv, 0

    def copies(self, pairs, target):
        made = []
        assert self.used + len(pairs) <= WIRES
        for source, landing in pairs:
            made.append(
                pltpu.make_async_remote_copy(
                    src_ref=source,
                    dst_ref=landing,
                    send_sem=self.send.at[self.used],
                    recv_sem=self.recv.at[self.used],
                    device_id=target,
                    device_id_type=MESH,
                )
            )
            self.used += 1
        return made


def start(copies):
    for copy in copies:
        copy.start()


def landed(copies):
    for copy in copies:
        copy.wait_recv()


def sent(copies):
    for copy in copies:
        copy.wait_send()


class Gather:
    def __init__(self, peers, wires, held, outer, vectors):
        self.peers, self.wires = peers, wires
        self.held, self.outer, self.vectors = held, outer, vectors
        self.steps = [{} for _ in range(8)]

    def parts(self, unit, x, c, z, y, columns=ALL768):
        both = y is None
        if unit >= 6:
            rows = pl.ds(48 * (unit - 6), 48)
            return [self.outer.at[x, c, z, ALL2 if both else y, rows, columns]]
        refs = [self.held.at[2 * unit + c, x, z, ALL2 if both else y, ALL3, ALL16, columns]]
        if unit == 0 and columns.start == 0:
            refs.append(self.vectors.at[x, c, z, ALL2 if both else y])
        return refs

    def send(self, unit, k, routes):
        made = []
        for target, spot in routes:
            pairs = [(part, part) for part in self.parts(unit, *spot)]
            made += self.wires.copies(pairs, target)
        start(made)
        self.steps[unit][k] = made

    def hop(self, unit, k):
        p = self.peers
        x, c, y, z = p.x, p.c, p.y, p.z
        if k > 0:
            landed(self.steps[unit][k - 1])
        if k == 0:
            self.send(unit, 0, [(p.across_z, (x, c, z, y))])
        elif k == 1:
            self.send(unit, 1, [(p.beside_z, (x, c, z, y)), (p.beside_z, (x, c, 3 - z, y))])
        elif k == 2:
            column = (x, c, ALL4, y)
            self.send(unit, 2, [(p.across_x, column), (p.across_y, column)])
        elif k == 3:
            over_x, over_y = shares(unit)
            depth = p.share_z if unit in SHARED else ALL4
            routes = [(p.across_x, (x, c, depth, 1 - y, over_x))]
            routes += [(p.across_y, (1 - x, c, depth, y, over_y))]
            self.send(unit, 3, routes)
            self.send(unit, 6, [(p.sibling, (x, c, ALL4, None)), (p.sibling, (1 - x, c, ALL4, y))])
        elif k == 4 and unit in SHARED:
            self.send(unit, 4, [(p.beside_z, (1 - x, c, p.share_z, 1 - y))])
        else:
            self.send(unit, 5, [(p.sibling, (1 - x, c, ALL4, 1 - y))])

    def last(self, unit):
        landed(self.steps[unit][5])
        landed(self.steps[unit][6])

    def close(self, units):
        for unit in units:
            for copies in self.steps[unit].values():
                sent(copies)


def gather_pack(unit, peers, squares, inner, held):
    x, c, y, z = peers.x, peers.c, peers.y, peers.z
    rests = []
    for k in range(2):
        m = 2 * unit + k
        values = squares[m][...] if m < 8 else inner[:, 768 * (m - 8) : 768 * (m - 7)]
        values = values.astype(WIDE)
        body = jnp.where(y == 0, values[0:16], values[8:24])
        rests.append(jnp.where(y == 0, values[16:24], values[0:8]))
        held[2 * unit + c, x, z, y, k] = body.astype(LOW)
    held[2 * unit + c, x, z, y, 2] = jnp.concatenate(rests, axis=0).astype(LOW)


def gather_vectors(peers, smalls, board, vectors):
    board[...] = jnp.zeros((16, 128), WIDE)
    for j, small in enumerate(smalls):
        board[j : j + 1, 0 : small.shape[1]] = small[...].astype(WIDE)
    index = (2 * peers.x + peers.c) * 8 + peers.s
    wide = board[...]
    row = lax.broadcasted_iota(jnp.int32, (16, 128), 0)
    by24 = pltpu.roll(wide, lax.rem(24 * index, 128), 1)
    by96 = pltpu.roll(wide, lax.rem(96 * index, 128), 1)
    rolled = jnp.where(row == 13, by96, by24).astype(LOW)
    vectors[peers.x, peers.c, peers.z, peers.y] = rolled


def assemble(unit, held, mats):
    def one(step, carry):
        x, c, z = lax.div(step, 8), lax.rem(lax.div(step, 4), 2), lax.rem(step, 4)
        low_half = held[2 * unit + c, x, z, 0, 2].astype(WIDE)
        high_half = held[2 * unit + c, x, z, 1, 2].astype(WIDE)
        for k in range(2):
            part = slice(8 * k, 8 * k + 8)
            middle = jnp.concatenate([low_half[part], high_half[part]], axis=0)
            mats[2 * unit + k, x, c, z, 0:16, :] = held[2 * unit + c, x, z, 0, k]
            mats[2 * unit + k, x, c, z, 16:32, :] = middle.astype(LOW)
            mats[2 * unit + k, x, c, z, 32:48, :] = held[2 * unit + c, x, z, 1, k]
        return carry

    lax.fori_loop(0, 16, one, 0)


def vmem():
    return pl.BlockSpec(memory_space=pltpu.VMEM)


def dot(left, right):
    return jnp.dot(left, right, preferred_element_type=WIDE)


def dot_nt(left, right):
    return lax.dot_general(left, right, (((1,), (1,)), ((), ())), preferred_element_type=WIDE)


def dot_tn(left, right):
    return lax.dot_general(left, right, (((0,), (0,)), ((), ())), preferred_element_type=WIDE)


def strip(n):
    return slice(256 * n, 256 * n + 256)


def columns(mats, m, n):
    return mats[m, :, :, :, :, strip(n)].reshape(768, 256)


def rows(mats, m, x):
    return mats[m, x].reshape(384, 768)


def outer_columns(outer, j, n):
    return outer[j // 2, j % 2, :, :, :, strip(n)].reshape(768, 256)


def outer_rows(outer, j, half):
    return outer[j // 2, j % 2, 2 * half : 2 * half + 2].reshape(384, 768)


def unpack_vectors(vectors, vec, inner_bias):
    lane = lax.broadcasted_iota(jnp.int32, (16, 128), 1)

    def shard(d):
        b, s = d // 8, d % 8
        return vectors[b // 2, b % 2, s // 2, s % 2].astype(WIDE)

    for width, tiles, ref in ((24, 6, vec), (96, 24, inner_bias)):
        for t in range(tiles):
            first = (128 * t) // width
            final = (128 * t + 127) // width
            total = shard(first)
            for d in range(first + 1, final + 1):
                total = jnp.where(lane >= width * d - 128 * t, shard(d), total)
            if width == 24:
                ref[:, 128 * t : 128 * t + 128] = total
            else:
                ref[0:1, 128 * t : 128 * t + 128] = total[13:14]


def pack_vectors(vec, inner_bias, c, place_at):
    lane = lax.broadcasted_iota(jnp.int32, (16, 128), 1)
    row = lax.broadcasted_iota(jnp.int32, (16, 128), 0)

    def shard(ref, width, d):
        t, offset = width * d // 128, width * d % 128
        block = ref[:, 128 * t : 128 * t + 128]
        if offset + width > 128:
            block = jnp.where(lane >= offset, block, ref[:, 128 * t + 128 : 128 * t + 256])
        return block

    for d in range(32):
        b, s = d // 8, d % 8
        block = shard(vec, 24, d)
        t, offset = 96 * d // 128, 96 * d % 128
        bias = inner_bias[0:1, 128 * t : 128 * t + 128]
        if offset + 96 > 128:
            bias = jnp.where(lane[0:1] >= offset, bias, inner_bias[0:1, 128 * t + 128 : 128 * t + 256])
        place_at(b % 2, b // 2, s // 2, s % 2, jnp.where(row == 13, jnp.broadcast_to(bias, (16, 128)), block))


def centered(values):
    center = values - jnp.mean(values, axis=-1, keepdims=True)
    scale = lax.rsqrt(jnp.mean(center * center, axis=-1, keepdims=True) + EPSILON)
    return (center * scale, scale)


def norm_grad(unit_values, scale, gain, grad):
    scaled = grad * gain
    mean = jnp.mean(scaled, axis=-1, keepdims=True)
    along = jnp.mean(scaled * unit_values, axis=-1, keepdims=True)
    return (scaled - mean - unit_values * along) * scale


def total_rows(values):
    return jnp.sum(values.astype(WIDE), axis=0, keepdims=True)


def lane_halves():
    lane = lax.broadcasted_iota(jnp.int32, (128, 128), 1)
    low_half = jnp.where(lane < 64, 1.0, 0.0).astype(LOW)
    high_half = jnp.where(lane < 64, 0.0, 1.0).astype(LOW)
    return (lane < 64, low_half, high_half)


def pair_rows(block, low_half, high_half):
    return jnp.concatenate([block * low_half, block * high_half], axis=0)


def attention(queries, keys, values, mask, probs, context):
    pick, low_half, high_half = lane_halves()

    def heads(h, carry):
        here = pl.ds(pl.multiple_of(128 * h, 128), 128)
        both = pair_rows(queries[:, here], low_half, high_half)
        bias = mask[...]
        scores = dot_nt(both, keys[:, here]) * SCALE + jnp.concatenate([bias, bias], axis=0)
        weights = jnp.exp(scores - jnp.max(scores, axis=1, keepdims=True))
        weights = weights * (1.0 / jnp.sum(weights, axis=1, keepdims=True))
        rounded = weights.astype(LOW)
        probs[h] = rounded
        mixed = dot(rounded, values[:, here])
        context[:, here] = jnp.where(pick, mixed[:128], mixed[128:]).astype(LOW)
        return carry

    lax.fori_loop(0, 6, heads, 0)


def attention_back(queries, keys, values, upstream, probs, dqueries, dkeys, dvalues, count):
    pick, low_half, high_half = lane_halves()

    def heads(h, carry):
        here = pl.ds(pl.multiple_of(128 * h, 128), 128)
        both = pair_rows(queries[:, here], low_half, high_half)
        both_up = pair_rows(upstream[:, here], low_half, high_half)
        dprobs = dot_nt(both_up, values[:, here])
        weights = probs[h].astype(WIDE)
        delta = jnp.sum(weights * dprobs, axis=1, keepdims=True)
        dscores = (weights * (dprobs - delta) * SCALE).astype(LOW)
        mixed = dot(dscores, keys[:, here])
        dqueries[:, here] = jnp.where(pick, mixed[:128], mixed[128:]).astype(LOW)
        dkeys[0:count, here] = dot_tn(dscores, both).astype(LOW)
        dvalues[0:count, here] = dot_tn(probs[h], both_up).astype(LOW)
        return carry

    lax.fori_loop(0, 6, heads, 0)


class Grads:
    ORDER = (6, 7, 4, 5, 2, 3, 0, 1)

    def __init__(self, peers, wires, held, r0, shared, pool, r2, r3, out, mine, credit, move):
        self.peers, self.wires, self.held = peers, wires, held
        self.r0, self.pool, self.r2, self.r3, self.out = r0, pool, r2, r3, out
        self.shared, self.mine, self.credit, self.move = shared, mine, credit, move
        self.kept = []
        self.stage = {}
        self.open = []
        self.first_sends = {}

    def at(self, unit):
        return self.ORDER.index(unit)

    def slot(self, unit, c):
        return jnp.where(c == self.peers.c, unit, 8 + self.at(unit) % 4)

    def ready(self, unit):
        turn = self.at(unit)
        if turn >= 4:
            sent(self.first_sends.pop(self.ORDER[turn - 4]))

    def ship(self, pairs, target):
        copies = self.wires.copies(pairs, target)
        start(copies)
        self.open += copies
        return copies

    def step0(self, unit):
        turn = self.at(unit)
        if turn >= 4:
            pl.semaphore_wait(self.credit, 1)
        ring = turn % 4
        copies = self.wires.copies([(self.held.at[8 + ring], self.r0.at[ring])], self.peers.sibling)
        start(copies)
        self.first_sends[unit] = copies
        self.stage[unit] = copies

    def corner(self, unit, depth):
        p, landing = self.peers, self.r2.at[unit, pl.ds(0, depth.size)]
        self.stage[unit] = []
        for columns, target in zip(shares(unit), (p.across_x, p.across_y)):
            source = self.held.at[unit, 1 - p.x, depth, 1 - p.y, ALL3, ALL16, columns]
            self.stage[unit] += self.ship([(source, landing.at[:, :, :, columns])], target)

    def hop(self, unit, k):
        p, held = self.peers, self.held
        x, y, z = p.x, p.y, p.z
        landed(self.stage[unit])
        if k == 0:
            turn = self.at(unit)
            ring = turn % 4

            def add(i, carry):
                j, d = lax.div(i, 4), lax.rem(i, 4)
                held[unit, j, d] = held[unit, j, d] + self.r0[ring, j, d]
                return carry

            lax.fori_loop(0, 8, add, 0)
            if turn < 4:
                pl.semaphore_signal(self.credit, inc=1, device_id=p.sibling, device_id_type=MESH)
            if unit in SHARED:
                pairs = [(held.at[unit, 1 - x, p.twin_share_z, 1 - y], self.shared.at[unit - SHARED[0]])]
                self.stage[unit] = self.ship(pairs, p.beside_z)
            else:
                self.corner(unit, ALL4)
        elif k == 0.5:
            for i in range(2):
                d = p.share_z.start + i
                block = held[unit, 1 - x, d, 1 - y] + self.shared[unit - SHARED[0], i]
                held[unit, 1 - x, d, 1 - y] = block
            self.corner(unit, p.share_z)
        elif k == 1:
            over_x, over_y = shares(unit)
            depth = p.share_z if unit in SHARED else ALL4
            for i in range(depth.size):
                d = depth.start + i
                here = (unit, x, d, 1 - y, ALL3, ALL16, over_x)
                held[here] = held[here] + self.r2[unit, i, :, :, over_x]
                here = (unit, 1 - x, d, y, ALL3, ALL16, over_y)
                held[here] = held[here] + self.r2[unit, i, :, :, over_y]
            pairs = [(held.at[unit, 1 - x, ALL4, y], self.pool.at[unit, 0])]
            self.stage[unit] = self.ship(pairs, p.across_x)
            pairs = [(held.at[unit, x, ALL4, 1 - y], self.pool.at[unit, 1])]
            self.stage[unit] += self.ship(pairs, p.across_y)
        elif k == 2:
            for d in range(4):
                total = held[unit, x, d, y].astype(WIDE) + self.pool[unit, 0, d].astype(WIDE)
                held[unit, x, d, y] = (total + self.pool[unit, 1, d].astype(WIDE)).astype(LOW)
            pairs = [(held.at[unit, x, d, y], self.r3.at[unit, i]) for i, d in enumerate((p.twin, 3 - p.twin))]
            self.stage[unit] = self.ship(pairs, p.beside_z)
        else:
            for i, d in enumerate((z, 3 - z)):
                held[unit, x, d, y] = held[unit, x, d, y] + self.r3[unit, i]
            pairs = [(held.at[unit, x, 3 - z, y], self.out.at[unit])]
            self.stage[unit] = self.ship(pairs, p.across_z)
            self.kept.append(self.move(held.at[unit, x, z, y], self.mine.at[unit]))
            start(self.kept[-1:])

    def finish(self):
        for unit in self.ORDER:
            landed(self.stage[unit])
        for copies in self.first_sends.values():
            sent(copies)
        sent(self.open)
        for copy in self.kept:
            copy.wait()

    def pair_grad(self, unit, first_left, first_right, second_left, second_right):
        self.ready(unit)
        for x in range(2):
            here = slice(384 * x, 384 * x + 384)
            one_left = jnp.transpose(first_left[:, here])
            two_left = jnp.transpose(second_left[:, here])
            for n in range(3):
                s = strip(n)
                one = dot(one_left, first_right[:, s])
                two = dot(two_left, second_right[:, s])
                for c in range(2):
                    slot = self.slot(unit, c)
                    for z in range(4):
                        for y in range(2):
                            base = 24 * (8 * c + 2 * z + y)
                            body = base + 8 * y
                            rest = base + 16 * (1 - y)
                            self.held[slot, x, z, y, 0, :, s] = one[body : body + 16].astype(LOW)
                            self.held[slot, x, z, y, 1, :, s] = two[body : body + 16].astype(LOW)
                            self.held[slot, x, z, y, 2, :, s] = jnp.concatenate(
                                [one[rest : rest + 8], two[rest : rest + 8]], axis=0
                            ).astype(LOW)

    def outer_grad(self, hidden, upstream):
        for j in range(4):
            x, c = j // 2, j % 2
            for half in range(2):
                here = slice(768 * j + 384 * half, 768 * j + 384 * half + 384)
                left = jnp.transpose(hidden[:, here])
                for n in range(3):
                    s = strip(n)
                    one = dot(left, upstream[:, s])
                    for unit in (6, 7):
                        slot = self.slot(unit, c)
                        for k in range(4):
                            base = 96 * k + 48 * (unit - 6)
                            z, y = 2 * half + k // 2, k % 2
                            block = one[base : base + 48].reshape(3, 16, 256)
                            self.held[slot, x, z, y, :, :, s] = block.astype(LOW)


def layer_kernel(*refs):
    squares_in, inner_in, outer_in, smalls_in = refs[0:8], refs[8], refs[9], refs[10:24]
    tokens_in, memory_in, cotangent_in, target_in, source_in = refs[24:29]
    output, out, mine, vout, left_out, memory_out, tokens_part = refs[29:36]
    squares, inner_own, smalls, refs = refs[36:44], refs[44], refs[45:59], refs[59:]
    (
        cotangent, target_ids, source_ids, output_low, tokens_sum,
        mats, outer, vectors, tokens, memory, board, mask_self, mask_cross,
        vec, inner_bias, query, key, value, probs, context, unit1, first_low,
        query2, key2, value2, probs2, context2, unit2, second_low,
        hidden, slope, total, grad, branch, upstream, dquery, dkey, dvalue,
        gvec, ginner,
        held, r0, shared, pool, r2, r3, vheld, v0, v1, v2, v3, left_part, memory_parts,
        credit, send, recv, local,
    ) = refs
    peers = Peers()
    peers.greet()
    c, x, y, z = peers.c, peers.x, peers.y, peers.z
    wires = Wires(send, recv)
    weights = Gather(peers, wires, held, outer, vectors)
    moves = []

    def move(source, target):
        copy = pltpu.make_async_copy(source, target, local.at[len(moves)])
        moves.append(copy)
        return copy

    grads = Grads(peers, wires, held, r0, shared, pool, r2, r3, out, mine, credit, move)
    own = slice(128, 256)
    early = [move(a, b) for a, b in zip(squares_in[0:2], squares[0:2])]
    early += [move(a, b) for a, b in zip(smalls_in, smalls)]
    loads = [move(a, b) for a, b in zip(squares_in[2:], squares[2:])]
    loads += [move(inner_in, inner_own), move(outer_in, outer.at[x, c, z, y])]
    loads += [move(target_in, target_ids), move(source_in, source_ids)]
    loads += [move(tokens_in, tokens.at[pl.ds(128, 128)]), move(cotangent_in, cotangent)]
    start(early + loads)
    state = {}

    def reduce_hop(unit, k):
        grads.hop(unit, (0, 0.5, 1, 2, 3)[k] if unit in SHARED else k)

    def follow(plan, hop, chunks):
        for step in plan:
            if step in chunks:
                chunks[step]()
            else:
                hop(step // 10, step % 10)

    def vector(j):
        return vec[j : j + 1, :]

    def pack(unit):
        gather_pack(unit, peers, squares, inner_own, held)

    def arrive(*units):
        for unit in units:
            weights.last(unit)
            if unit < 6:
                assemble(unit, held, mats)

    left = wires.copies([(tokens_in, tokens.at[pl.ds(0, 128)])], peers.after)
    mirrored = wires.copies([(memory_in, memory.at[pl.ds(128, 128)])], peers.mirror)
    folds = [
        wires.copies([(memory_in, memory.at[pl.ds(256 * k, 128)])], peers.folds[k]) for k in range(2)
    ]
    kept = [move(memory_in, memory.at[pl.ds(256 * k, 128)]) for k in range(2)]

    def prepare():
        for copy in loads:
            copy.wait()
        for unit in range(1, 6):
            pack(unit)
        fill_masks(peers, target_ids, source_ids, mask_self, mask_cross)

    def exchange_tokens():
        start(left)

    def exchange_memory():
        start(mirrored)
        for k in range(2):
            @pl.when(jnp.logical_not(peers.alone[k]))
            def _():
                start(folds[k])

            @pl.when(peers.alone[k])
            def _():
                kept[k].start()

    def self_attention():
        arrive(0, 1)
        unpack_vectors(vectors, vec, inner_bias)
        landed(left)
        for n in range(3):
            s = strip(n)
            query[:, s] = (dot(tokens[own, :], columns(mats, 0, n)) + vec[0:1, s]).astype(LOW)
            key[:, s] = dot(tokens[...], columns(mats, 1, n)).astype(LOW)
            value[:, s] = (dot(tokens[...], columns(mats, 2, n)) + vec[1:2, s]).astype(LOW)
        attention(query, key, value, mask_self, probs, context)
        for n in range(3):
            s = strip(n)
            total[:, s] = (
                tokens[own, s].astype(WIDE) + dot(context[...], columns(mats, 3, n)) + vec[2:3, s]
            )
        unit, state[1] = centered(total[...])
        unit1[...] = unit
        first = unit * vector(3) + vector(4)
        total[...] = first
        first_low[...] = first.astype(LOW)

    def cross_projections():
        arrive(2, 3)
        for n in range(3):
            s = strip(n)
            query2[:, s] = (dot(first_low[...], columns(mats, 4, n)) + vec[5:6, s]).astype(LOW)
        landed(mirrored)
        for k in range(2):
            @pl.when(jnp.logical_not(peers.alone[k]))
            def _():
                landed(folds[k])
                sent(folds[k])

            @pl.when(peers.alone[k])
            def _():
                kept[k].wait()

        for n in range(3):
            s = strip(n)
            key2[:, s] = dot(memory[...], columns(mats, 5, n)).astype(LOW)
            value2[:, s] = (dot(memory[...], columns(mats, 6, n)) + vec[6:7, s]).astype(LOW)

    def cross_attention():
        attention(query2, key2, value2, mask_cross, probs2, context2)
        for n in range(3):
            s = strip(n)
            total[:, s] = total[:, s] + dot(context2[...], columns(mats, 7, n)) + vec[7:8, s]
        unit, state[2] = centered(total[...])
        unit2[...] = unit
        second = unit * vector(8) + vector(9)
        total[...] = second + vector(10)
        second_low[...] = second.astype(LOW)

    def feed(j):
        for n in range(3):
            s = slice(768 * j + 256 * n, 768 * j + 256 * n + 256)
            pre = dot(second_low[...], columns(mats, 8 + j, n)) + inner_bias[0:1, s]
            normal = 0.5 + 0.5 * lax.erf(pre * 0.7071067811865476)
            hidden[:, s] = (pre * normal).astype(LOW)
            slope[:, s] = (
                normal + pre * (0.3989422804014327 * jnp.exp(-0.5 * pre * pre))
            ).astype(LOW)

    def feed_one():
        arrive(4)
        feed(0)
        feed(1)

    def feed_two():
        arrive(5)
        feed(2)
        feed(3)
        weights.close(range(6))

    forward = {
        "prepare": prepare,
        "tokens": exchange_tokens,
        "memory": exchange_memory,
        "self": self_attention,
        "project": cross_projections,
        "cross": cross_attention,
        "feed1": feed_one,
        "feed2": feed_two,
    }
    for copy in early:
        copy.wait()
    pack(0)
    gather_vectors(peers, smalls, board, vectors)
    peers.meet()
    follow(FORWARD, weights.hop, forward)
    arrive(6, 7)
    for n in range(3):
        s = strip(n)
        summed = total[:, s]
        for j in range(4):
            here = slice(768 * j, 768 * j + 768)
            summed = summed + dot(hidden[:, here], outer_columns(outer, j, n))
        total[:, s] = summed
    unit, scale3 = centered(total[...])
    arrived = cotangent[...].astype(WIDE)
    dhidden = norm_grad(unit, scale3, vector(11), arrived)
    grad[...] = dhidden
    branch[...] = dhidden.astype(LOW)
    grads.outer_grad(hidden, branch)
    grads.step0(6)
    grads.step0(7)
    output_low[...] = (unit * vector(11) + vector(12)).astype(LOW)
    ends = [move(output_low, output)]
    start(ends)
    gvec[11:12, :] = total_rows(arrived * unit)
    gvec[12:13, :] = total_rows(arrived)
    gvec[10:11, :] = total_rows(branch[...])
    weights.close(range(6, 8))
    sent(left + mirrored)

    def slopes():
        for j in range(4):
            for half in range(2):
                s = slice(768 * j + 384 * half, 768 * j + 384 * half + 384)
                raised = dot_nt(branch[...], outer_rows(outer, j, half)) * slope[:, s].astype(WIDE)
                raised = raised.astype(LOW)
                slope[:, s] = raised
                ginner[0:1, s] = total_rows(raised)

    def inner_grad(unit):
        one, two = [slope.at[:, pl.ds(768 * j, 768)] for j in (2 * unit - 8, 2 * unit - 7)]
        grads.pair_grad(unit, second_low, one, second_low, two)
        grads.step0(unit)

    def inner_back():
        for x in range(2):
            s = slice(384 * x, 384 * x + 384)
            summed = grad[:, s]
            for j in range(4):
                summed = summed + dot_nt(slope[:, 768 * j : 768 * j + 768], rows(mats, 8 + j, x))
            grad[:, s] = summed

    def norm_back_at(held_unit, scale, gain, gain_row):
        arrived = grad[...]
        unit = held_unit[...]
        gvec[gain_row : gain_row + 1, :] = total_rows(arrived * unit)
        gvec[gain_row + 1 : gain_row + 2, :] = total_rows(arrived)
        dhidden = norm_grad(unit, scale, gain, arrived)
        grad[...] = dhidden
        branch[...] = dhidden.astype(LOW)
        gvec[gain_row - 1 : gain_row, :] = total_rows(branch[...])

    def cross_norm():
        norm_back_at(unit2, state[2], vector(8), 8)
        for x in range(2):
            upstream[:, 384 * x : 384 * x + 384] = dot_nt(branch[...], rows(mats, 7, x)).astype(LOW)

    def cross_back():
        attention_back(query2, key2, value2, upstream, probs2, dquery, dkey, dvalue, 384)

    def cross_grads():
        grads.pair_grad(2, first_low, dquery, memory, dkey)
        grads.step0(2)
        grads.pair_grad(3, memory, dvalue, context2, branch)
        grads.step0(3)

    def cross_inputs():
        gvec[5:6, :] = total_rows(dquery[...])
        gvec[6:7, :] = total_rows(dvalue[...])
        for x in range(2):
            s = slice(384 * x, 384 * x + 384)
            grad[:, s] = grad[:, s] + dot_nt(dquery[...], rows(mats, 4, x))
            backed = dot_nt(dkey[...], rows(mats, 5, x)) + dot_nt(dvalue[...], rows(mats, 6, x))
            for block in range(3):
                memory_parts[block, :, s] = backed[128 * block : 128 * block + 128].astype(LOW)

    back = [
        wires.copies([(memory_parts.at[2 * k], memory_out.at[2 * k])], peers.folds[k]) for k in range(2)
    ]
    stay = [
        move(memory_parts.at[2 * k], memory_out.at[2 * k]) for k in range(2)
    ]

    def memory_home():
        state["home"] = grads.ship([(memory_parts.at[1], memory_out.at[1])], peers.mirror)
        for k in range(2):
            @pl.when(jnp.logical_not(peers.alone[k]))
            def _():
                start(back[k])

            @pl.when(peers.alone[k])
            def _():
                stay[k].start()

    def self_norm():
        norm_back_at(unit1, state[1], vector(3), 3)
        for x in range(2):
            upstream[:, 384 * x : 384 * x + 384] = dot_nt(branch[...], rows(mats, 3, x)).astype(LOW)

    dkey_two, dvalue_two = dkey.at[pl.ds(0, 256)], dvalue.at[pl.ds(0, 256)]

    def self_back():
        attention_back(query, key, value, upstream, probs, dquery, dkey, dvalue, 256)

    def self_grads():
        grads.pair_grad(0, tokens.at[pl.ds(128, 128)], dquery, tokens, dkey_two)
        grads.step0(0)
        grads.pair_grad(1, tokens, dvalue_two, context, branch)
        grads.step0(1)

    def vectors_near():
        gvec[0:1, :] = total_rows(dquery[...])
        gvec[1:2, :] = total_rows(dvalue_two[...])
        gvec[13:16, :] = jnp.zeros((3, 768), WIDE)

        def put(c, x, z, y, block):
            vheld[c, x, z, y] = block

        pack_vectors(gvec, ginner, peers.c, put)
        state["v"] = grads.ship([(vheld.at[1 - c], v0)], peers.sibling)

    def vectors_y():
        landed(state["v"])
        vheld[c] = vheld[c] + v0[...]
        state["v"] = grads.ship([(vheld.at[c, ALL2, ALL4, 1 - y], v1)], peers.across_y)

    def vectors_x():
        landed(state["v"])
        for j in range(2):
            for k in range(4):
                vheld[c, j, k, y] = vheld[c, j, k, y] + v1[j, k]
        state["v"] = grads.ship([(vheld.at[c, 1 - x, ALL4, y], v2)], peers.across_x)

    def vectors_p():
        landed(state["v"])
        for k in range(4):
            vheld[c, x, k, y] = vheld[c, x, k, y] + v2[k]
        twin = peers.twin
        pairs = [(vheld.at[c, x, twin, y], v3.at[0]), (vheld.at[c, x, 3 - twin, y], v3.at[1])]
        state["v"] = grads.ship(pairs, peers.beside_z)

    def vectors_m():
        landed(state["v"])
        vheld[c, x, z, y] = vheld[c, x, z, y] + v3[0]
        vheld[c, x, 3 - z, y] = vheld[c, x, 3 - z, y] + v3[1]
        state["v"] = grads.ship([(vheld.at[c, x, 3 - z, y], vout.at[1])], peers.across_z)
        ends.append(move(vheld.at[c, x, z, y], vout.at[0]))
        start(ends[-1:])

    def self_inputs():
        for k in range(2):
            s = slice(384 * k, 384 * k + 384)
            backed = dot_nt(dkey_two[...], rows(mats, 1, k)) + dot_nt(dvalue_two[...], rows(mats, 2, k))
            left_part[:, s] = backed[0:128].astype(LOW)
            tokens_sum[:, s] = grad[:, s] + dot_nt(dquery[...], rows(mats, 0, k)) + backed[128:256]
        ends.append(move(tokens_sum, tokens_part))
        start(ends[-1:])
        state["left"] = grads.ship([(left_part, left_out)], peers.before)

    backward = {
        "slopes": slopes,
        "inner4": partial(inner_grad, 4),
        "inner5": partial(inner_grad, 5),
        "inner": inner_back,
        "norm2": cross_norm,
        "cross": cross_back,
        "grads2": cross_grads,
        "inputs2": cross_inputs,
        "home": memory_home,
        "norm1": self_norm,
        "self": self_back,
        "grads1": self_grads,
        "inputs1": self_inputs,
        "v": vectors_near,
        "vy": vectors_y,
        "vx": vectors_x,
        "vp": vectors_p,
        "vm": vectors_m,
    }
    follow(BACKWARD, reduce_hop, backward)
    landed(state["v"] + state["left"] + state["home"])
    for k in range(2):
        @pl.when(jnp.logical_not(peers.alone[k]))
        def _():
            landed(back[k])
            sent(back[k])

        @pl.when(peers.alone[k])
        def _():
            stay[k].wait()

    grads.finish()
    for copy in ends:
        copy.wait()


def fill_masks(peers, target_ids, source_ids, mask_self, mask_cross):
    def ids(ref, block):
        here = pl.ds(pl.multiple_of(128 * block, 128), 128)
        return jnp.broadcast_to(ref[:, here].astype(WIDE), (128, 128))

    s = peers.s
    here = ids(target_ids, s)
    queries = jnp.transpose(here)
    row = lax.broadcasted_iota(jnp.int32, (128, 128), 0)
    column = lax.broadcasted_iota(jnp.int32, (128, 128), 1)
    before = jnp.where(s > 0, ids(target_ids, lax.rem(s + 7, 8)), -1.0)
    mask_self[:, 0:128] = jnp.where(queries == before, 0.0, NEGATIVE)
    seen = jnp.where(queries == here, 0.0, NEGATIVE)
    mask_self[:, 128:256] = jnp.where(column <= row, seen, NEGATIVE)
    for k in range(3):
        block = ids(source_ids, lax.rem(14 + k - s, 8))
        mask_cross[:, 128 * k : 128 * k + 128] = jnp.where(queries == block, 0.0, NEGATIVE)


def layer_call(*inputs):
    shapes = [
        jax.ShapeDtypeStruct((128, 768), LOW),
        jax.ShapeDtypeStruct((8, 3, 16, 768), LOW),
        jax.ShapeDtypeStruct((8, 3, 16, 768), LOW),
        jax.ShapeDtypeStruct((2, 16, 128), WIDE),
        jax.ShapeDtypeStruct((128, 768), LOW),
        jax.ShapeDtypeStruct((3, 128, 768), LOW),
        jax.ShapeDtypeStruct((128, 768), WIDE),
    ]

    def low(*shape):
        return pltpu.VMEM(shape, LOW)

    def wide(*shape):
        return pltpu.VMEM(shape, WIDE)

    scratch = [low(24, 768)] * 8 + [low(24, 3072)] + [low(1, 24)] * 13 + [low(1, 96)]
    scratch += [
        low(128, 768),
        pltpu.VMEM((1, 1024), jnp.int32),
        pltpu.VMEM((1, 1024), jnp.int32),
        low(128, 768),
        wide(128, 768),
        low(12, 2, 2, 4, 48, 768),
        low(2, 2, 4, 2, 96, 768),
        low(2, 2, 4, 2, 16, 128),
        low(256, 768),
        low(384, 768),
        wide(16, 128),
        wide(128, 256),
        wide(128, 384),
        wide(16, 768),
        wide(8, 3072),
        low(128, 768),
        low(256, 768),
        low(256, 768),
        low(6, 256, 256),
        low(128, 768),
        wide(128, 768),
        low(128, 768),
        low(128, 768),
        low(384, 768),
        low(384, 768),
        low(6, 256, 384),
        low(128, 768),
        wide(128, 768),
        low(128, 768),
        low(128, 3072),
        low(128, 3072),
        wide(128, 768),
        wide(128, 768),
        low(128, 768),
        low(128, 768),
        low(128, 768),
        low(384, 768),
        low(384, 768),
        wide(16, 768),
        wide(8, 3072),
        low(12, 2, 4, 2, 3, 16, 768),
        low(4, 2, 4, 2, 3, 16, 768),
        low(4, 2, 3, 16, 768),
        low(8, 2, 4, 3, 16, 768),
        low(8, 4, 3, 16, 768),
        low(8, 2, 3, 16, 768),
        wide(2, 2, 4, 2, 16, 128),
        wide(2, 4, 2, 16, 128),
        wide(2, 4, 16, 128),
        wide(4, 16, 128),
        wide(2, 16, 128),
        low(128, 768),
        low(3, 128, 768),
        pltpu.SemaphoreType.REGULAR,
        pltpu.SemaphoreType.DMA((WIRES,)),
        pltpu.SemaphoreType.DMA((WIRES,)),
        pltpu.SemaphoreType.DMA((44,)),
    ]
    anywhere = pl.BlockSpec(memory_space=pl.ANY)
    return pl.pallas_call(
        layer_kernel,
        out_shape=shapes,
        in_specs=[anywhere] * 29,
        out_specs=[anywhere] * 7,
        scratch_shapes=scratch,
        compiler_params=pltpu.CompilerParams(
            collective_id=0, has_side_effects=True, vmem_limit_bytes=VMEM_BYTES
        ),
    )(*inputs)


def final_kernel(output_low, parts, mine, vparts, left, memory_low, tokens_part, *outs):
    output, tokens_grad, memory_grad = outs[:3]
    squares, inner, outer, smalls = outs[3:11], outs[11], outs[12], outs[13:]
    output[...] = output_low[...]
    b, s = lax.axis_index(BATCH), lax.axis_index(SEQ)
    even = lax.rem(s, 2) == 0
    tokens_grad[...] = tokens_part[...] + left[...].astype(WIDE)
    memory_grad[...] = (
        memory_low[0].astype(WIDE) + memory_low[1].astype(WIDE) + memory_low[2].astype(WIDE)
    )

    def summed(unit):
        total = (
            mine[unit].astype(WIDE) + parts[unit].astype(WIDE)
        )
        return total.reshape(48, 768)

    for unit in range(6):
        total = summed(unit)
        for k in range(2):
            body, rest = total[16 * k : 16 * k + 16], total[32 + 8 * k : 40 + 8 * k]
            matrix = jnp.where(
                even, jnp.concatenate([body, rest], axis=0), jnp.concatenate([rest, body], axis=0)
            )
            m = 2 * unit + k
            if m < 8:
                squares[m][...] = matrix
            else:
                inner[:, 768 * (m - 8) : 768 * (m - 7)] = matrix
    outer[0:48, :] = summed(6)
    outer[48:96, :] = summed(7)
    index = 8 * b + s
    vectors = vparts[0] + vparts[1]
    row = lax.broadcasted_iota(jnp.int32, (16, 128), 0)
    by24 = pltpu.roll(vectors, lax.rem(128 * 24 - 24 * index, 128), 1)
    by96 = pltpu.roll(vectors, lax.rem(128 * 96 - 96 * index, 128), 1)
    small = jnp.where(row == 13, by96, by24)
    for j, ref in enumerate(smalls):
        ref[...] = small[j : j + 1, 0 : ref.shape[1]]


def final_call(*inputs):
    shapes = [
        jax.ShapeDtypeStruct((128, 768), LOW),
        jax.ShapeDtypeStruct((128, 768), WIDE),
        jax.ShapeDtypeStruct((128, 768), WIDE),
    ]
    shapes += [jax.ShapeDtypeStruct((24, 768), WIDE)] * 8
    shapes += [jax.ShapeDtypeStruct((24, 3072), WIDE), jax.ShapeDtypeStruct((96, 768), WIDE)]
    shapes += [jax.ShapeDtypeStruct((1, 24), WIDE)] * 13 + [jax.ShapeDtypeStruct((1, 96), WIDE)]
    return pl.pallas_call(
        final_kernel,
        out_shape=shapes,
        in_specs=[vmem()] * 7,
        out_specs=[vmem()] * 27,
        compiler_params=pltpu.CompilerParams(vmem_limit_bytes=VMEM_BYTES),
    )(*inputs)


def fast_shards(tokens, memory, target_segments, memory_segments, cotangent, *weights):
    squares = weights[0:4] + weights[9:13]
    inner, inner_bias, outer = weights[18:21]
    smalls = list(weights[4:9]) + list(weights[13:18]) + list(weights[21:24]) + [inner_bias]
    results = layer_call(
        *squares,
        inner,
        outer,
        *[small[None] for small in smalls],
        tokens[0],
        memory[0],
        cotangent[0],
        target_segments,
        memory_segments,
    )
    results = final_call(*results)
    output, tokens_grad, memory_grad = results[:3]
    matrices, inner_grad, outer_grad = results[3:11], results[11], results[12]
    vector = [small.reshape(-1) for small in results[13:]]
    return (
        (output[None], tokens_grad[None], memory_grad[None])
        + tuple(matrices[0:4])
        + tuple(vector[0:5])
        + tuple(matrices[4:8])
        + tuple(vector[5:10])
        + (inner_grad, vector[13], outer_grad)
        + tuple(vector[10:13])
    )


def fits(mesh):
    return mesh.shape[BATCH] == 4 and mesh.shape[SEQ] == 8


def solution(mesh):
    in_specs = (
        P(BATCH, SEQ, None),
        P(BATCH, SEQ, None),
        P(BATCH, None),
        P(BATCH, None),
        P(BATCH, SEQ, None),
        P(BOTH, None),
        P(BOTH, None),
        P(BOTH, None),
        P(BOTH, None),
        P(BOTH),
        P(BOTH),
        P(BOTH),
        P(BOTH),
        P(BOTH),
        P(BOTH, None),
        P(BOTH, None),
        P(BOTH, None),
        P(BOTH, None),
        P(BOTH),
        P(BOTH),
        P(BOTH),
        P(BOTH),
        P(BOTH),
        P(BOTH, None),
        P(BOTH),
        P(BOTH, None),
        P(BOTH),
        P(BOTH),
        P(BOTH),
    )
    out_specs = (
        P(BATCH, SEQ, None),
        P(BATCH, SEQ, None),
        P(BATCH, SEQ, None),
        P(BOTH, None),
        P(BOTH, None),
        P(BOTH, None),
        P(BOTH, None),
        P(BOTH),
        P(BOTH),
        P(BOTH),
        P(BOTH),
        P(BOTH),
        P(BOTH, None),
        P(BOTH, None),
        P(BOTH, None),
        P(BOTH, None),
        P(BOTH),
        P(BOTH),
        P(BOTH),
        P(BOTH),
        P(BOTH),
        P(BOTH, None),
        P(BOTH),
        P(BOTH, None),
        P(BOTH),
        P(BOTH),
        P(BOTH),
    )
    quick = fits(mesh)
    return jax.shard_map(fast_shards if quick else shards, mesh=mesh, in_specs=in_specs, out_specs=out_specs, check_vma=False)
```
